128 devices in a mesh: dp: 32 (over z, x_hi, y), tensor: 4 (over x_lo, core).
Axes of the slice: x: 4 (x_hi: 2, x_lo: 2; x = x_hi * 2 + x_lo), y: 4, z: 4, core: 2. Of those that a mesh axis runs over, the one named last changes fastest.
Arguments:
- layer_input: float32 [12288, 2048], P('dp', 'tensor'), may hold values from -6 to 6
- attn_norm: float32 [2048], replicated, may hold values from 0.5 to 1.5
- w_query: bfloat16 [2048, 2048], P(None, 'tensor'), may hold values from -0.125 to 0.125
- w_key: bfloat16 [2048, 2048], P(None, 'tensor'), may hold values from -0.125 to 0.125
- w_value: bfloat16 [2048, 2048], P(None, 'tensor'), may hold values from -0.125 to 0.125
- query_norm: float32 [2048], P('tensor'), may hold values from 0.5 to 1.5
- key_norm: float32 [2048], P('tensor'), may hold values from 0.5 to 1.5
- w_output: bfloat16 [2048, 2048], P('tensor'), may hold values from -0.5 to 0.5
- moe_norm: float32 [2048], replicated, may hold values from 0.5 to 1.5
- w_router: bfloat16 [2048, 64], replicated, may hold values from -0.0625 to 0.0625
- w_gate: bfloat16 [64, 2048, 1024], P('dp', None, 'tensor'), may hold values from -0.125 to 0.125
- w_up: bfloat16 [64, 2048, 1024], P('dp', None, 'tensor'), may hold values from -0.125 to 0.125
- w_down: bfloat16 [64, 1024, 2048], P('dp', 'tensor'), may hold values from -0.5 to 0.5
- segments: int32 [32, 384], P('dp'), may hold values from 0 to 5, never falling along the last dimension, each value on 1 to 192 neighbouring positions
- positions: int32 [32, 384], P('dp'), may hold values from 0 to 1535
- routes: int32 [12288, 8], P('dp'), may hold values from 0 to 63, all different within a row; in each aligned block of 384 rows (0 to 383, 384 to 767, ...) at most 56 rows name the same one
- out_grad: float32 [12288, 2048], P('dp', 'tensor'), may hold values from -6 to 6
Outputs:
- layer_output: float32 [12288, 2048], P('dp', 'tensor')
- input_grad: float32 [12288, 2048], P('dp', 'tensor')
- attn_norm_grad: float32 [2048], replicated
- w_query_grad: float32 [2048, 2048], P(None, 'tensor')
- w_key_grad: float32 [2048, 2048], P(None, 'tensor')
- w_value_grad: float32 [2048, 2048], P(None, 'tensor')
- query_norm_grad: float32 [2048], P('tensor')
- key_norm_grad: float32 [2048], P('tensor')
- w_output_grad: float32 [2048, 2048], P('tensor')
- moe_norm_grad: float32 [2048], replicated
- w_router_grad: float32 [2048, 64], replicated
- w_gate_grad: float32 [64, 2048, 1024], P('dp', None, 'tensor')
- w_up_grad: float32 [64, 2048, 1024], P('dp', None, 'tensor')
- w_down_grad: float32 [64, 1024, 2048], P('dp', 'tensor')
The draws below stay inside these ranges and needn't reach their ends.
Inputs may be any that keep to these rules, and one draw needn't show every extreme that they name: `routes`: each token names 8 different experts. Among the 384 tokens of one sequence no expert is named more than 56 times, and in some sequence an expert is named exactly 56 times. `segments`: within a sequence the numbers never fall.
All inputs are finite; a program needn't handle non-finite values.
Results may differ from the reference program's by a relative error of at most 0.028.
Values may be sent and summed in bfloat16 or wider, within the bound.
A program may use at most 320 MiB of HBM per device.

```python
import math
import jax
import jax.numpy as jnp
import numpy as np
from jax import lax

D = 2048
HEADS = 16
HDIM = 128
FFE = 1024
TOP = 8
TOK = 384
EXPERTS = 64
SEQS = 32
TOKENS = 12288
CAP = 56


def plant(drawn, rng, smallest, high):
    index_at = [jax.random.randint(jax.random.fold_in(rng, axis), (), 0, length) for axis, length in enumerate(drawn.shape)]
    main_axis = drawn.shape.index(max(drawn.shape))
    neighbour = index_at[:main_axis] + [(index_at[main_axis] + 1) % drawn.shape[main_axis]] + index_at[main_axis + 1:]
    return drawn.at[tuple(index_at)].set(smallest).at[tuple(neighbour)].set(high)


def block_scale(stream_key, dims, cuts, least, top_value):
    level, own = 1.0, jax.random.fold_in(stream_key, 6)
    for axis_at, shards_of in cuts:
        heights = jnp.exp(jax.random.uniform(jax.random.fold_in(own, axis_at), (shards_of,), jnp.float32, least / len(cuts), top_value / len(cuts)))
        level = level * jnp.repeat(heights, dims[axis_at] // shards_of).reshape([-1 if axis == axis_at else 1 for axis in range(len(dims))])
    return level


def profile(amount, total, bound, slope):
    loads = [(1 << 20) // math.isqrt(rank ** slope) + 1 for rank in range(2, amount + 1)]
    spare, holding = total - bound - (amount - 1), [1] * (amount - 1)
    while spare > 0:
        movable = [i for i in range(amount - 1) if holding[i] < bound]
        pool, remaining = sum([loads[i] for i in movable]), spare
        for i in movable:
            addition = min(bound - holding[i], max(1, remaining * loads[i] // pool), spare)
            holding[i] = holding[i] + addition
            spare = spare - addition
    return np.array([bound] + holding)


def uneven(stream_key, count, total, reach, lean):
    if count == 2:
        one = jax.random.randint(stream_key, (), max(1, total - reach), min(reach, total - 1) + 1)
        return jnp.stack([one, total - one])
    sizes = jnp.asarray(profile(count, total, reach, lean), jnp.int32)
    couples = (count - 1) // 2
    source_of, sink = sizes[1:1 + 2 * couples:2], sizes[2:2 + 2 * couples:2]
    room = jnp.minimum(source_of - 1, reach - sink)
    moved = jax.random.randint(jax.random.fold_in(stream_key, 1), (couples,), 0, 1 << 20) % (room + 1)
    sizes = sizes.at[1:1 + 2 * couples:2].set(source_of - moved).at[2:2 + 2 * couples:2].set(sink + moved)
    return sizes[jax.random.permutation(jax.random.fold_in(stream_key, 2), count)]


def shared_out(own_key, own, number, rows, count, top, bound, slope):
    order = jax.random.permutation(own_key, count)
    crowded, ordinary = load_shares(count, rows * top, bound, slope, True), load_shares(count, rows * top, bound, slope, False)
    places = jnp.arange(count)

    def named(lengths, turn):
        used = int((lengths > 0).sum())
        fixed = max(1, used // 4)
        passed = fixed + (places - fixed + turn * (used - fixed)) % max(1, count - fixed)
        return jnp.zeros((count,), jnp.int32).at[order[jnp.where(places < fixed, places, passed)]].set(jnp.asarray(lengths, jnp.int32))

    lengths = jnp.where(number % 4 == 0, named(crowded, number // 4), named(ordinary, number - number // 4 - 1))
    mixed = jax.random.permutation(jax.random.fold_in(own, 3), count)
    source_of, taker = mixed[0:count // 2 * 2:2], mixed[1:count // 2 * 2:2]
    margin = jnp.minimum(lengths[source_of] - 1, bound - lengths[taker]) // 2
    margin = jnp.where((source_of == order[0]) | (taker == order[0]) | (lengths[taker] == 0), 0, jnp.maximum(margin, 0))
    passed = jax.random.randint(jax.random.fold_in(own, 4), (count // 2,), 0, 1 << 20) % (margin + 1)
    lengths = lengths.at[source_of].add(-passed).at[taker].add(passed)
    members = jnp.searchsorted(jnp.cumsum(lengths), jnp.arange(rows * top), side="right").astype(jnp.int32)
    table = members.reshape(top, rows).T
    table = table[jax.random.permutation(jax.random.fold_in(own, 1), rows)]
    turn = jax.random.randint(jax.random.fold_in(own, 2), (rows, 1), 0, top)
    return jnp.take_along_axis(table, (jnp.arange(top)[None, :] + turn) % top, axis=1)


def load_shares(number_of, total, reach, skew, full):
    portions = [(1 << 20) // math.isqrt(standing ** skew) + 1 for standing in range(1, number_of + 1)]
    largest = reach if full else min(reach, max(-(-total // number_of), total * portions[0] // sum(portions)))
    least = 1 if total - largest >= number_of - 1 else 0
    holding, surplus = [largest] + [least] * (number_of - 1), total - largest - least * (number_of - 1)
    while surplus > 0:
        free = [i for i in range(1, number_of) if holding[i] < largest] or [i for i in range(1, number_of) if holding[i] < reach]
        whole, remaining = sum([portions[i] for i in free]), surplus
        for i in free:
            extra = min(reach - holding[i], max(1, remaining * portions[i] // whole), surplus)
            holding[i] = holding[i] + extra
            surplus = surplus - extra
    return np.array(holding)


def noise(stream_key, dims, width, most, pieces=(), kind=jnp.bfloat16):
    level = block_scale(stream_key, dims, pieces, -0.22, 0.18) if pieces else 1.0
    values = jax.random.normal(stream_key, dims, jnp.float32) * width * level
    return jnp.minimum(jnp.maximum(values, -most), most).astype(kind)


def setup_inputs(seed: int = 0) -> dict:
    arg_keys = jax.random.split(jax.random.key(seed), 18)
    layer_input = noise(arg_keys[0], (TOKENS, D), 1.0, 6.0, ((0, 32), (1, 4)), jnp.float32)
    attn_norm = jnp.clip(1.0 + 0.1 * jax.random.normal(arg_keys[1], (D,), jnp.float32), 0.5, 1.5)
    w_query = noise(arg_keys[2], (D, HEADS * HDIM), D ** -0.5, 0.125, ((1, 4),))
    w_key = noise(arg_keys[3], (D, HEADS * HDIM), D ** -0.5, 0.125, ((1, 4),))
    w_value = noise(arg_keys[4], (D, HEADS * HDIM), D ** -0.5, 0.125, ((1, 4),))
    query_norm = jnp.clip(1.0 + 0.1 * jax.random.normal(arg_keys[5], (HEADS * HDIM,), jnp.float32), 0.5, 1.5)
    key_norm = jnp.clip(1.0 + 0.1 * jax.random.normal(arg_keys[6], (HEADS * HDIM,), jnp.float32), 0.5, 1.5)
    w_output = noise(arg_keys[7], (HEADS * HDIM, D), (HEADS * HDIM // 16) ** -0.5, 0.5, ((0, 4),))
    moe_norm = jnp.clip(1.0 + 0.1 * jax.random.normal(arg_keys[8], (D,), jnp.float32), 0.5, 1.5)
    w_router = noise(arg_keys[9], (D, EXPERTS), (4 * D) ** -0.5, 0.0625)
    w_gate = noise(arg_keys[10], (EXPERTS, D, FFE), D ** -0.5, 0.125, ((0, 32), (2, 4)))
    w_up = noise(arg_keys[11], (EXPERTS, D, FFE), D ** -0.5, 0.125, ((0, 32), (2, 4)))
    w_down = noise(arg_keys[12], (EXPERTS, FFE, D), (FFE // 8) ** -0.5, 0.5, ((0, 32), (1, 4)))
    segments = jax.vmap(lambda own: jnp.searchsorted(jnp.cumsum(uneven(own, max(TOK // 64, 3), TOK, TOK // 2, 2)), jnp.arange(TOK), side="right"))(jax.random.split(arg_keys[13], SEQS)).reshape((SEQS, TOK)).astype(jnp.int32)
    positions = plant(jax.random.randint(arg_keys[14], (SEQS, TOK), 0, 4 * TOK), jax.random.fold_in(arg_keys[14], 1), 0, (4 * TOK) - 1).astype(jnp.int32)
    routes_keys = jax.random.split(jax.random.fold_in(arg_keys[15], 1), TOKENS // TOK)
    routes_turns = jax.random.permutation(jax.random.fold_in(arg_keys[15], 3), TOKENS // TOK)
    routes = jax.vmap(lambda own, number: shared_out(jax.random.fold_in(arg_keys[15], 2), own, number, TOK, EXPERTS, TOP, CAP, 1))(routes_keys, routes_turns).reshape((TOKENS, TOP))
    out_grad = noise(arg_keys[16], (TOKENS, D), 1.0, 6.0, ((0, 32), (1, 4)), jnp.float32)
    return {"layer_input": layer_input, "attn_norm": attn_norm, "w_query": w_query, "w_key": w_key, "w_value": w_value, "query_norm": query_norm, "key_norm": key_norm, "w_output": w_output, "moe_norm": moe_norm, "w_router": w_router, "w_gate": w_gate, "w_up": w_up, "w_down": w_down, "segments": segments, "positions": positions, "routes": routes, "out_grad": out_grad}


EPS = 1e-06
HIGH = lax.Precision.HIGHEST

@jax.custom_vjp
def low(v):
    return lax.optimization_barrier(v.astype(jnp.bfloat16)).astype(jnp.float32)

@jax.custom_vjp
def low_back(v):
    return v

def low_keep(v):
    return (low(v), None)

def low_pass(kept, grad):
    return (grad,)

def back_keep(v):
    return (v, None)

def back_low(kept, grad):
    return (low(grad),)
low.defvjp(low_keep, low_pass)
low_back.defvjp(back_keep, back_low)

def inv_rms(value):
    return lax.rsqrt(lax.optimization_barrier(jnp.mean(value * value, axis=-1, keepdims=True)) + EPS)

def rope_angles(places):
    half = HDIM // 2
    frequency = jnp.exp(jnp.arange(half, dtype=jnp.float32) * (-2.0 * jnp.log(10000.0) / HDIM))
    angle = places.astype(jnp.float32)[:, None] * frequency[None, :]
    return (jnp.cos(angle)[:, None, :], jnp.sin(angle)[:, None, :])

def rotate(value, cosine, sine):
    half = value.shape[-1] // 2
    first = value[..., :half]
    second = value[..., half:]
    return jnp.concatenate([first * cosine - second * sine, second * cosine + first * sine], axis=-1)

def attend(block, labels, places, attn_norm, w_query, w_key, w_value, query_norm, key_norm, w_output):
    length = block.shape[0]
    normed_in = low(block * inv_rms(block) * attn_norm)
    cosine, sine = rope_angles(places)

    def project(weight, gain):
        pre = low_back(jnp.dot(normed_in, weight, precision=HIGH)).reshape(length, HEADS, HDIM)
        return low(rotate(pre * inv_rms(pre) * gain.reshape(HEADS, HDIM), cosine, sine))
    query = project(w_query, query_norm)
    key = project(w_key, key_norm)
    values = low_back(low(jnp.dot(normed_in, w_value, precision=HIGH))).reshape(length, HEADS, HDIM)
    scores = low_back(jnp.einsum('thd,shd->hts', query, key, precision=HIGH) * HDIM ** (-0.5))
    same = labels[:, None] == labels[None, :]
    probs = low(jax.nn.softmax(jnp.where(same[None], scores, -1e+30), axis=-1))
    mixed = jnp.einsum('hts,shd->thd', probs, values, precision=HIGH).reshape(length, HEADS * HDIM)
    mixed = low_back(low(mixed))
    return low_back(jnp.dot(mixed, w_output, precision=HIGH))

def slot_tables(routes):
    flat = routes.reshape(SEQS, TOK * TOP)
    hits = (flat[:, :, None] == jnp.arange(EXPERTS, dtype=jnp.int32)[None, None, :]).astype(jnp.int32)
    rank = lax.optimization_barrier(jnp.sum(jnp.cumsum(hits, axis=1) * hits, axis=2)) - 1
    where = (jnp.arange(SEQS, dtype=jnp.int32)[:, None] * CAP + rank).astype(jnp.int32).reshape(TOKENS, TOP)
    owners = (jnp.arange(TOKENS * TOP, dtype=jnp.int32) // TOP).astype(jnp.int32)
    table = jnp.full((EXPERTS, SEQS * CAP), TOKENS, jnp.int32).at[routes.reshape(-1), where.reshape(-1)].set(owners)
    return (table, where)

def forward(layer_input, attn_norm, w_query, w_key, w_value, query_norm, key_norm, w_output, moe_norm, w_router, w_gate, w_up, w_down, segments, positions, routes, table, where):
    blocks = layer_input.reshape(SEQS, TOK, D)

    def one_sequence(items):
        return attend(items[0], items[1], items[2], attn_norm, w_query, w_key, w_value, query_norm, key_norm, w_output)
    attn = lax.map(jax.checkpoint(one_sequence), (blocks, segments, positions)).reshape(TOKENS, D)
    mid = layer_input + attn
    normed_mid = low(mid * inv_rms(mid) * moe_norm)
    logits = jnp.dot(normed_mid, w_router, precision=HIGH)
    gates = jax.nn.softmax(jnp.take_along_axis(logits, routes, axis=1), axis=-1)
    padded = jnp.concatenate([normed_mid, jnp.zeros((1, D), normed_mid.dtype)], axis=0)

    def one_expert(items):
        gate_weight, up_weight, down_weight, index = items
        rows = padded[index]
        gate_pre = low_back(jnp.dot(rows, gate_weight, precision=HIGH))
        up_pre = low_back(jnp.dot(rows, up_weight, precision=HIGH))
        hidden = low(jax.nn.silu(gate_pre) * up_pre)
        return low_back(low(jnp.dot(hidden, down_weight, precision=HIGH)))
    expert_out = lax.map(jax.checkpoint(one_expert), (w_gate, w_up, w_down, table))
    picked = expert_out[routes, where]
    return mid + jnp.einsum('tk,tkd->td', gates, picked, precision=HIGH)

def reference(layer_input, attn_norm, w_query, w_key, w_value, query_norm, key_norm, w_output, moe_norm, w_router, w_gate, w_up, w_down, segments, positions, routes, out_grad):
    table, where = slot_tables(routes)
    floats = (layer_input, attn_norm, w_query.astype(jnp.float32), w_key.astype(jnp.float32), w_value.astype(jnp.float32), query_norm, key_norm, w_output.astype(jnp.float32), moe_norm, w_router.astype(jnp.float32), w_gate.astype(jnp.float32), w_up.astype(jnp.float32), w_down.astype(jnp.float32))

    def forward_fn(*params):
        return forward(*params, segments, positions, routes, table, where)
    output, pull = jax.vjp(forward_fn, *floats)
    grads = pull(out_grad)
    return (output, grads[0], grads[1], grads[2], grads[3], grads[4], grads[5], grads[6], grads[7], grads[8], grads[9], grads[10], grads[11], grads[12])
```

```python
import jax
import jax.numpy as jnp
from jax import lax
from jax.sharding import PartitionSpec as P

HDIM = 128
TOP = 8
SLOTS = 64
HALF = SLOTS // 2
EPS = 1e-06
HIGH = lax.Precision.HIGHEST
F32 = jnp.float32
BF16 = jnp.bfloat16


def dot(a, b, dims, **kw):
    return lax.dot_general(a, b, (dims, ((), ())), preferred_element_type=F32, **kw)


def nn(a, b):
    return dot(a, b, ((1,), (0,)))


def nt(a, b):
    return dot(a, b, ((1,), (1,)))


def tn(a, b):
    return dot(a, b, ((0,), (0,)))


def cross(value):
    return lax.ppermute(value, "tensor", [(0, 2), (2, 0), (1, 3), (3, 1)])


def swap(value):
    return lax.ppermute(value, "tensor", [(0, 1), (1, 0), (2, 3), (3, 2)])


def inv_rms(value):
    return lax.rsqrt(jnp.mean(value * value, axis=-1, keepdims=True) + EPS)


def rope_angles(places):
    half = HDIM // 2
    frequency = jnp.exp(jnp.arange(half, dtype=F32) * (-2.0 * jnp.log(10000.0) / HDIM))
    angle = places.astype(F32)[:, None] * frequency[None, :]
    return (jnp.cos(angle)[:, None, :], jnp.sin(angle)[:, None, :])


def rotate(value, cosine, sine):
    half = value.shape[-1] // 2
    first = value[..., :half]
    second = value[..., half:]
    return jnp.concatenate(
        [first * cosine - second * sine, second * cosine + first * sine], axis=-1
    )


def norm_back(pre, scale_head, gain, grad_normed):
    weighted = grad_normed * gain
    pre_grad = scale_head * weighted - pre * scale_head**3 * jnp.mean(
        weighted * pre, axis=-1, keepdims=True
    )
    gain_grad = jnp.sum(grad_normed * pre * scale_head, axis=0).reshape(-1)
    return (pre_grad, gain_grad)


def attention_scores(query, key, same):
    raw = jnp.einsum("thd,shd->hts", query, key, preferred_element_type=F32) * HDIM ** (-0.5)
    return jnp.where(same, raw, -1e30)


def per_device(
    layer_input,
    attn_norm,
    w_query,
    w_key,
    w_value,
    query_norm,
    key_norm,
    w_output,
    moe_norm,
    w_router,
    w_gate,
    w_up,
    w_down,
    segments,
    positions,
    routes,
    out_grad,
):
    length, quarter = layer_input.shape
    width = 4 * quarter
    rank_t = lax.axis_index("tensor")
    side = rank_t // 2
    core = rank_t % 2
    first_side = side == 0
    first_core = core == 0
    groups = lax.axis_size("dp")
    experts = 2 * groups
    local_heads = w_query.shape[1] // HDIM
    scale = HDIM ** (-0.5)

    def own(vector):
        return lax.dynamic_slice_in_dim(vector, rank_t * quarter, quarter, 0)

    def gather(mine):
        far = cross(mine)
        near = swap(mine)
        near_far = swap(far)
        a = jnp.where(first_side, mine, far)
        b = jnp.where(first_side, far, mine)
        c = jnp.where(first_side, near, near_far)
        d = jnp.where(first_side, near_far, near)
        return jnp.concatenate(
            [
                jnp.where(first_core, a, c),
                jnp.where(first_core, c, a),
                jnp.where(first_core, b, d),
                jnp.where(first_core, d, b),
            ],
            axis=1,
        )

    def scatter_sum(part):
        p0, p1, p2, p3 = (part[:, i * quarter : (i + 1) * quarter] for i in range(4))
        sent = jnp.where(
            first_core, jnp.concatenate([p1, p3], axis=1), jnp.concatenate([p0, p2], axis=1)
        ).astype(BF16)
        got = swap(sent).astype(F32)
        low_half = jnp.where(first_core, p0, p1) + got[:, :quarter]
        high_half = jnp.where(first_core, p2, p3) + got[:, quarter:]
        back = cross(jnp.where(first_side, high_half, low_half).astype(BF16))
        return jnp.where(first_side, low_half, high_half) + back.astype(F32)

    def sum_tensor(value):
        value = value + swap(value)
        return value + cross(value)

    def pick(pair, which):
        return jnp.where(which, pair[0], pair[1])

    quarters = []
    for w in (w_gate, w_up, w_down):
        mine = pick(w, first_side)
        far = cross(pick(w, jnp.logical_not(first_side)))
        quarters.append((mine, far, swap(mine), swap(far)))

    experts_row = jnp.arange(experts, dtype=jnp.int32)
    chosen = jnp.any(routes[:, :, None] == experts_row[None, None, :], axis=1)
    chosen_low = chosen.astype(BF16)
    before = (jnp.arange(length)[:, None] > jnp.arange(length)[None, :]).astype(BF16)
    rank = nn(before, chosen_low).astype(jnp.int32)
    place = jnp.where(chosen, rank, -1).reshape(length, groups, 2)
    place = jnp.where(first_side, place[:, :, 0], place[:, :, 1]).T
    spots = core * HALF + jnp.arange(HALF, dtype=jnp.int32)
    select = (
        (place[:, None, :] == spots[None, :, None]).astype(BF16).reshape(groups * HALF, length)
    )

    def to_experts(rows):
        return lax.all_to_all(
            rows.reshape(groups, HALF, rows.shape[-1]), "dp", split_axis=0, concat_axis=0, tiled=True
        ).reshape(groups * HALF, rows.shape[-1])

    grad_full = gather(out_grad.astype(BF16))
    grad_rows = to_experts(nn(select, grad_full).astype(BF16))

    in_full = gather(layer_input.astype(BF16)).astype(F32)
    first_scale = inv_rms(in_full)
    normed_in = (in_full * first_scale * attn_norm).astype(BF16)
    cosine, sine = rope_angles(positions[0])
    labels = segments[0]
    same = (labels[:, None] == labels[None, :])[None]
    query_pre = nn(normed_in, w_query).reshape(length, local_heads, HDIM)
    key_pre = nn(normed_in, w_key).reshape(length, local_heads, HDIM)
    query_scale = inv_rms(query_pre)
    key_scale = inv_rms(key_pre)
    query_gain = query_norm.reshape(local_heads, HDIM)
    key_gain = key_norm.reshape(local_heads, HDIM)
    query = rotate(query_pre * query_scale * query_gain, cosine, sine).astype(BF16)
    key = rotate(key_pre * key_scale * key_gain, cosine, sine).astype(BF16)
    values = nn(normed_in, w_value).astype(BF16).reshape(length, local_heads, HDIM)
    scores = attention_scores(query, key, same)
    highest = jnp.max(scores, axis=-1, keepdims=True)
    powered = jnp.exp(scores - highest)
    total = jnp.sum(powered, axis=-1, keepdims=True)
    log_total = highest + jnp.log(total)
    mixed = jnp.einsum(
        "hts,shd->thd", (powered / total).astype(BF16), values, preferred_element_type=F32
    )
    mixed = mixed.reshape(length, local_heads * HDIM).astype(BF16)
    mid = layer_input + scatter_sum(nn(mixed, w_output))
    mid_full = gather(mid.astype(BF16)).astype(F32)
    second_scale = inv_rms(mid_full)
    normed_mid = (mid_full * second_scale * moe_norm).astype(BF16)

    logits = nn(normed_mid, w_router)
    masked = jnp.where(chosen, logits, -1e30)
    raised = jnp.where(chosen, jnp.exp(masked - jnp.max(masked, axis=1, keepdims=True)), 0.0)
    gates = raised / jnp.sum(raised, axis=1, keepdims=True)
    gates_side = gates.reshape(length, groups, 2)
    gates_side = jnp.where(first_side, gates_side[:, :, 0], gates_side[:, :, 1])
    select_cube = select.reshape(groups, HALF, length).astype(F32)
    slot_gates = jnp.sum(select_cube * gates_side.T[:, None, :], axis=2)
    rows = to_experts(nn(select, normed_mid).astype(BF16))
    slot_gates = lax.all_to_all(slot_gates, "dp", split_axis=0, concat_axis=0, tiled=True)
    slot_gates = slot_gates.reshape(groups * HALF, 1)

    expert_out = 0.0
    saved = []
    for i in range(4):
        gate_w, up_w, down_w = (w[i] for w in quarters)
        gate_pre = nn(rows, gate_w)
        up_pre = nn(rows, up_w)
        hidden = jax.nn.silu(gate_pre) * up_pre
        expert_out = expert_out + nn(hidden.astype(BF16), down_w)
        saved.append((gate_pre, up_pre, hidden))
    expert_out = expert_out.astype(BF16)
    slot_grad = jnp.sum(grad_rows.astype(F32) * expert_out.astype(F32), axis=1)
    rows_grad = 0.0
    weight_grads = []
    for i in range(4):
        gate_w, up_w, down_w = (w[i] for w in quarters)
        gate_pre, up_pre, hidden = saved[i]
        hidden_grad = slot_gates * nt(grad_rows, down_w)
        sig = jax.nn.sigmoid(gate_pre)
        gate_pre_grad = (hidden_grad * up_pre * sig * (1.0 + gate_pre * (1.0 - sig))).astype(BF16)
        up_pre_grad = (hidden_grad * gate_pre * sig).astype(BF16)
        rows_grad = rows_grad + nt(gate_pre_grad, gate_w) + nt(up_pre_grad, up_w)
        weight_grads.append(
            (
                tn(rows, gate_pre_grad),
                tn(rows, up_pre_grad),
                tn((slot_gates * hidden).astype(BF16), grad_rows),
            )
        )

    def from_experts(value):
        return lax.all_to_all(
            value.astype(BF16).reshape(groups, HALF, width), "dp", split_axis=0, concat_axis=0, tiled=True
        ).reshape(groups * HALF, width)

    slot_grad = lax.all_to_all(
        slot_grad.reshape(groups, HALF), "dp", split_axis=0, concat_axis=0, tiled=True
    )
    back_rows = from_experts(rows_grad)
    returned = from_experts(expert_out)

    expert_grads = []
    for i in range(3):
        mine, far, near, near_far = (weight_grads[j][i] for j in range(4))
        mine = mine + swap(near.astype(BF16)).astype(F32)
        far = far + swap(near_far.astype(BF16)).astype(F32)
        other = cross(far.astype(BF16)).astype(F32)
        expert_grads.append(
            jnp.stack([jnp.where(first_side, mine, other), jnp.where(first_side, other, mine)])
        )

    gate_grad = jnp.sum(select_cube * slot_grad[:, :, None], axis=1).T
    zero = jnp.zeros_like(gate_grad)
    gate_grad = jnp.stack(
        [jnp.where(first_side, gate_grad, zero), jnp.where(first_side, zero, gate_grad)], axis=2
    ).reshape(length, experts)
    gate_grad = sum_tensor(gate_grad)
    logit_grad = gates * (gate_grad - jnp.sum(gates * gate_grad, axis=1, keepdims=True))
    normed_mid_own = lax.dynamic_slice_in_dim(normed_mid, rank_t * quarter, quarter, 1)
    w_router_own = lax.dynamic_slice_in_dim(w_router, rank_t * quarter, quarter, 0)
    w_router_grad = dot(
        normed_mid_own.astype(F32), logit_grad, ((0,), (0,)), precision=HIGH
    )
    router_back = dot(logit_grad, w_router_own.astype(F32), ((1,), (1,)), precision=HIGH)
    normed_grad = scatter_sum(tn(select, back_rows)) + router_back
    moe_norm_grad = jnp.sum(
        normed_grad * mid * second_scale, axis=0
    )
    normed_grad_full = gather(normed_grad.astype(BF16)).astype(F32)
    weighted_full = normed_grad_full * moe_norm
    shrink = second_scale**3 * jnp.mean(weighted_full * mid_full, axis=-1, keepdims=True)
    attn_grad = (
        grad_full.astype(F32) + second_scale * weighted_full - mid_full * shrink
    ).astype(BF16)
    mid_grad = out_grad + second_scale * (normed_grad * own(moe_norm)) - mid * shrink

    select_gated = (select_cube * gates_side.T[:, None, :]).reshape(groups * HALF, length)
    layer_output = mid + scatter_sum(tn(select_gated.astype(BF16), returned))

    w_output_grad = tn(mixed, attn_grad)
    mixed_grad = nt(attn_grad, w_output).astype(BF16).reshape(length, local_heads, HDIM)
    probs = jnp.exp(scores - log_total)
    value_grad = jnp.einsum(
        "hts,thd->shd", probs.astype(BF16), mixed_grad, preferred_element_type=F32
    ).astype(BF16)
    prob_grad = jnp.einsum("thd,shd->hts", mixed_grad, values, preferred_element_type=F32)
    score_grad = (probs * (prob_grad - jnp.sum(probs * prob_grad, axis=-1, keepdims=True))).astype(
        BF16
    )
    query_rot_grad = jnp.einsum("hts,shd->thd", score_grad, key, preferred_element_type=F32) * scale
    key_rot_grad = jnp.einsum("hts,thd->shd", score_grad, query, preferred_element_type=F32) * scale
    query_pre_grad, query_norm_grad = norm_back(
        query_pre, query_scale, query_gain, rotate(query_rot_grad, cosine, -sine)
    )
    key_pre_grad, key_norm_grad = norm_back(
        key_pre, key_scale, key_gain, rotate(key_rot_grad, cosine, -sine)
    )
    query_low = query_pre_grad.astype(BF16).reshape(length, local_heads * HDIM)
    key_low = key_pre_grad.astype(BF16).reshape(length, local_heads * HDIM)
    value_low = value_grad.reshape(length, local_heads * HDIM)
    w_query_grad = tn(normed_in, query_low)
    w_key_grad = tn(normed_in, key_low)
    w_value_grad = tn(normed_in, value_low)
    in_part = nt(query_low, w_query) + nt(key_low, w_key) + nt(value_low, w_value)
    in_grad = scatter_sum(in_part)
    attn_norm_grad = jnp.sum(in_grad * layer_input * first_scale, axis=0)
    weighted_in = in_grad * own(attn_norm)
    mean_in = sum_tensor(jnp.sum(weighted_in * layer_input, axis=-1, keepdims=True)) / width
    input_grad = mid_grad + first_scale * weighted_in - layer_input * first_scale**3 * mean_in

    stacked = jnp.concatenate(
        [w_output_grad[:, i * quarter : (i + 1) * quarter] for i in range(4)]
        + [w_query_grad, w_key_grad, w_value_grad, w_router_grad.T]
        + [jnp.stack([attn_norm_grad, moe_norm_grad, query_norm_grad, key_norm_grad])],
        axis=0,
    ).astype(BF16)
    n_rows = stacked.shape[0]
    piece = -(-n_rows // (groups * 16)) * 16
    stacked = jnp.pad(stacked, ((0, groups * piece - n_rows), (0, 0)))
    pieces = lax.all_to_all(
        stacked.reshape(groups, piece, quarter), "dp", split_axis=0, concat_axis=0, tiled=True
    )
    whole = jnp.sum(pieces.astype(F32), axis=0).astype(BF16)
    big = lax.all_gather(whole, "dp", axis=0, tiled=True)
    base = width + 3 * w_query.shape[0]
    small = big[base : base + experts + 4]
    everywhere = lax.all_gather(small[: experts + 2], "tensor", axis=1, tiled=True).astype(F32)
    rows_w = w_query.shape[0]
    rows_o = w_output.shape[0]
    summed = [big[width + i * rows_w : width + (i + 1) * rows_w].astype(F32) for i in range(3)]
    output_grad = jnp.concatenate(
        [big[i * rows_o : (i + 1) * rows_o] for i in range(4)], axis=1
    ).astype(F32)
    return (
        layer_output,
        input_grad,
        everywhere[experts],
        summed[0],
        summed[1],
        summed[2],
        small[experts + 2].astype(F32),
        small[experts + 3].astype(F32),
        output_grad,
        everywhere[experts + 1],
        everywhere[:experts].T,
        expert_grads[0],
        expert_grads[1],
        expert_grads[2],
    )


def solution(mesh):
    placed = (
        P("dp", "tensor"),
        P(),
        P(None, "tensor"),
        P(None, "tensor"),
        P(None, "tensor"),
        P("tensor"),
        P("tensor"),
        P("tensor", None),
        P(),
        P(),
        P("dp", None, "tensor"),
        P("dp", None, "tensor"),
        P("dp", "tensor", None),
        P("dp", None),
        P("dp", None),
        P("dp", None),
        P("dp", "tensor"),
    )
    return jax.shard_map(
        per_device,
        mesh=mesh,
        in_specs=placed,
        out_specs=(
            P("dp", "tensor"),
            P("dp", "tensor"),
            P(),
            P(None, "tensor"),
            P(None, "tensor"),
            P(None, "tensor"),
            P("tensor"),
            P("tensor"),
            P("tensor", None),
            P(),
            P(),
            P("dp", None, "tensor"),
            P("dp", None, "tensor"),
            P("dp", "tensor", None),
        ),
        check_vma=False,
    )
```

```python
import functools

import jax
import jax.numpy as jnp
from jax import lax
from jax.experimental import pallas as pl
from jax.experimental.pallas import tpu as pltpu
from jax.sharding import PartitionSpec as P

HDIM = 128
TOP = 8
SLOTS = 64
HALF = SLOTS // 2
EPS = 1e-06
HIGH = lax.Precision.HIGHEST
F32 = jnp.float32
BF16 = jnp.bfloat16
MESH = pl.DeviceIdType.MESH
SMALL = 80
LANES = 128


def dot(a, b, dims, **kw):
    return lax.dot_general(a, b, (dims, ((), ())), preferred_element_type=F32, **kw)


def nn(a, b):
    return dot(a, b, ((1,), (0,)))


def nt(a, b):
    return dot(a, b, ((1,), (1,)))


def tn(a, b):
    return dot(a, b, ((0,), (0,)))


def cross(value):
    return lax.ppermute(value, "tensor", [(0, 2), (2, 0), (1, 3), (3, 1)])


def swap(value):
    return lax.ppermute(value, "tensor", [(0, 1), (1, 0), (2, 3), (3, 2)])


def inv_rms(value):
    return lax.rsqrt(jnp.mean(value * value, axis=-1, keepdims=True) + EPS)


def rope_angles(places):
    half = HDIM // 2
    frequency = jnp.exp(jnp.arange(half, dtype=F32) * (-2.0 * jnp.log(10000.0) / HDIM))
    angle = places.astype(F32)[:, None] * frequency[None, :]
    cosine, sine = jnp.cos(angle), jnp.sin(angle)
    return (
        jnp.concatenate([cosine, cosine], axis=1),
        jnp.concatenate([-sine, sine], axis=1),
    )


def two_parts(column):
    high = column.astype(BF16)
    rest = (column - high.astype(F32)).astype(BF16)
    lane = lax.broadcasted_iota(jnp.int32, (column.shape[0], LANES), 1)
    return jnp.where(
        lane == 0, high.astype(F32), jnp.where(lane == 1, rest.astype(F32), 0.0)
    ).astype(BF16)


def one_column(pair):
    wide = pair.astype(F32)
    return wide[:, 0:1] + wide[:, 1:2]


def expert_body(
    rows_in, og_in, wg_all, wu_all, wd_all,
    out_ref, back_in, kept_g, kept_u, kept_d, got_g, got_u, got_d,
    rows_s, og_s, wgu_s, wd_s, back_s, gu_s, hid_s, keep_s, move_s, down_keep, down_move,
    rs_sem, og_sem, w_sem, bs, br, ls, ks, ms, mr,
):
    plane = Plane()
    swap = (plane.dp, lax.axis_index("tensor") + 1 - 2 * plane.core)
    groups, slots, more = rows_s.shape
    width = og_s.shape[2]
    hidden = hid_s.shape[1]
    span = hidden // 4
    per = groups // 4
    tile = per * slots

    def load(e, _):
        g = plane.entry(e)
        pltpu.make_async_copy(rows_in.at[g], rows_s.at[e], rs_sem.at[e // per]).start()
        pltpu.make_async_copy(og_in.at[g], og_s.at[e], og_sem.at[e // per]).start()
        return 0

    lax.fori_loop(0, per, load, 0)
    w_copies = []
    for i in range(4):
        at = slice(i * span, (i + 1) * span)
        high = slice(hidden + i * span, hidden + (i + 1) * span)
        w_copies.append(pltpu.make_async_copy(wg_all.at[i], wgu_s.at[:, at], w_sem.at[0, i]))
        w_copies.append(pltpu.make_async_copy(wu_all.at[i], wgu_s.at[:, high], w_sem.at[1, i]))
    for i in range(4):
        at = slice(i * span, (i + 1) * span)
        w_copies.append(pltpu.make_async_copy(wd_all.at[i], wd_s.at[at], w_sem.at[2, i]))
    for c in w_copies:
        c.start()
    lax.fori_loop(per, groups, load, 0)

    barrier = pltpu.get_barrier_semaphore()

    plane.greet(barrier)
    pl.semaphore_signal(barrier, inc=1, device_id=swap, device_id_type=MESH)
    pl.semaphore_wait(barrier, groups)

    def back_copy(e):
        g = plane.entry(e)
        return pltpu.make_async_remote_copy(
            src_ref=back_s.at[e],
            dst_ref=back_in.at[plane.dp],
            send_sem=bs.at[e],
            recv_sem=br.at[e],
            device_id=plane.device(g),
            device_id_type=MESH,
        )

    own_back = pltpu.make_async_copy(back_s.at[groups - 1], back_in.at[plane.dp], ls.at[0])

    def one_tile(k, _):
        first = pl.multiple_of(k * per, per)
        here = pl.ds(pl.multiple_of(k * tile, tile), tile)
        part = pl.ds(first, per)
        pltpu.make_async_copy(rows_in.at[pl.ds(0, per)], rows_s.at[part], rs_sem.at[k]).wait()

        @pl.when(k == 0)
        def _():
            for c in w_copies[:8]:
                c.wait()

        mine = rows_s[part].reshape(tile, more)
        rows = mine[:, :width]
        gate = one_column(mine[:, width:])
        both = nn(rows, wgu_s[...])
        gp = both[:, :hidden]
        up = both[:, hidden:]
        sig = jax.nn.sigmoid(gp)
        act = gp * sig
        hid = act * up
        hid_s[here, :] = (gate * hid).astype(BF16)

        @pl.when(k == 0)
        def _():
            for c in w_copies[8:]:
                c.wait()

        low = nn(hid.astype(BF16), wd_s[...]).astype(BF16)
        out_ref[part] = low.reshape(per, slots, width)
        pltpu.make_async_copy(og_in.at[pl.ds(0, per)], og_s.at[part], og_sem.at[k]).wait()
        grads = og_s[part].reshape(tile, width)
        slot = jnp.sum(grads.astype(F32) * low.astype(F32), axis=1, keepdims=True)
        back_s[part, :, width:] = two_parts(slot).reshape(per, slots, more - width)
        hidden_grad = gate * nt(grads, wd_s[...])
        gu_s[here, :hidden] = (hidden_grad * up * sig * (1.0 + gp * (1.0 - sig))).astype(BF16)
        gu_s[here, hidden:] = (hidden_grad * act).astype(BF16)
        back = nt(gu_s[here, :], wgu_s[...]).astype(BF16)
        back_s[part, :, :width] = back.reshape(per, slots, width)

        def send(j, _):
            e = first + j

            @pl.when(e < groups - 1)
            def _():
                back_copy(e).start()

            @pl.when(e == groups - 1)
            def _():
                own_back.start()

            return 0

        lax.fori_loop(0, per, send, 0)
        return 0

    lax.fori_loop(0, 4, one_tile, 0)

    half = hidden // 2
    wide_block = keep_s.shape[1]

    def column_copies(i, slot):
        at = pl.ds(pl.multiple_of(i * wide_block, wide_block), wide_block)
        local = [
            pltpu.make_async_copy(keep_s.at[slot, :, :half], kept_g.at[at], ks.at[slot, 0]),
            pltpu.make_async_copy(keep_s.at[slot, :, half:], kept_u.at[at], ks.at[slot, 1]),
        ]
        far = [
            pltpu.make_async_remote_copy(
                src_ref=move_s.at[slot, :, side],
                dst_ref=target.at[at],
                send_sem=ms.at[slot, n],
                recv_sem=mr.at[i, n],
                device_id=swap,
                device_id_type=MESH,
            )
            for n, (side, target) in enumerate(
                ((slice(0, half), got_g), (slice(half, hidden), got_u))
            )
        ]
        return local + far

    def columns(i, _):
        slot = lax.rem(i, 2)

        @pl.when(i >= 2)
        def _():
            for c in column_copies(i - 2, slot):
                c.wait()

        at = pl.ds(pl.multiple_of(i * wide_block, wide_block), wide_block)
        rows = rows_s[:, :, at].reshape(groups * slots, wide_block)
        grad = tn(rows, gu_s[...])
        keep_s[slot, :, :half] = grad[:, :half]
        keep_s[slot, :, half:] = grad[:, hidden : hidden + half]
        move_s[slot, :, :half] = grad[:, half:hidden].astype(BF16)
        move_s[slot, :, half:] = grad[:, hidden + half :].astype(BF16)
        for c in column_copies(i, slot):
            c.start()
        return 0

    steps = width // wide_block
    lax.fori_loop(0, steps, columns, 0)
    downs = []
    for i in range(4):
        at = slice(i * span, (i + 1) * span)
        grad = tn(hid_s[:, at], og_s[...].reshape(groups * slots, width))
        if i < 2:
            down_keep[at] = grad
            downs.append(pltpu.make_async_copy(down_keep.at[at], kept_d.at[at], ls.at[1 + i]))
        else:
            at = slice((i - 2) * span, (i - 1) * span)
            down_move[at] = grad.astype(BF16)
            downs.append(
                pltpu.make_async_remote_copy(
                    src_ref=down_move.at[at],
                    dst_ref=got_d.at[at],
                    send_sem=ms.at[2, i - 2],
                    recv_sem=mr.at[steps, i - 2],
                    device_id=swap,
                    device_id_type=MESH,
                )
            )
        downs[-1].start()
    for i in (steps - 2, steps - 1):
        for c in column_copies(i, i % 2):
            c.wait()
    for c in downs:
        c.wait()

    def finish(e, _):
        back_copy(e).wait()
        return 0

    lax.fori_loop(0, groups - 1, finish, 0)
    own_back.wait()


def run_experts(rows, grads, weights):
    groups, slots, more = rows.shape
    width = grads.shape[2]
    hidden = 4 * weights[0].shape[2]
    half = hidden // 2
    count = groups * slots
    block = 256
    whole = pl.BlockSpec(memory_space=pltpu.VMEM)
    free = pl.BlockSpec(memory_space=pl.ANY)
    f = jax.ShapeDtypeStruct
    vm = pltpu.VMEM
    dma = pltpu.SemaphoreType.DMA
    return pl.pallas_call(
        expert_body,
        in_specs=[free] * 5,
        out_specs=[whole] + [free] * 7,
        out_shape=[
            f((groups, slots, width), BF16),
            f((groups, slots, more), BF16),
            f((width, half), F32),
            f((width, half), F32),
            f((half, width), F32),
            f((width, half), BF16),
            f((width, half), BF16),
            f((half, width), BF16),
        ],
        scratch_shapes=[
            vm((groups, slots, more), BF16),
            vm((groups, slots, width), BF16),
            vm((width, 2 * hidden), BF16),
            vm((hidden, width), BF16),
            vm((groups, slots, more), BF16),
            vm((count, 2 * hidden), BF16),
            vm((count, hidden), BF16),
            vm((2, block, hidden), F32),
            vm((2, block, hidden), BF16),
            vm((half, width), F32),
            vm((half, width), BF16),
            dma((4,)),
            dma((4,)),
            dma((3, 4)),
            dma((31,)),
            dma((31,)),
            dma((3,)),
            dma((2, 2)),
            dma((3, 2)),
            dma((width // block + 1, 2)),
        ],
        compiler_params=pltpu.CompilerParams(
            collective_id=2, has_side_effects=True, vmem_limit_bytes=61 << 20
        ),
        name="experts",
    )(rows, grads, *weights)


def head_scale(pre):
    return lax.rsqrt(jnp.mean(pre * pre, axis=1, keepdims=True) + EPS)


def turn(value, cosine, sine):
    return value * cosine + pltpu.roll(value, HDIM // 2, 1) * sine


def softmax_rows(query, key, same):
    raw = nt(query, key) * HDIM ** (-0.5)
    raw = jnp.where(same, raw, -1e30)
    powered = jnp.exp(raw - jnp.max(raw, axis=1, keepdims=True))
    return powered / jnp.sum(powered, axis=1, keepdims=True)


class Near:
    def __init__(self, send_sems, recv_sems):
        self.dp = lax.axis_index("dp")
        self.t = lax.axis_index("tensor")
        self.core = lax.rem(self.t, 2)
        self.first_core = self.core == 0
        self.low_x = self.t < 2
        self.far = lax.rem(self.t + 2, 4)
        self.swap = (self.dp, self.t + 1 - 2 * self.core)
        self.cross = (self.dp, self.far)
        self.diag = (self.dp, self.far + 1 - 2 * self.core)
        self.sems = (send_sems, recv_sems)
        self.used = 0

    def send(self, source, target, device):
        k = self.used
        self.used = k + 1
        c = pltpu.make_async_remote_copy(
            src_ref=source,
            dst_ref=target,
            send_sem=self.sems[0].at[k],
            recv_sem=self.sems[1].at[k],
            device_id=device,
            device_id_type=MESH,
        )
        c.start()
        return c

    def gather_start(self, buf):
        here = buf.at[self.t]
        return [self.send(here, here, self.cross), self.send(here, here, self.swap)]

    def gather_relay(self, buf, copies):
        copies[0].wait()
        there = buf.at[self.far]
        copies.append(self.send(there, there, self.swap))

    def split(self, part, low_s, high_s, sent):
        quarter = part.shape[1] // 4
        p = [part[:, i * quarter : (i + 1) * quarter] for i in range(4)]
        low_s[...] = jnp.where(self.first_core, p[0], p[1])
        high_s[...] = jnp.where(self.first_core, p[2], p[3])
        sent[:, :quarter] = jnp.where(self.first_core, p[1], p[0]).astype(BF16)
        sent[:, quarter:] = jnp.where(self.first_core, p[3], p[2]).astype(BF16)

    def sum_parts(self, low_s, high_s, sent, got, go, back):
        quarter = go.shape[1]
        self.send(sent, got, self.swap).wait()
        low = low_s[...] + got[:, :quarter].astype(F32)
        high = high_s[...] + got[:, quarter:].astype(F32)
        go[...] = jnp.where(self.low_x, high, low).astype(BF16)
        self.send(go, back, self.cross).wait()
        return jnp.where(self.low_x, low, high) + back[...].astype(F32)


class Plane:
    def __init__(self):
        self.dp = lax.axis_index("dp")
        t = lax.axis_index("tensor")
        self.y = lax.rem(self.dp, 4)
        self.xh = lax.rem(self.dp // 4, 2)
        self.z = self.dp // 8
        self.core = lax.rem(t, 2)
        self.side = lax.rem(t // 2 + self.xh, 2)

    def at(self, dz, dx, dy):
        return (lax.rem(self.z + dz, 4) * 2 + lax.rem(self.xh + dx, 2)) * 4 + lax.rem(
            self.y + dy, 4
        )

    def device(self, group):
        return (group, lax.rem(self.side + lax.rem(group // 4, 2), 2) * 2 + self.core)

    def entry(self, e):
        o = jnp.where(e == 31, 0, lax.rem(11 * e + 5, 31) + 1)
        return self.at(o // 8, lax.rem(o // 4, 2), lax.rem(o, 4))

    def greet(self, barrier):
        def one(e, _):
            pl.semaphore_signal(
                barrier, inc=1, device_id=self.device(self.entry(e)), device_id_type=MESH
            )
            return 0

        lax.fori_loop(0, 31, one, 0)

    def exchange(self, source, target, send_sems, recv_sems, local_sem, ordered):
        def copy(e):
            group = self.entry(e)
            return pltpu.make_async_remote_copy(
                src_ref=source.at[e if ordered else group],
                dst_ref=target.at[self.dp],
                send_sem=send_sems.at[e],
                recv_sem=recv_sems.at[e],
                device_id=self.device(group),
                device_id_type=MESH,
            )

        def start(e, _):
            copy(e).start()
            return 0

        def finish(e, _):
            copy(e).wait()
            return 0

        own = pltpu.make_async_copy(source.at[31 if ordered else self.dp], target.at[self.dp], local_sem)
        lax.fori_loop(0, 31, start, 0)
        own.start()

        def wait():
            lax.fori_loop(0, 31, finish, 0)
            own.wait()

        return wait


def wide(buf):
    return jnp.concatenate([buf[i] for i in range(4)], axis=1)


def front_body(
    x_ref, og_ref, gain1_ref, gain2_ref, wq_ref, wk_ref, wv_ref, wo_ref, qn_ref, kn_ref, cos_ref,
    sin_ref, col_ref, row_ref, routes_ref, ids_ref, router_ref, wg_ref, wu_ref, wd_ref,
    normed_ref, fs_ref, qpre_ref, kpre_ref, q_ref, k_ref, v_ref, mixed_ref, mid_ref, mids_ref, ogs_ref,
    nm_ref, gates_ref, place_ref, rows_in, og_in, wg_all, wu_all, wd_all,
    xs, low_s, high_s, sent, got, go, back, og_out, rows_out,
    ts, tr, as_, ar, bs, br, ls,
):
    near = Near(ts, tr)
    plane = Plane()
    side = plane.side
    barrier = pltpu.get_barrier_semaphore()
    plane.greet(barrier)
    pl.semaphore_signal(barrier, inc=1, device_id=near.swap, device_id_type=MESH)
    pl.semaphore_signal(barrier, inc=1, device_id=near.cross, device_id_type=MESH)
    pl.semaphore_wait(barrier, 33)
    t = near.t
    length = x_ref.shape[0]
    quarter = x_ref.shape[1]
    width = 4 * quarter

    ogs_ref[t] = og_ref[...].astype(BF16)
    og_copies = near.gather_start(ogs_ref)
    xs[t] = x_ref[...].astype(BF16)
    x_copies = near.gather_start(xs)
    weights = ((wg_ref, wg_all), (wu_ref, wu_all), (wd_ref, wd_all))
    kept = [
        pltpu.make_async_copy(w.at[side], w_all.at[0], ls.at[2 + i])
        for i, (w, w_all) in enumerate(weights)
    ]
    w_cross = [near.send(wg_ref.at[1 - side], wg_all.at[1], near.cross)]

    chosen = routes_ref[0:1, :] == ids_ref[...]
    for k in range(1, TOP):
        chosen = jnp.logical_or(chosen, routes_ref[k : k + 1, :] == ids_ref[...])
    mask = jnp.where(chosen, 1.0, 0.0)
    earlier = lax.broadcasted_iota(jnp.int32, (length, length), 0) < lax.broadcasted_iota(
        jnp.int32, (length, length), 1
    )
    rank = nn(mask.astype(BF16), jnp.where(earlier, 1.0, 0.0).astype(BF16))
    rank = jnp.where(chosen, rank, -1.0).astype(jnp.int32)
    experts = rank.shape[0] // 2
    place_ref[...] = jnp.where(side == 0, rank[:experts], rank[experts:])
    base = near.core * HALF

    def hits(i):
        place = place_ref[i * 8 : (i + 1) * 8, :]
        spots = lax.broadcasted_iota(jnp.int32, (8, HALF, length), 1) + base
        return jnp.broadcast_to(place[:, None, :], (8, HALF, length)) == spots

    near.gather_relay(ogs_ref, og_copies)
    near.gather_relay(xs, x_copies)
    for c in og_copies[1:]:
        c.wait()
    og = wide(ogs_ref)
    for i in range(experts // 8):
        select = jnp.where(hits(i), 1.0, 0.0).reshape(8 * HALF, length).astype(BF16)
        og_out[i * 8 : (i + 1) * 8] = nn(select, og).astype(BF16).reshape(8, HALF, width)
    og_wait = plane.exchange(og_out, og_in, as_, ar, ls.at[0], False)
    for c in kept:
        c.start()
    w_swap = [near.send(w.at[side], w_all.at[2], near.swap) for w, w_all in weights]

    for c in x_copies[1:]:
        c.wait()
    x = wide(xs).astype(F32)
    scale = lax.rsqrt(jnp.mean(x * x, axis=1, keepdims=True) + EPS)
    fs_ref[...] = scale
    normed = (x * scale * gain1_ref[...]).astype(BF16)
    normed_ref[...] = normed
    qpre = nn(normed, wq_ref[...])
    kpre = nn(normed, wk_ref[...])
    qpre_ref[...] = qpre
    kpre_ref[...] = kpre
    v_ref[...] = nn(normed, wv_ref[...]).astype(BF16)
    cosine = cos_ref[...]
    sine = sin_ref[...]
    same = col_ref[...] == row_ref[...]
    for h in range(q_ref.shape[1] // HDIM):
        at = slice(h * HDIM, (h + 1) * HDIM)
        qh = qpre[:, at]
        kh = kpre[:, at]
        query = turn(qh * head_scale(qh) * qn_ref[:, at], cosine, sine).astype(BF16)
        key = turn(kh * head_scale(kh) * kn_ref[:, at], cosine, sine).astype(BF16)
        q_ref[:, at] = query
        k_ref[:, at] = key
        probs = softmax_rows(query, key, same).astype(BF16)
        mixed_ref[:, at] = nn(probs, v_ref[:, at]).astype(BF16)
    near.split(nn(mixed_ref[...], wo_ref[...]), low_s, high_s, sent)
    mid = x_ref[...] + near.sum_parts(low_s, high_s, sent, got, go, back)
    mid_ref[...] = mid
    mids_ref[t] = mid.astype(BF16)
    mid_copies = near.gather_start(mids_ref)
    w_cross.append(near.send(wu_ref.at[1 - side], wu_all.at[1], near.cross))
    w_cross.append(near.send(wd_ref.at[1 - side], wd_all.at[1], near.cross))
    near.gather_relay(mids_ref, mid_copies)
    for c in mid_copies[1:]:
        c.wait()
    mid = wide(mids_ref).astype(F32)
    scale = lax.rsqrt(jnp.mean(mid * mid, axis=1, keepdims=True) + EPS)
    normed = (mid * scale * gain2_ref[...]).astype(BF16)
    nm_ref[...] = normed

    logits = nt(router_ref[...], normed)
    masked = jnp.where(chosen, logits, -1e30)
    raised = jnp.where(chosen, jnp.exp(masked - jnp.max(masked, axis=0, keepdims=True)), 0.0)
    gates = raised / jnp.sum(raised, axis=0, keepdims=True)
    gates_ref[...] = gates
    gates_side = jnp.where(side == 0, gates[:experts], gates[experts:])
    for i in range(experts // 8):
        hit = hits(i)
        select = jnp.where(hit, 1.0, 0.0).reshape(8 * HALF, length).astype(BF16)
        rows_out[i * 8 : (i + 1) * 8, :, :width] = (
            nn(select, normed).astype(BF16).reshape(8, HALF, width)
        )
        gate = jnp.broadcast_to(gates_side[i * 8 : (i + 1) * 8][:, None, :], (8, HALF, length))
        column = jnp.sum(
            jnp.where(hit, gate, 0.0).reshape(8 * HALF, length), axis=1, keepdims=True
        )
        rows_out[i * 8 : (i + 1) * 8, :, width:] = two_parts(column).reshape(8, HALF, LANES)
    rows_wait = plane.exchange(rows_out, rows_in, bs, br, ls.at[1], False)
    for c, (w, w_all) in zip(w_cross, weights):
        c.wait()
        w_swap.append(near.send(w_all.at[1], w_all.at[3], near.swap))
    og_wait()
    rows_wait()
    for c in w_swap + kept:
        c.wait()


def run_front(
    x, og, gain1, gain2, wq, wk, wv, wo, qn, kn, cosine, sine, labels, routes, ids, router, wg, wu,
    wd, groups,
):
    length, quarter = x.shape
    width = 4 * quarter
    inner = wq.shape[1]
    whole = pl.BlockSpec(memory_space=pltpu.VMEM)
    free = pl.BlockSpec(memory_space=pl.ANY)
    f = jax.ShapeDtypeStruct
    vm = pltpu.VMEM
    dma = pltpu.SemaphoreType.DMA
    return pl.pallas_call(
        front_body,
        in_specs=[whole] * 17 + [free] * 3,
        out_specs=[whole] * 14 + [free] * 5,
        out_shape=[
            f((length, width), BF16),
            f((length, 1), F32),
            f((length, inner), F32),
            f((length, inner), F32),
            f((length, inner), BF16),
            f((length, inner), BF16),
            f((length, inner), BF16),
            f((length, inner), BF16),
            f((length, quarter), F32),
            f((4, length, quarter), BF16),
            f((4, length, quarter), BF16),
            f((length, width), BF16),
            f((2 * groups, length), F32),
            f((groups, length), jnp.int32),
            f((groups, HALF, width + LANES), BF16),
            f((groups, HALF, width), BF16),
            f((4,) + wg.shape[1:], BF16),
            f((4,) + wu.shape[1:], BF16),
            f((4,) + wd.shape[1:], BF16),
        ],
        scratch_shapes=[
            vm((4, length, quarter), BF16),
            vm((length, quarter), F32),
            vm((length, quarter), F32),
            vm((length, 2 * quarter), BF16),
            vm((length, 2 * quarter), BF16),
            vm((length, quarter), BF16),
            vm((length, quarter), BF16),
            vm((groups, HALF, width), BF16),
            vm((groups, HALF, width + LANES), BF16),
            dma((20,)),
            dma((20,)),
            dma((31,)),
            dma((31,)),
            dma((31,)),
            dma((31,)),
            dma((5,)),
        ],
        compiler_params=pltpu.CompilerParams(
            collective_id=1, has_side_effects=True, vmem_limit_bytes=60 << 20
        ),
        name="front",
    )(
        x, og, gain1, gain2, wq, wk, wv, wo, qn, kn, cosine, sine, labels[:, None], labels[None, :],
        routes, ids, router, wg, wu, wd,
    )


def middle_body(
    rows_ref, out_rows, place_ref, gates_ref, nm_ref, router_ref, mid_ref, og_ref, mids_ref, ogs_ref,
    gain_ref, normed_ref, wq_ref, wk_ref, wv_ref, wo_ref, qn_ref, kn_ref, cos_ref, sin_ref, col_ref,
    row_ref, qpre_ref, kpre_ref, q_ref, k_ref, v_ref, mixed_ref,
    stack_ref, small_ref, mid_grad_ref, keep_ref, sent_ref, returned,
    low_s, low_f, high_f, sent, got, go, back, ngs, gg_s, ts, tr, os, orr, ls,
):
    near = Near(ts, tr)
    plane = Plane()
    side = plane.side
    t = near.t
    groups, slots, more = rows_ref.shape
    length, width = normed_ref.shape
    quarter = width // 4
    inner = q_ref.shape[1]

    barrier = pltpu.get_barrier_semaphore()

    plane.greet(barrier)
    pl.semaphore_signal(barrier, inc=1, device_id=near.swap, device_id_type=MESH)
    pl.semaphore_signal(barrier, inc=1, device_id=near.cross, device_id_type=MESH)
    pl.semaphore_wait(barrier, groups + 1)

    out_wait = plane.exchange(out_rows, returned, os, orr, ls.at[0], True)

    base = near.core * slots
    part = None
    for i in range(groups // 8):
        at = slice(i * 8, (i + 1) * 8)
        spots = lax.broadcasted_iota(jnp.int32, (8, slots, length), 1) + base
        hit = jnp.broadcast_to(place_ref[at, :][:, None, :], (8, slots, length)) == spots
        select = jnp.where(hit, 1.0, 0.0).reshape(8 * slots, length)
        tile = rows_ref[at].reshape(8 * slots, more)
        column = one_column(tile[:, width:])
        gg_s[0, at] = jnp.sum((select * column).reshape(8, slots, length), axis=1)
        term = tn(select.astype(BF16), tile[:, :width])
        part = term if part is None else part + term
    gate_swap = near.send(gg_s.at[0], gg_s.at[1], near.swap)
    near.split(part, low_f, high_f, sent)
    swapped = near.send(sent, got, near.swap)
    gate_swap.wait()
    gg_s[2] = gg_s[0] + gg_s[1]
    gate_cross = near.send(gg_s.at[2], gg_s.at[3], near.cross)
    swapped.wait()
    low = low_f[...] + got[:, :quarter].astype(F32)
    high = high_f[...] + got[:, quarter:].astype(F32)
    go[...] = jnp.where(near.low_x, high, low).astype(BF16)
    crossed = near.send(go, back, near.cross)
    gate_cross.wait()
    own, other = gg_s[2], gg_s[3]
    gate_grad = jnp.concatenate(
        [jnp.where(side == 0, own, other), jnp.where(side == 0, other, own)], axis=0
    )
    gates = gates_ref[...]
    logit_grad = gates * (gate_grad - jnp.sum(gates * gate_grad, axis=0, keepdims=True))
    mine = pl.ds(pl.multiple_of(t * quarter, quarter), quarter)
    router_back = dot(
        logit_grad, router_ref[:, mine].astype(F32), ((0,), (0,)), precision=HIGH
    )
    experts = gates.shape[0]
    small_ref[:experts, :] = dot(
        logit_grad, nm_ref[:, mine].astype(F32), ((1,), (0,)), precision=HIGH
    ).astype(BF16)
    mid = wide(mids_ref).astype(F32)
    scale = lax.rsqrt(jnp.mean(mid * mid, axis=1, keepdims=True) + EPS)
    mid_own = mid_ref[...]
    crossed.wait()
    ng = jnp.where(near.low_x, low, high) + back[...].astype(F32) + router_back
    ngs[t] = ng.astype(BF16)
    ng_copies = near.gather_start(ngs)
    moe = jnp.sum(ng * mid_own * scale, axis=0, keepdims=True)
    near.gather_relay(ngs, ng_copies)
    for c in ng_copies[1:]:
        c.wait()

    weighted = wide(ngs).astype(F32) * gain_ref[...]
    shrink = scale * scale * scale * jnp.mean(weighted * mid, axis=1, keepdims=True)
    mid_grad_ref[...] = og_ref[...] + scale * (ng * gain_ref[:, mine]) - mid_own * shrink
    attn_grad = (wide(ogs_ref).astype(F32) + scale * weighted - mid * shrink).astype(BF16)

    wo_grad = tn(mixed_ref[...], attn_grad).astype(BF16)
    for i in range(4):
        stack_ref[i * inner : (i + 1) * inner, :] = wo_grad[:, i * quarter : (i + 1) * quarter]
    mixed_grad = nt(attn_grad, wo_ref[...]).astype(BF16)
    cosine = cos_ref[...]
    sine = sin_ref[...]
    same = col_ref[...] == row_ref[...]
    factor = HDIM ** (-0.5)

    def norm_back(pre, gain, rotated):
        grad = rotated * cosine - pltpu.roll(rotated, HDIM // 2, 1) * sine
        head = head_scale(pre)
        weighted = grad * gain
        mean = jnp.mean(weighted * pre, axis=1, keepdims=True)
        low = (head * weighted - pre * (head * head * head * mean)).astype(BF16)
        return low, jnp.sum(grad * pre * head, axis=0, keepdims=True)

    q_sums, k_sums = [], []
    for h in range(inner // HDIM):
        at = slice(h * HDIM, (h + 1) * HDIM)
        query = q_ref[:, at]
        key = k_ref[:, at]
        mg = mixed_grad[:, at]
        probs = softmax_rows(query, key, same)
        low_s[:, 2 * inner + h * HDIM : 2 * inner + (h + 1) * HDIM] = tn(
            probs.astype(BF16), mg
        ).astype(BF16)
        prob_grad = nt(mg, v_ref[:, at])
        weighted_p = probs * prob_grad
        score = (weighted_p - probs * jnp.sum(weighted_p, axis=1, keepdims=True)).astype(BF16)
        low_q, total = norm_back(qpre_ref[:, at], qn_ref[:, at], nn(score, key) * factor)
        low_s[:, h * HDIM : (h + 1) * HDIM] = low_q
        q_sums.append(total)
        low_k, total = norm_back(kpre_ref[:, at], kn_ref[:, at], tn(score, query) * factor)
        low_s[:, inner + h * HDIM : inner + (h + 1) * HDIM] = low_k
        k_sums.append(total)
    row = lax.broadcasted_iota(jnp.int32, (small_ref.shape[0] - experts, quarter), 0)
    rest = jnp.zeros(row.shape, F32)
    for i, value in enumerate(
        (moe, jnp.concatenate(q_sums, axis=1), jnp.concatenate(k_sums, axis=1))
    ):
        rest = jnp.where(row == i + 1, jnp.broadcast_to(value, row.shape), rest)
    small_ref[experts:, :] = rest.astype(BF16)
    part = None
    for i, w in enumerate((wq_ref, wk_ref, wv_ref)):
        term = nt(low_s[:, i * inner : (i + 1) * inner], w[...])
        part = term if part is None else part + term
    near.split(part, low_f, high_f, sent_ref)
    keep_ref[:, :quarter] = low_f[...]
    keep_ref[:, quarter:] = high_f[...]
    normed = normed_ref[...]
    for i in range(3):
        stack_ref[(i + 1) * width : (i + 2) * width, :] = tn(
            normed, low_s[:, i * inner : (i + 1) * inner]
        ).astype(BF16)

    out_wait()


def run_middle(
    rows, out_rows, place, gates, nm, router, mid, og, mids, ogs, gain, normed, wq, wk, wv, wo, qn,
    kn, cosine, sine, labels, qpre, kpre, q, k, v, mixed,
):
    length, width = normed.shape
    quarter = width // 4
    groups = place.shape[0]
    inner = wq.shape[1]
    whole = pl.BlockSpec(memory_space=pltpu.VMEM)
    free = pl.BlockSpec(memory_space=pl.ANY)
    f = jax.ShapeDtypeStruct
    vm = pltpu.VMEM
    dma = pltpu.SemaphoreType.DMA
    return pl.pallas_call(
        middle_body,
        in_specs=[whole, free] + [whole] * 26,
        out_specs=[whole] * 5 + [free],
        out_shape=[
            f((4 * width, quarter), BF16),
            f((SMALL, quarter), BF16),
            f((length, quarter), F32),
            f((length, 2 * quarter), F32),
            f((length, 2 * quarter), BF16),
            f(out_rows.shape, BF16),
        ],
        scratch_shapes=[
            vm((length, 3 * inner), BF16),
            vm((length, quarter), F32),
            vm((length, quarter), F32),
            vm((length, 2 * quarter), BF16),
            vm((length, 2 * quarter), BF16),
            vm((length, quarter), BF16),
            vm((length, quarter), BF16),
            vm((4, length, quarter), BF16),
            vm((4, groups, length), F32),
            dma((8,)),
            dma((8,)),
            dma((31,)),
            dma((31,)),
            dma((1,)),
        ],
        compiler_params=pltpu.CompilerParams(
            collective_id=3, has_side_effects=True, vmem_limit_bytes=61 << 20
        ),
        name="middle",
    )(
        rows, out_rows, place, gates, nm, router, mid, og, mids, ogs, gain, normed, wq, wk, wv, wo,
        qn, kn, cosine, sine, labels[:, None], labels[None, :], qpre, kpre, q, k, v, mixed,
    )


def tail_body(
    stack_ref, small_ref, keep_ref, sent_ref, x_ref, mid_grad_ref, fs_ref, gain_ref, mid_ref,
    ret_ref, sel_ref, kept_g, kept_u, kept_d, got_g, got_u, got_d,
    out_ref, small_out_ref, input_ref, layer_ref, mine_g, mine_u, mine_d, other_g, other_u, other_d,
    recv1, buf1, recv2, buf2, recv3, small_in, got, out_sent, out_got, go, back, out_go, out_back,
    mean_in, kb, gb, nb, kd, gd, far_g, far_u, far_d, ss, rs, sss, srs, ts, tr, ws,
):
    dp = lax.axis_index("dp")
    t = lax.axis_index("tensor")
    y = lax.rem(dp, 4)
    xh = lax.rem(dp // 4, 2)
    z = dp // 8
    core = lax.rem(t, 2)
    first_core = core == 0
    low_x = t < 2
    half = stack_ref.shape[0] // 2
    n1, n2, n3 = half // 4, half // 16, half // 32
    quarter = x_ref.shape[1]

    def at_z(k):
        return ((lax.rem(z + k, 4) * 2 + xh) * 4 + y, t)

    def at_y(k):
        return ((z * 2 + xh) * 4 + lax.rem(y + k, 4), t)

    at_x = ((z * 2 + 1 - xh) * 4 + y, t)
    at_swap = (dp, t + 1 - 2 * core)
    at_cross = (dp, lax.rem(t + 2, 4))
    at_diag = (dp, lax.rem(t + 2, 4) + 1 - 2 * core)

    barrier = pltpu.get_barrier_semaphore()
    for k in range(1, 4):
        pl.semaphore_signal(barrier, inc=1, device_id=at_z(k), device_id_type=MESH)
        pl.semaphore_signal(barrier, inc=1, device_id=at_y(k), device_id_type=MESH)
    for there in (at_x, at_swap, at_cross, at_diag):
        pl.semaphore_signal(barrier, inc=1, device_id=there, device_id_type=MESH)
    pl.semaphore_wait(barrier, 10)

    def send(source, target, sems, device):
        c = pltpu.make_async_remote_copy(
            src_ref=source,
            dst_ref=target,
            send_sem=sems[0],
            recv_sem=sems[1],
            device_id=device,
            device_id_type=MESH,
        )
        c.start()
        return c

    def copy(source, target, phase, h, k, device):
        return send(source, target, (ss.at[phase, h, k], rs.at[phase, h, k]), device)

    def small_copy(slot, k, device):
        return send(small_in.at[slot], small_in.at[slot], (sss.at[k], srs.at[k]), device)

    def near(source, target, k, device):
        return send(source, target, (ts.at[k], tr.at[k]), device)

    def rows_at(start, size):
        return pl.ds(pl.multiple_of(start, 128), size)

    ways = (((z, at_z), (y, at_y)), ((y, at_y), (z, at_z)))
    first, second, third = [], [], []
    for h in range(2):
        pos, at = ways[h][0]
        for k in range(1, 4):
            there = rows_at(h * half + lax.rem(pos + k, 4) * n1, n1)
            first.append(copy(stack_ref.at[there], recv1.at[h, k - 1], 0, h, k - 1, at(k)))

    swapped = near(sent_ref, got, 0, at_swap)
    part = tn(sel_ref[...], ret_ref[...])
    p = [part[:, i * quarter : (i + 1) * quarter] for i in range(4)]
    out_sent[:, :quarter] = jnp.where(first_core, p[1], p[0]).astype(BF16)
    out_sent[:, quarter:] = jnp.where(first_core, p[3], p[2]).astype(BF16)
    out_low = jnp.where(first_core, p[0], p[1])
    out_high = jnp.where(first_core, p[2], p[3])
    out_swapped = near(out_sent, out_got, 1, at_swap)
    swapped.wait()
    low_half = keep_ref[:, :quarter] + got[:, :quarter].astype(F32)
    high_half = keep_ref[:, quarter:] + got[:, quarter:].astype(F32)
    go[...] = jnp.where(low_x, high_half, low_half).astype(BF16)
    crossed = near(go, back, 2, at_cross)
    in_mine = jnp.where(low_x, low_half, high_half)
    out_swapped.wait()
    out_low = out_low + out_got[:, :quarter].astype(F32)
    out_high = out_high + out_got[:, quarter:].astype(F32)
    out_go[...] = jnp.where(low_x, out_high, out_low).astype(BF16)
    crossed.wait()
    in_grad = in_mine + back[...].astype(F32)
    x = x_ref[...]
    fs = fs_ref[...]
    weighted = in_grad * gain_ref[...]
    mean = jnp.sum(weighted * x, axis=1, keepdims=True)
    mean_in[0] = jnp.broadcast_to(mean, mean_in.shape[1:])
    mean_swap = near(mean_in.at[0], mean_in.at[1], 3, at_swap)
    row = lax.broadcasted_iota(jnp.int32, (16, quarter), 0)
    norm_row = jnp.sum(in_grad * x * fs, axis=0, keepdims=True)
    small_in[z] = small_ref[...]
    last = small_ref.shape[0] - 16
    small_in[z, last:, :] = jnp.where(
        row == 0, jnp.broadcast_to(norm_row, (16, quarter)), small_ref[last:, :].astype(F32)
    ).astype(BF16)
    small = [small_copy(z, k - 1, at_z(k)) for k in range(1, 4)]
    mean_swap.wait()
    mean_in[2] = mean_in[0] + mean_in[1]
    mean_cross = near(mean_in.at[2], mean_in.at[3], 4, at_cross)
    out_crossed = near(out_go, out_back, 5, at_cross)
    mean_cross.wait()
    mean = (mean_in[2] + mean_in[3])[:, 0:1] / (4 * quarter)
    input_ref[...] = mid_grad_ref[...] + fs * weighted - x * (fs * fs * fs * mean)
    out_crossed.wait()
    layer_ref[...] = mid_ref[...] + (jnp.where(low_x, out_low, out_high) + out_back[...].astype(F32))

    block = kb.shape[1]
    loads = []
    for kept, gotten in ((kept_g, got_g), (kept_u, got_u)):
        for i in range(kept_g.shape[0] // block):
            slot = len(loads) % 2
            at = slice(i * block, (i + 1) * block)
            loads.append(
                (
                    pltpu.make_async_copy(kept.at[at], kb.at[slot], ws.at[slot, 0]),
                    pltpu.make_async_copy(gotten.at[at], gb.at[slot], ws.at[slot, 1]),
                )
            )
    span = far_d.shape[0]
    down_loads = [
        (
            pltpu.make_async_copy(kept_d.at[at], kd.at[i], ws.at[2 + i, 0]),
            pltpu.make_async_copy(got_d.at[at], gd.at[i], ws.at[2 + i, 1]),
        )
        for i, at in enumerate((slice(0, span), slice(span, 2 * span)))
    ]
    for c in loads[0] + down_loads[0] + down_loads[1]:
        c.start()
    stores = []
    for n, pair in enumerate(loads):
        if n + 1 < len(loads):
            for c in loads[n + 1]:
                c.start()
        for c in pair:
            c.wait()
        slot = n % 2
        per = len(loads) // 2
        far, mine = ((far_g, mine_g), (far_u, mine_u))[n // per]
        at = slice((n % per) * block, (n % per + 1) * block)
        total = kb[slot] + gb[slot].astype(F32)
        if n >= 2:
            stores[n - 2].wait()
        nb[slot] = total[:, :span]
        far[at, :] = total[:, span:].astype(BF16)
        stores.append(pltpu.make_async_copy(nb.at[slot], mine.at[at], ws.at[slot, 2]))
        stores[-1].start()
        if n == per - 1:
            others = [near(far_g, other_g, 6, at_cross)]
    for pair in down_loads:
        for c in pair:
            c.wait()
    kd[0] = kd[0] + gd[0].astype(F32)
    far_d[...] = (kd[1] + gd[1].astype(F32)).astype(BF16)
    stores.append(pltpu.make_async_copy(kd.at[0], mine_d, ws.at[2, 2]))
    stores[-1].start()
    for c in stores[-3:]:
        c.wait()

    def small_total(start, count):
        total = small_in[start].astype(F32)
        for i in range(start + 1, start + count):
            total = total + small_in[i].astype(F32)
        return total.astype(BF16)

    bases = []
    for h in range(2):
        pos, _ = ways[h][0]
        for c in first[3 * h : 3 * h + 3]:
            c.wait()
        base = h * half + pos * n1
        step = n1 // 4

        def add_first(i, _, h=h, base=base):
            here = rows_at(i * step, step)
            total = stack_ref[rows_at(base + i * step, step), :].astype(F32)
            for k in range(3):
                total = total + recv1[h, k, here, :].astype(F32)
            buf1[h, here, :] = total.astype(BF16)
            return 0

        lax.fori_loop(0, n1 // step, add_first, 0)
        pos2, at2 = ways[h][1]
        for k in range(1, 4):
            there = rows_at(lax.rem(pos2 + k, 4) * n2, n2)
            second.append(copy(buf1.at[h, there], recv2.at[h, k - 1], 1, h, k - 1, at2(k)))
        bases.append(base)
    for c in small:
        c.wait()
    small_in[4 + y] = small_total(0, 4)
    small = [small_copy(4 + y, 3 + k - 1, at_y(k)) for k in range(1, 4)]
    for h in range(2):
        pos2, _ = ways[h][1]
        for c in second[3 * h : 3 * h + 3]:
            c.wait()
        total = buf1[h, rows_at(pos2 * n2, n2), :].astype(F32)
        for k in range(3):
            total = total + recv2[h, k].astype(F32)
        buf2[h] = total.astype(BF16)
        third.append(
            copy(buf2.at[h, rows_at((1 - xh) * n3, n3)], recv3.at[h], 2, h, 0, at_x)
        )
        bases[h] = bases[h] + pos2 * n2
    for c in small:
        c.wait()
    small_in[8 + xh] = small_total(4, 4)
    small = small_copy(8 + xh, 6, at_x)
    ahead = []
    for h in range(2):
        third[h].wait()
        total = buf2[h, rows_at(xh * n3, n3), :].astype(F32) + recv3[h].astype(F32)
        here = rows_at(bases[h] + xh * n3, n3)
        out_ref[here, :] = total.astype(BF16)
        ahead.append(copy(out_ref.at[here], out_ref.at[here], 3, h, 0, at_x))
    later = []
    for c in ahead:
        c.wait()
    others.append(near(far_u, other_u, 7, at_cross))
    others.append(near(far_d, other_d, 8, at_cross))
    for h in range(2):
        _, at2 = ways[h][1]
        here = rows_at(bases[h], n2)
        for k in range(1, 4):
            later.append(copy(out_ref.at[here], out_ref.at[here], 4, h, k - 1, at2(k)))
    small.wait()
    small_out_ref[t] = small_total(8, 2)
    small = [
        near(small_out_ref.at[t], small_out_ref.at[t], 9 + i, there)
        for i, there in enumerate((at_swap, at_cross, at_diag))
    ]
    ended = []
    for h in range(2):
        for c in later[3 * h : 3 * h + 3]:
            c.wait()
        pos, at = ways[h][0]
        here = rows_at(h * half + pos * n1, n1)
        for k in range(1, 4):
            ended.append(copy(out_ref.at[here], out_ref.at[here], 5, h, k - 1, at(k)))
    for c in small + others + ended:
        c.wait()


def run_tail(
    stack, small, keep, sent, x, mid_grad, fs, gain, mid, returned, select, pieces
):
    rows, cols = stack.shape
    half = rows // 2
    length = x.shape[0]
    deep, wide_half = pieces[0].shape
    span = wide_half // 2
    shapes = [(deep, span), (deep, span), (span, deep)]
    whole = pl.BlockSpec(memory_space=pltpu.VMEM)
    free = pl.BlockSpec(memory_space=pl.ANY)
    f = jax.ShapeDtypeStruct
    vm = pltpu.VMEM
    return pl.pallas_call(
        tail_body,
        in_specs=[whole] * 11 + [free] * 6,
        out_specs=[whole] * 4 + [free] * 6,
        out_shape=[
            f(stack.shape, BF16),
            f((4,) + small.shape, BF16),
            f(x.shape, F32),
            f(x.shape, F32),
        ]
        + [f(shape, F32) for shape in shapes]
        + [f(shape, BF16) for shape in shapes],
        scratch_shapes=[
            vm((2, 3, half // 4, cols), BF16),
            vm((2, half // 4, cols), BF16),
            vm((2, 3, half // 16, cols), BF16),
            vm((2, half // 16, cols), BF16),
            vm((2, half // 32, cols), BF16),
            vm((10,) + small.shape, BF16),
            vm((length, 2 * cols), BF16),
            vm((length, 2 * cols), BF16),
            vm((length, 2 * cols), BF16),
            vm((length, cols), BF16),
            vm((length, cols), BF16),
            vm((length, cols), BF16),
            vm((length, cols), BF16),
            vm((4, length, LANES), F32),
            vm((2, 512, wide_half), F32),
            vm((2, 512, wide_half), BF16),
            vm((2, 512, span), F32),
            vm((2, span, deep), F32),
            vm((2, span, deep), BF16),
            vm((deep, span), BF16),
            vm((deep, span), BF16),
            vm((span, deep), BF16),
            pltpu.SemaphoreType.DMA((6, 2, 3)),
            pltpu.SemaphoreType.DMA((6, 2, 3)),
            pltpu.SemaphoreType.DMA((7,)),
            pltpu.SemaphoreType.DMA((7,)),
            pltpu.SemaphoreType.DMA((12,)),
            pltpu.SemaphoreType.DMA((12,)),
            pltpu.SemaphoreType.DMA((4, 3)),
        ],
        compiler_params=pltpu.CompilerParams(
            collective_id=0, has_side_effects=True, vmem_limit_bytes=62 << 20
        ),
        cost_estimate=pl.CostEstimate(flops=0, bytes_accessed=500_000_000, transcendentals=0),
        name="sum_over_dp",
    )(stack, small, keep, sent, x, mid_grad, fs, gain, mid, returned, select, *pieces)


def per_device(
    layer_input,
    attn_norm,
    w_query,
    w_key,
    w_value,
    query_norm,
    key_norm,
    w_output,
    moe_norm,
    w_router,
    w_gate,
    w_up,
    w_down,
    segments,
    positions,
    routes,
    out_grad,
):
    length, quarter = layer_input.shape
    width = 4 * quarter
    rank_t = lax.axis_index("tensor")
    core = rank_t % 2
    low_x = rank_t // 2 == 0
    high_group = (lax.axis_index("dp") // 4) % 2 == 1
    first_side = jnp.logical_xor(low_x, high_group)
    groups = lax.axis_size("dp")
    experts = 2 * groups

    def own(vector):
        return lax.dynamic_slice_in_dim(vector, rank_t * quarter, quarter, 0)

    cosine, sine = rope_angles(positions[0])
    labels = segments[0]
    gain_q = query_norm[None, :]
    gain_k = key_norm[None, :]
    gain_1 = attn_norm[None, :]
    gain_2 = moe_norm[None, :]
    by_side = jnp.arange(experts, dtype=jnp.int32).reshape(groups, 2).T.reshape(experts, 1)
    router_by_side = w_router.reshape(width, groups, 2).transpose(2, 1, 0).reshape(experts, width)
    (
        normed_in, first_scale, qpre, kpre, query, key, values, mixed, mid, mids, grads_full, normed_mid, gates,
        place, rows, grad_rows, *expert_weights,
    ) = run_front(
        layer_input, out_grad, gain_1, gain_2, w_query, w_key, w_value, w_output, gain_q, gain_k,
        cosine, sine, labels, routes.T, by_side, router_by_side, w_gate, w_up, w_down, groups,
    )

    gates_side = jnp.where(first_side, gates[:groups], gates[groups:])
    spots = core * HALF + jnp.arange(HALF, dtype=jnp.int32)
    select_gated = (
        jnp.where(place[:, None, :] == spots[None, :, None], gates_side[:, None, :], 0.0)
        .astype(BF16)
        .reshape(groups * HALF, length)
    )

    expert_out, back_rows, *pieces = run_experts(rows, grad_rows, expert_weights)

    stack, small, mid_grad, keep, sent, returned = run_middle(
        back_rows, expert_out, place, gates, normed_mid, router_by_side, mid, out_grad, mids,
        grads_full, gain_2, normed_in, w_query, w_key, w_value, w_output, gain_q, gain_k, cosine,
        sine, labels, qpre, kpre, query, key, values, mixed,
    )

    big, everywhere, input_grad, layer_output, *halves = run_tail(
        stack, small, keep, sent, layer_input, mid_grad, first_scale, own(attn_norm)[None, :], mid,
        returned.reshape(groups * HALF, width), select_gated, pieces,
    )
    kept, others = halves[:3], halves[3:]
    expert_grads = []
    for mine, other in zip(kept, others):
        other = other.astype(F32)
        expert_grads.append(
            jnp.stack([jnp.where(first_side, mine, other), jnp.where(first_side, other, mine)])
        )
    small = lax.dynamic_index_in_dim(everywhere, rank_t, 0, keepdims=False)
    everywhere = everywhere.astype(F32)
    rows_w = w_query.shape[0]
    rows_o = w_output.shape[0]
    summed = [big[width + i * rows_w : width + (i + 1) * rows_w].astype(F32) for i in range(3)]
    output_grad = jnp.concatenate(
        [big[i * rows_o : (i + 1) * rows_o] for i in range(4)], axis=1
    ).astype(F32)
    return (
        layer_output,
        input_grad,
        everywhere[:, experts].reshape(width),
        summed[0],
        summed[1],
        summed[2],
        small[experts + 2].astype(F32),
        small[experts + 3].astype(F32),
        output_grad,
        everywhere[:, experts + 1].reshape(width),
        everywhere[:, :experts]
        .reshape(4, 2, groups, quarter)
        .transpose(0, 3, 2, 1)
        .reshape(width, experts),
        expert_grads[0],
        expert_grads[1],
        expert_grads[2],
    )


def solution(mesh):
    placed = (
        P("dp", "tensor"),
        P(),
        P(None, "tensor"),
        P(None, "tensor"),
        P(None, "tensor"),
        P("tensor"),
        P("tensor"),
        P("tensor", None),
        P(),
        P(),
        P("dp", None, "tensor"),
        P("dp", None, "tensor"),
        P("dp", "tensor", None),
        P("dp", None),
        P("dp", None),
        P("dp", None),
        P("dp", "tensor"),
    )
    return jax.shard_map(
        per_device,
        mesh=mesh,
        in_specs=placed,
        out_specs=(
            P("dp", "tensor"),
            P("dp", "tensor"),
            P(),
            P(None, "tensor"),
            P(None, "tensor"),
            P(None, "tensor"),
            P("tensor"),
            P("tensor"),
            P("tensor", None),
            P(),
            P(),
            P("dp", None, "tensor"),
            P("dp", None, "tensor"),
            P("dp", "tensor", None),
        ),
        check_vma=False,
    )
```

```python
import functools

import jax
import jax.numpy as jnp
from jax import lax
from jax.experimental import pallas as pl
from jax.experimental.pallas import tpu as pltpu
from jax.sharding import PartitionSpec as P

HDIM = 128
TOP = 8
SLOTS = 64
HALF = SLOTS // 2
EPS = 1e-06
HIGH = lax.Precision.HIGHEST
F32 = jnp.float32
BF16 = jnp.bfloat16
MESH = pl.DeviceIdType.MESH
SMALL = 80
LANES = 128
LATE = 8


def dot(a, b, dims, **kw):
    return lax.dot_general(a, b, (dims, ((), ())), preferred_element_type=F32, **kw)


def nn(a, b):
    return dot(a, b, ((1,), (0,)))


def nt(a, b):
    return dot(a, b, ((1,), (1,)))


def tn(a, b):
    return dot(a, b, ((0,), (0,)))


def cross(value):
    return lax.ppermute(value, "tensor", [(0, 2), (2, 0), (1, 3), (3, 1)])


def swap(value):
    return lax.ppermute(value, "tensor", [(0, 1), (1, 0), (2, 3), (3, 2)])


def inv_rms(value):
    return lax.rsqrt(jnp.mean(value * value, axis=-1, keepdims=True) + EPS)


def rope_angles(places):
    half = HDIM // 2
    frequency = jnp.exp(jnp.arange(half, dtype=F32) * (-2.0 * jnp.log(10000.0) / HDIM))
    angle = places.astype(F32)[:, None] * frequency[None, :]
    cosine, sine = jnp.cos(angle), jnp.sin(angle)
    return (
        jnp.concatenate([cosine, cosine], axis=1),
        jnp.concatenate([-sine, sine], axis=1),
    )


def two_parts(column):
    high = column.astype(BF16)
    rest = (column - high.astype(F32)).astype(BF16)
    lane = lax.broadcasted_iota(jnp.int32, (column.shape[0], LANES), 1)
    return jnp.where(
        lane == 0, high.astype(F32), jnp.where(lane == 1, rest.astype(F32), 0.0)
    ).astype(BF16)


def one_column(pair):
    wide = pair.astype(F32)
    return wide[:, 0:1] + wide[:, 1:2]


def expert_body(
    rows_in, rows_late, og_in, wg_all, wu_all, wd_all,
    out_ref, back_in, kept_g, kept_u, kept_d, got_g, got_u, got_d,
    rows_s, og_s, wgu_s, wd_s, back_s, gu_s, hid_s, keep_s, move_s, down_keep, down_move,
    rs_sem, og_sem, w_sem, bs, br, ls, ks, ms, mr, late_s, late_r,
):
    plane = Plane()
    swap = (plane.dp, lax.axis_index("tensor") + 1 - 2 * plane.core)
    groups, slots, more = rows_s.shape
    width = og_s.shape[2]
    hidden = hid_s.shape[1]
    span = hidden // 4
    per = groups // 4
    tile = per * slots

    late = rows_late.shape[0]
    early = groups - late

    def load(e, _):
        g = plane.source(e)

        @pl.when(e < early)
        def _():
            pltpu.make_async_copy(rows_in.at[g], rows_s.at[e], rs_sem.at[e // per]).start()

        pltpu.make_async_copy(og_in.at[g], og_s.at[e], og_sem.at[e // per]).start()
        return 0

    lax.fori_loop(0, per, load, 0)
    w_copies = []
    for i in range(4):
        at = slice(i * span, (i + 1) * span)
        high = slice(hidden + i * span, hidden + (i + 1) * span)
        w_copies.append(pltpu.make_async_copy(wg_all.at[i], wgu_s.at[:, at], w_sem.at[0, i]))
        w_copies.append(pltpu.make_async_copy(wu_all.at[i], wgu_s.at[:, high], w_sem.at[1, i]))
    for i in range(4):
        at = slice(i * span, (i + 1) * span)
        w_copies.append(pltpu.make_async_copy(wd_all.at[i], wd_s.at[at], w_sem.at[2, i]))
    for c in w_copies:
        c.start()
    lax.fori_loop(per, groups, load, 0)

    barrier = pltpu.get_barrier_semaphore()

    plane.greet(barrier)
    pl.semaphore_signal(barrier, inc=1, device_id=swap, device_id_type=MESH)
    pl.semaphore_wait(barrier, groups)

    def late_copy(i):
        return pltpu.make_async_remote_copy(
            src_ref=rows_late.at[i],
            dst_ref=rows_s.at[early + i],
            send_sem=late_s.at[i],
            recv_sem=late_r.at[i],
            device_id=plane.device(plane.entry(early + i)),
            device_id_type=MESH,
        )

    def late_start(i, _):
        late_copy(i).start()
        return 0

    lax.fori_loop(0, late - 1, late_start, 0)
    own_rows = pltpu.make_async_copy(rows_late.at[late - 1], rows_s.at[groups - 1], ls.at[3])
    own_rows.start()

    def back_copy(e):
        g = plane.source(e)
        return pltpu.make_async_remote_copy(
            src_ref=back_s.at[e],
            dst_ref=back_in.at[plane.dp],
            send_sem=bs.at[e],
            recv_sem=br.at[e],
            device_id=plane.device(g),
            device_id_type=MESH,
        )

    own_back = pltpu.make_async_copy(back_s.at[groups - 1], back_in.at[plane.dp], ls.at[0])

    def one_tile(k, _):
        first = pl.multiple_of(k * per, per)
        here = pl.ds(pl.multiple_of(k * tile, tile), tile)
        part = pl.ds(first, per)

        @pl.when(k < early // per)
        def _():
            pltpu.make_async_copy(rows_in.at[pl.ds(0, per)], rows_s.at[part], rs_sem.at[k]).wait()

        @pl.when(k >= early // per)
        def _():
            def arrive(j, _):
                i = first + j - early

                @pl.when(i < late - 1)
                def _():
                    late_copy(i).wait()

                @pl.when(i == late - 1)
                def _():
                    own_rows.wait()

                return 0

            lax.fori_loop(0, per, arrive, 0)

        @pl.when(k == 0)
        def _():
            for c in w_copies[:8]:
                c.wait()

        mine = rows_s[part].reshape(tile, more)
        rows = mine[:, :width]
        gate = one_column(mine[:, width:])
        both = nn(rows, wgu_s[...])
        gp = both[:, :hidden]
        up = both[:, hidden:]
        sig = jax.nn.sigmoid(gp)
        act = gp * sig
        hid = act * up
        hid_s[here, :] = (gate * hid).astype(BF16)

        @pl.when(k == 0)
        def _():
            for c in w_copies[8:]:
                c.wait()

        low = nn(hid.astype(BF16), wd_s[...]).astype(BF16)
        out_ref[part] = low.reshape(per, slots, width)
        pltpu.make_async_copy(og_in.at[pl.ds(0, per)], og_s.at[part], og_sem.at[k]).wait()
        grads = og_s[part].reshape(tile, width)
        slot = jnp.sum(grads.astype(F32) * low.astype(F32), axis=1, keepdims=True)
        back_s[part, :, width:] = two_parts(slot).reshape(per, slots, more - width)
        hidden_grad = gate * nt(grads, wd_s[...])
        gu_s[here, :hidden] = (hidden_grad * up * sig * (1.0 + gp * (1.0 - sig))).astype(BF16)
        gu_s[here, hidden:] = (hidden_grad * act).astype(BF16)
        back = nt(gu_s[here, :], wgu_s[...]).astype(BF16)
        back_s[part, :, :width] = back.reshape(per, slots, width)

        def send(j, _):
            e = first + j

            @pl.when(e < groups - 1)
            def _():
                back_copy(e).start()

            @pl.when(e == groups - 1)
            def _():
                own_back.start()

            return 0

        lax.fori_loop(0, per, send, 0)
        return 0

    lax.fori_loop(0, 4, one_tile, 0)

    half = hidden // 2
    wide_block = keep_s.shape[1]

    def column_copies(i, slot):
        at = pl.ds(pl.multiple_of(i * wide_block, wide_block), wide_block)
        local = [
            pltpu.make_async_copy(keep_s.at[slot, :, :half], kept_g.at[at], ks.at[slot, 0]),
            pltpu.make_async_copy(keep_s.at[slot, :, half:], kept_u.at[at], ks.at[slot, 1]),
        ]
        far = [
            pltpu.make_async_remote_copy(
                src_ref=move_s.at[slot, :, side],
                dst_ref=target.at[at],
                send_sem=ms.at[slot, n],
                recv_sem=mr.at[i, n],
                device_id=swap,
                device_id_type=MESH,
            )
            for n, (side, target) in enumerate(
                ((slice(0, half), got_g), (slice(half, hidden), got_u))
            )
        ]
        return local + far

    def columns(i, _):
        slot = lax.rem(i, 2)

        @pl.when(i >= 2)
        def _():
            for c in column_copies(i - 2, slot):
                c.wait()

        at = pl.ds(pl.multiple_of(i * wide_block, wide_block), wide_block)
        rows = rows_s[:, :, at].reshape(groups * slots, wide_block)
        grad = tn(rows, gu_s[...])
        keep_s[slot, :, :half] = grad[:, :half]
        keep_s[slot, :, half:] = grad[:, hidden : hidden + half]
        move_s[slot, :, :half] = grad[:, half:hidden].astype(BF16)
        move_s[slot, :, half:] = grad[:, hidden + half :].astype(BF16)
        for c in column_copies(i, slot):
            c.start()
        return 0

    steps = width // wide_block
    lax.fori_loop(0, steps, columns, 0)
    downs = []
    for i in range(4):
        at = slice(i * span, (i + 1) * span)
        grad = tn(hid_s[:, at], og_s[...].reshape(groups * slots, width))
        if i < 2:
            down_keep[at] = grad
            downs.append(pltpu.make_async_copy(down_keep.at[at], kept_d.at[at], ls.at[1 + i]))
        else:
            at = slice((i - 2) * span, (i - 1) * span)
            down_move[at] = grad.astype(BF16)
            downs.append(
                pltpu.make_async_remote_copy(
                    src_ref=down_move.at[at],
                    dst_ref=got_d.at[at],
                    send_sem=ms.at[2, i - 2],
                    recv_sem=mr.at[steps, i - 2],
                    device_id=swap,
                    device_id_type=MESH,
                )
            )
        downs[-1].start()
    for i in (steps - 2, steps - 1):
        for c in column_copies(i, i % 2):
            c.wait()
    for c in downs:
        c.wait()

    def finish(e, _):
        back_copy(e).wait()
        return 0

    lax.fori_loop(0, groups - 1, finish, 0)
    own_back.wait()


def run_experts(rows, late, grads, weights):
    groups, slots, more = rows.shape
    width = grads.shape[2]
    hidden = 4 * weights[0].shape[2]
    half = hidden // 2
    count = groups * slots
    block = 256
    whole = pl.BlockSpec(memory_space=pltpu.VMEM)
    free = pl.BlockSpec(memory_space=pl.ANY)
    f = jax.ShapeDtypeStruct
    vm = pltpu.VMEM
    dma = pltpu.SemaphoreType.DMA
    return pl.pallas_call(
        expert_body,
        in_specs=[free] * 6,
        out_specs=[whole] + [free] * 7,
        out_shape=[
            f((groups, slots, width), BF16),
            f((groups, slots, more), BF16),
            f((width, half), F32),
            f((width, half), F32),
            f((half, width), F32),
            f((width, half), BF16),
            f((width, half), BF16),
            f((half, width), BF16),
        ],
        scratch_shapes=[
            vm((groups, slots, more), BF16),
            vm((groups, slots, width), BF16),
            vm((width, 2 * hidden), BF16),
            vm((hidden, width), BF16),
            vm((groups, slots, more), BF16),
            vm((count, 2 * hidden), BF16),
            vm((count, hidden), BF16),
            vm((2, block, hidden), F32),
            vm((2, block, hidden), BF16),
            vm((half, width), F32),
            vm((half, width), BF16),
            dma((4,)),
            dma((4,)),
            dma((3, 4)),
            dma((31,)),
            dma((31,)),
            dma((4,)),
            dma((2, 2)),
            dma((3, 2)),
            dma((width // block + 1, 2)),
            dma((late.shape[0],)),
            dma((late.shape[0],)),
        ],
        compiler_params=pltpu.CompilerParams(
            collective_id=2, has_side_effects=True, vmem_limit_bytes=61 << 20
        ),
        name="experts",
    )(rows, late, grads, *weights)


def head_scale(pre):
    return lax.rsqrt(jnp.mean(pre * pre, axis=1, keepdims=True) + EPS)


def turn(value, cosine, sine):
    return value * cosine + pltpu.roll(value, HDIM // 2, 1) * sine


def softmax_rows(query, key, same):
    raw = nt(query, key) * HDIM ** (-0.5)
    raw = jnp.where(same, raw, -1e30)
    powered = jnp.exp(raw - jnp.max(raw, axis=1, keepdims=True))
    return powered / jnp.sum(powered, axis=1, keepdims=True)


class Near:
    def __init__(self, send_sems, recv_sems):
        self.dp = lax.axis_index("dp")
        self.t = lax.axis_index("tensor")
        self.core = lax.rem(self.t, 2)
        self.first_core = self.core == 0
        self.low_x = self.t < 2
        self.far = lax.rem(self.t + 2, 4)
        self.swap = (self.dp, self.t + 1 - 2 * self.core)
        self.cross = (self.dp, self.far)
        self.diag = (self.dp, self.far + 1 - 2 * self.core)
        self.sems = (send_sems, recv_sems)
        self.used = 0

    def send(self, source, target, device):
        k = self.used
        self.used = k + 1
        c = pltpu.make_async_remote_copy(
            src_ref=source,
            dst_ref=target,
            send_sem=self.sems[0].at[k],
            recv_sem=self.sems[1].at[k],
            device_id=device,
            device_id_type=MESH,
        )
        c.start()
        return c

    def gather_start(self, buf):
        here = buf.at[self.t]
        return [self.send(here, here, self.cross), self.send(here, here, self.swap)]

    def gather_relay(self, buf, copies):
        copies[0].wait()
        there = buf.at[self.far]
        copies.append(self.send(there, there, self.swap))

    def split(self, part, low_s, high_s, sent):
        quarter = part.shape[1] // 4
        p = [part[:, i * quarter : (i + 1) * quarter] for i in range(4)]
        low_s[...] = jnp.where(self.first_core, p[0], p[1])
        high_s[...] = jnp.where(self.first_core, p[2], p[3])
        sent[:, :quarter] = jnp.where(self.first_core, p[1], p[0]).astype(BF16)
        sent[:, quarter:] = jnp.where(self.first_core, p[3], p[2]).astype(BF16)

    def sum_parts(self, low_s, high_s, sent, got, go, back):
        quarter = go.shape[1]
        self.send(sent, got, self.swap).wait()
        low = low_s[...] + got[:, :quarter].astype(F32)
        high = high_s[...] + got[:, quarter:].astype(F32)
        go[...] = jnp.where(self.low_x, high, low).astype(BF16)
        self.send(go, back, self.cross).wait()
        return jnp.where(self.low_x, low, high) + back[...].astype(F32)


class Plane:
    def __init__(self):
        self.dp = lax.axis_index("dp")
        t = lax.axis_index("tensor")
        self.y = lax.rem(self.dp, 4)
        self.xh = lax.rem(self.dp // 4, 2)
        self.z = self.dp // 8
        self.core = lax.rem(t, 2)
        self.side = lax.rem(t // 2 + self.xh, 2)

    def at(self, dz, dx, dy):
        return (lax.rem(self.z + dz, 4) * 2 + lax.rem(self.xh + dx, 2)) * 4 + lax.rem(
            self.y + dy, 4
        )

    def device(self, group):
        return (group, lax.rem(self.side + lax.rem(group // 4, 2), 2) * 2 + self.core)

    def entry(self, e):
        o = jnp.where(e == 31, 0, lax.rem(11 * e + 5, 31) + 1)
        return self.at(o // 8, lax.rem(o // 4, 2), lax.rem(o, 4))

    def source(self, e):
        o = jnp.where(e == 31, 0, lax.rem(11 * e + 5, 31) + 1)
        return self.at(4 - o // 8, 2 - lax.rem(o // 4, 2), 4 - lax.rem(o, 4))

    def greet(self, barrier):
        def one(e, _):
            pl.semaphore_signal(
                barrier, inc=1, device_id=self.device(self.entry(e)), device_id_type=MESH
            )
            return 0

        lax.fori_loop(0, 31, one, 0)

    def exchange(self, source, target, send_sems, recv_sems, local_sem, back, count=32):
        def copy(e):
            group = self.source(e) if back else self.entry(e)
            return pltpu.make_async_remote_copy(
                src_ref=source.at[e if back else group],
                dst_ref=target.at[self.dp],
                send_sem=send_sems.at[e],
                recv_sem=recv_sems.at[e],
                device_id=self.device(group),
                device_id_type=MESH,
            )

        def start(e, _):
            copy(e).start()
            return 0

        def finish(e, _):
            copy(e).wait()
            return 0

        lax.fori_loop(0, min(count, 31), start, 0)
        if count == 32:
            own = pltpu.make_async_copy(
                source.at[31 if back else self.dp], target.at[self.dp], local_sem
            )
            own.start()

        def wait():
            lax.fori_loop(0, min(count, 31), finish, 0)
            if count == 32:
                own.wait()

        return wait


def wide(buf):
    return jnp.concatenate([buf[i] for i in range(4)], axis=1)


def front_body(
    x_ref, og_ref, gain1_ref, gain2_ref, wq_ref, wk_ref, wv_ref, wo_ref, qn_ref, kn_ref, cos_ref,
    sin_ref, col_ref, row_ref, routes_ref, ids_ref, router_ref, wg_ref, wu_ref, wd_ref,
    normed_ref, fs_ref, qpre_ref, kpre_ref, q_ref, k_ref, v_ref, mixed_ref, mid_ref, mids_ref, ogs_ref,
    nm_ref, gates_ref, place_ref, rows_in, rows_late, og_in, wg_all, wu_all, wd_all,
    xs, low_s, high_s, sent, got, go, back, og_out, rows_out,
    ts, tr, as_, ar, bs, br, ls, late_sem,
):
    near = Near(ts, tr)
    plane = Plane()
    side = plane.side
    barrier = pltpu.get_barrier_semaphore()
    plane.greet(barrier)
    pl.semaphore_signal(barrier, inc=1, device_id=near.swap, device_id_type=MESH)
    pl.semaphore_signal(barrier, inc=1, device_id=near.cross, device_id_type=MESH)
    pl.semaphore_wait(barrier, 33)
    t = near.t
    length = x_ref.shape[0]
    quarter = x_ref.shape[1]
    width = 4 * quarter

    ogs_ref[t] = og_ref[...].astype(BF16)
    og_copies = near.gather_start(ogs_ref)
    xs[t] = x_ref[...].astype(BF16)
    x_copies = near.gather_start(xs)
    weights = ((wg_ref, wg_all), (wu_ref, wu_all), (wd_ref, wd_all))
    kept = [
        pltpu.make_async_copy(w.at[side], w_all.at[0], ls.at[2 + i])
        for i, (w, w_all) in enumerate(weights)
    ]
    w_cross = [near.send(wg_ref.at[1 - side], wg_all.at[1], near.cross)]

    chosen = routes_ref[0:1, :] == ids_ref[...]
    for k in range(1, TOP):
        chosen = jnp.logical_or(chosen, routes_ref[k : k + 1, :] == ids_ref[...])
    mask = jnp.where(chosen, 1.0, 0.0)
    earlier = lax.broadcasted_iota(jnp.int32, (length, length), 0) < lax.broadcasted_iota(
        jnp.int32, (length, length), 1
    )
    rank = nn(mask.astype(BF16), jnp.where(earlier, 1.0, 0.0).astype(BF16))
    rank = jnp.where(chosen, rank, -1.0).astype(jnp.int32)
    experts = rank.shape[0] // 2
    place_ref[...] = jnp.where(side == 0, rank[:experts], rank[experts:])
    base = near.core * HALF

    def hits(i):
        place = place_ref[i * 8 : (i + 1) * 8, :]
        spots = lax.broadcasted_iota(jnp.int32, (8, HALF, length), 1) + base
        return jnp.broadcast_to(place[:, None, :], (8, HALF, length)) == spots

    near.gather_relay(ogs_ref, og_copies)
    near.gather_relay(xs, x_copies)
    for c in og_copies[1:]:
        c.wait()
    og = wide(ogs_ref)
    for i in range(experts // 8):
        select = jnp.where(hits(i), 1.0, 0.0).reshape(8 * HALF, length).astype(BF16)
        og_out[i * 8 : (i + 1) * 8] = nn(select, og).astype(BF16).reshape(8, HALF, width)
    og_wait = plane.exchange(og_out, og_in, as_, ar, ls.at[0], False)
    for c in kept:
        c.start()
    w_swap = [near.send(w.at[side], w_all.at[2], near.swap) for w, w_all in weights]

    for c in x_copies[1:]:
        c.wait()
    x = wide(xs).astype(F32)
    scale = lax.rsqrt(jnp.mean(x * x, axis=1, keepdims=True) + EPS)
    fs_ref[...] = scale
    normed = (x * scale * gain1_ref[...]).astype(BF16)
    normed_ref[...] = normed
    qpre = nn(normed, wq_ref[...])
    kpre = nn(normed, wk_ref[...])
    qpre_ref[...] = qpre
    kpre_ref[...] = kpre
    v_ref[...] = nn(normed, wv_ref[...]).astype(BF16)
    cosine = cos_ref[...]
    sine = sin_ref[...]
    same = col_ref[...] == row_ref[...]
    for h in range(q_ref.shape[1] // HDIM):
        at = slice(h * HDIM, (h + 1) * HDIM)
        qh = qpre[:, at]
        kh = kpre[:, at]
        query = turn(qh * head_scale(qh) * qn_ref[:, at], cosine, sine).astype(BF16)
        key = turn(kh * head_scale(kh) * kn_ref[:, at], cosine, sine).astype(BF16)
        q_ref[:, at] = query
        k_ref[:, at] = key
        probs = softmax_rows(query, key, same).astype(BF16)
        mixed_ref[:, at] = nn(probs, v_ref[:, at]).astype(BF16)
    near.split(nn(mixed_ref[...], wo_ref[...]), low_s, high_s, sent)
    mid = x_ref[...] + near.sum_parts(low_s, high_s, sent, got, go, back)
    mid_ref[...] = mid
    mids_ref[t] = mid.astype(BF16)
    mid_copies = near.gather_start(mids_ref)
    w_cross.append(near.send(wu_ref.at[1 - side], wu_all.at[1], near.cross))
    w_cross.append(near.send(wd_ref.at[1 - side], wd_all.at[1], near.cross))
    near.gather_relay(mids_ref, mid_copies)
    for c in mid_copies[1:]:
        c.wait()
    mid = wide(mids_ref).astype(F32)
    scale = lax.rsqrt(jnp.mean(mid * mid, axis=1, keepdims=True) + EPS)
    normed = (mid * scale * gain2_ref[...]).astype(BF16)
    nm_ref[...] = normed

    logits = nt(router_ref[...], normed)
    masked = jnp.where(chosen, logits, -1e30)
    raised = jnp.where(chosen, jnp.exp(masked - jnp.max(masked, axis=0, keepdims=True)), 0.0)
    gates = raised / jnp.sum(raised, axis=0, keepdims=True)
    gates_ref[...] = gates
    gates_side = jnp.where(side == 0, gates[:experts], gates[experts:])
    for i in range(experts // 8):
        hit = hits(i)
        select = jnp.where(hit, 1.0, 0.0).reshape(8 * HALF, length).astype(BF16)
        rows_out[i * 8 : (i + 1) * 8, :, :width] = (
            nn(select, normed).astype(BF16).reshape(8, HALF, width)
        )
        gate = jnp.broadcast_to(gates_side[i * 8 : (i + 1) * 8][:, None, :], (8, HALF, length))
        column = jnp.sum(
            jnp.where(hit, gate, 0.0).reshape(8 * HALF, length), axis=1, keepdims=True
        )
        rows_out[i * 8 : (i + 1) * 8, :, width:] = two_parts(column).reshape(8, HALF, LANES)
    early = 32 - rows_late.shape[0]
    rows_wait = plane.exchange(rows_out, rows_in, bs, br, ls.at[1], False, early)

    def late_copy(i):
        return pltpu.make_async_copy(
            rows_out.at[plane.entry(early + i)], rows_late.at[i], late_sem.at[i]
        )

    def late_start(i, _):
        late_copy(i).start()
        return 0

    def late_wait(i, _):
        late_copy(i).wait()
        return 0

    lax.fori_loop(0, 32 - early, late_start, 0)
    for c, (w, w_all) in zip(w_cross, weights):
        c.wait()
        w_swap.append(near.send(w_all.at[1], w_all.at[3], near.swap))
    og_wait()
    rows_wait()
    lax.fori_loop(0, 32 - early, late_wait, 0)
    for c in w_swap + kept:
        c.wait()


def run_front(
    x, og, gain1, gain2, wq, wk, wv, wo, qn, kn, cosine, sine, labels, routes, ids, router, wg, wu,
    wd, groups,
):
    length, quarter = x.shape
    width = 4 * quarter
    inner = wq.shape[1]
    whole = pl.BlockSpec(memory_space=pltpu.VMEM)
    free = pl.BlockSpec(memory_space=pl.ANY)
    f = jax.ShapeDtypeStruct
    vm = pltpu.VMEM
    dma = pltpu.SemaphoreType.DMA
    return pl.pallas_call(
        front_body,
        in_specs=[whole] * 17 + [free] * 3,
        out_specs=[whole] * 14 + [free] * 6,
        out_shape=[
            f((length, width), BF16),
            f((length, 1), F32),
            f((length, inner), F32),
            f((length, inner), F32),
            f((length, inner), BF16),
            f((length, inner), BF16),
            f((length, inner), BF16),
            f((length, inner), BF16),
            f((length, quarter), F32),
            f((4, length, quarter), BF16),
            f((4, length, quarter), BF16),
            f((length, width), BF16),
            f((2 * groups, length), F32),
            f((groups, length), jnp.int32),
            f((groups, HALF, width + LANES), BF16),
            f((LATE, HALF, width + LANES), BF16),
            f((groups, HALF, width), BF16),
            f((4,) + wg.shape[1:], BF16),
            f((4,) + wu.shape[1:], BF16),
            f((4,) + wd.shape[1:], BF16),
        ],
        scratch_shapes=[
            vm((4, length, quarter), BF16),
            vm((length, quarter), F32),
            vm((length, quarter), F32),
            vm((length, 2 * quarter), BF16),
            vm((length, 2 * quarter), BF16),
            vm((length, quarter), BF16),
            vm((length, quarter), BF16),
            vm((groups, HALF, width), BF16),
            vm((groups, HALF, width + LANES), BF16),
            dma((20,)),
            dma((20,)),
            dma((31,)),
            dma((31,)),
            dma((31,)),
            dma((31,)),
            dma((5,)),
            dma((LATE,)),
        ],
        compiler_params=pltpu.CompilerParams(
            collective_id=1, has_side_effects=True, vmem_limit_bytes=60 << 20
        ),
        name="front",
    )(
        x, og, gain1, gain2, wq, wk, wv, wo, qn, kn, cosine, sine, labels[:, None], labels[None, :],
        routes, ids, router, wg, wu, wd,
    )


def middle_body(
    rows_ref, out_rows, place_ref, gates_ref, nm_ref, router_ref, mid_ref, og_ref, mids_ref, ogs_ref,
    gain_ref, normed_in, wq_in, wk_in, wv_in, wo_in, qn_ref, kn_ref, cos_ref, sin_ref, col_ref,
    row_ref, qpre_ref, kpre_ref, q_ref, k_ref, v_ref, mixed_ref,
    stack_ref, small_ref, mid_grad_ref, keep_ref, sent_ref, returned,
    low_s, low_f, high_f, sent, got, go, back, ngs, gg_s, probs_s, normed_ref, wq_ref, wk_ref, wv_ref,
    wo_ref, ts, tr, os, orr, ls,
):
    near = Near(ts, tr)
    plane = Plane()
    loads = [
        pltpu.make_async_copy(source, target, ls.at[1 + i])
        for i, (source, target) in enumerate(
            (
                (wo_in, wo_ref),
                (wq_in, wq_ref),
                (wk_in, wk_ref),
                (wv_in, wv_ref),
                (normed_in, normed_ref),
            )
        )
    ]
    for c in loads:
        c.start()
    side = plane.side
    t = near.t
    groups, slots, more = rows_ref.shape
    length, width = normed_ref.shape
    quarter = width // 4
    inner = q_ref.shape[1]

    barrier = pltpu.get_barrier_semaphore()

    plane.greet(barrier)
    pl.semaphore_signal(barrier, inc=1, device_id=near.swap, device_id_type=MESH)
    pl.semaphore_signal(barrier, inc=1, device_id=near.cross, device_id_type=MESH)
    pl.semaphore_wait(barrier, groups + 1)

    out_wait = plane.exchange(out_rows, returned, os, orr, ls.at[0], True)

    base = near.core * slots
    part = None
    for i in range(groups // 8):
        at = slice(i * 8, (i + 1) * 8)
        spots = lax.broadcasted_iota(jnp.int32, (8, slots, length), 1) + base
        hit = jnp.broadcast_to(place_ref[at, :][:, None, :], (8, slots, length)) == spots
        select = jnp.where(hit, 1.0, 0.0).reshape(8 * slots, length)
        tile = rows_ref[at].reshape(8 * slots, more)
        column = one_column(tile[:, width:])
        gg_s[0, at] = jnp.sum((select * column).reshape(8, slots, length), axis=1)
        term = tn(select.astype(BF16), tile[:, :width])
        part = term if part is None else part + term
    gate_swap = near.send(gg_s.at[0], gg_s.at[1], near.swap)
    near.split(part, low_f, high_f, sent)
    swapped = near.send(sent, got, near.swap)
    gate_swap.wait()
    gg_s[2] = gg_s[0] + gg_s[1]
    gate_cross = near.send(gg_s.at[2], gg_s.at[3], near.cross)
    swapped.wait()
    low = low_f[...] + got[:, :quarter].astype(F32)
    high = high_f[...] + got[:, quarter:].astype(F32)
    go[...] = jnp.where(near.low_x, high, low).astype(BF16)
    crossed = near.send(go, back, near.cross)
    gate_cross.wait()
    own, other = gg_s[2], gg_s[3]
    gate_grad = jnp.concatenate(
        [jnp.where(side == 0, own, other), jnp.where(side == 0, other, own)], axis=0
    )
    gates = gates_ref[...]
    logit_grad = gates * (gate_grad - jnp.sum(gates * gate_grad, axis=0, keepdims=True))
    mine = pl.ds(pl.multiple_of(t * quarter, quarter), quarter)
    router_back = dot(
        logit_grad, router_ref[:, mine].astype(F32), ((0,), (0,)), precision=HIGH
    )
    experts = gates.shape[0]
    small_ref[:experts, :] = dot(
        logit_grad, nm_ref[:, mine].astype(F32), ((1,), (0,)), precision=HIGH
    ).astype(BF16)
    mid = wide(mids_ref).astype(F32)
    scale = lax.rsqrt(jnp.mean(mid * mid, axis=1, keepdims=True) + EPS)
    mid_own = mid_ref[...]
    same = col_ref[...] == row_ref[...]
    heads = inner // HDIM

    def attention_probs(h):
        at = slice(h * HDIM, (h + 1) * HDIM)
        probs_s[h] = softmax_rows(q_ref[:, at], k_ref[:, at], same)

    for h in range(heads // 2):
        attention_probs(h)
    crossed.wait()
    ng = jnp.where(near.low_x, low, high) + back[...].astype(F32) + router_back
    ngs[t] = ng.astype(BF16)
    ng_copies = near.gather_start(ngs)
    moe = jnp.sum(ng * mid_own * scale, axis=0, keepdims=True)
    for h in range(heads // 2, heads):
        attention_probs(h)
    near.gather_relay(ngs, ng_copies)
    for c in ng_copies[1:]:
        c.wait()

    weighted = wide(ngs).astype(F32) * gain_ref[...]
    shrink = scale * scale * scale * jnp.mean(weighted * mid, axis=1, keepdims=True)
    mid_grad_ref[...] = og_ref[...] + scale * (ng * gain_ref[:, mine]) - mid_own * shrink
    attn_grad = (wide(ogs_ref).astype(F32) + scale * weighted - mid * shrink).astype(BF16)

    for c in loads:
        c.wait()
    wo_grad = tn(mixed_ref[...], attn_grad).astype(BF16)
    for i in range(4):
        stack_ref[i * inner : (i + 1) * inner, :] = wo_grad[:, i * quarter : (i + 1) * quarter]
    mixed_grad = nt(attn_grad, wo_ref[...]).astype(BF16)
    cosine = cos_ref[...]
    sine = sin_ref[...]
    factor = HDIM ** (-0.5)

    def norm_back(pre, gain, rotated):
        grad = rotated * cosine - pltpu.roll(rotated, HDIM // 2, 1) * sine
        head = head_scale(pre)
        weighted = grad * gain
        mean = jnp.mean(weighted * pre, axis=1, keepdims=True)
        low = (head * weighted - pre * (head * head * head * mean)).astype(BF16)
        return low, jnp.sum(grad * pre * head, axis=0, keepdims=True)

    q_sums, k_sums = [], []
    for h in range(inner // HDIM):
        at = slice(h * HDIM, (h + 1) * HDIM)
        query = q_ref[:, at]
        key = k_ref[:, at]
        mg = mixed_grad[:, at]
        probs = probs_s[h]
        low_s[:, 2 * inner + h * HDIM : 2 * inner + (h + 1) * HDIM] = tn(
            probs.astype(BF16), mg
        ).astype(BF16)
        prob_grad = nt(mg, v_ref[:, at])
        weighted_p = probs * prob_grad
        score = (weighted_p - probs * jnp.sum(weighted_p, axis=1, keepdims=True)).astype(BF16)
        low_q, total = norm_back(qpre_ref[:, at], qn_ref[:, at], nn(score, key) * factor)
        low_s[:, h * HDIM : (h + 1) * HDIM] = low_q
        q_sums.append(total)
        low_k, total = norm_back(kpre_ref[:, at], kn_ref[:, at], tn(score, query) * factor)
        low_s[:, inner + h * HDIM : inner + (h + 1) * HDIM] = low_k
        k_sums.append(total)
    row = lax.broadcasted_iota(jnp.int32, (small_ref.shape[0] - experts, quarter), 0)
    rest = jnp.zeros(row.shape, F32)
    for i, value in enumerate(
        (moe, jnp.concatenate(q_sums, axis=1), jnp.concatenate(k_sums, axis=1))
    ):
        rest = jnp.where(row == i + 1, jnp.broadcast_to(value, row.shape), rest)
    small_ref[experts:, :] = rest.astype(BF16)
    part = None
    for i, w in enumerate((wq_ref, wk_ref, wv_ref)):
        term = nt(low_s[:, i * inner : (i + 1) * inner], w[...])
        part = term if part is None else part + term
    near.split(part, low_f, high_f, sent_ref)
    keep_ref[:, :quarter] = low_f[...]
    keep_ref[:, quarter:] = high_f[...]
    normed = normed_ref[...]
    for i in range(3):
        stack_ref[(i + 1) * width : (i + 2) * width, :] = tn(
            normed, low_s[:, i * inner : (i + 1) * inner]
        ).astype(BF16)

    out_wait()


def run_middle(
    rows, out_rows, place, gates, nm, router, mid, og, mids, ogs, gain, normed, wq, wk, wv, wo, qn,
    kn, cosine, sine, labels, qpre, kpre, q, k, v, mixed,
):
    length, width = normed.shape
    quarter = width // 4
    groups = place.shape[0]
    inner = wq.shape[1]
    whole = pl.BlockSpec(memory_space=pltpu.VMEM)
    free = pl.BlockSpec(memory_space=pl.ANY)
    f = jax.ShapeDtypeStruct
    vm = pltpu.VMEM
    dma = pltpu.SemaphoreType.DMA
    return pl.pallas_call(
        middle_body,
        in_specs=[whole, free] + [whole] * 9 + [free] * 5 + [whole] * 12,
        out_specs=[whole] * 5 + [free],
        out_shape=[
            f((4 * width, quarter), BF16),
            f((SMALL, quarter), BF16),
            f((length, quarter), F32),
            f((length, 2 * quarter), F32),
            f((length, 2 * quarter), BF16),
            f(out_rows.shape, BF16),
        ],
        scratch_shapes=[
            vm((length, 3 * inner), BF16),
            vm((length, quarter), F32),
            vm((length, quarter), F32),
            vm((length, 2 * quarter), BF16),
            vm((length, 2 * quarter), BF16),
            vm((length, quarter), BF16),
            vm((length, quarter), BF16),
            vm((4, length, quarter), BF16),
            vm((4, groups, length), F32),
            vm((inner // HDIM, length, length), F32),
            vm(normed.shape, BF16),
            vm(wq.shape, BF16),
            vm(wk.shape, BF16),
            vm(wv.shape, BF16),
            vm(wo.shape, BF16),
            dma((8,)),
            dma((8,)),
            dma((31,)),
            dma((31,)),
            dma((6,)),
        ],
        compiler_params=pltpu.CompilerParams(
            collective_id=3, has_side_effects=True, vmem_limit_bytes=61 << 20
        ),
        name="middle",
    )(
        rows, out_rows, place, gates, nm, router, mid, og, mids, ogs, gain, normed, wq, wk, wv, wo,
        qn, kn, cosine, sine, labels[:, None], labels[None, :], qpre, kpre, q, k, v, mixed,
    )


def tail_body(
    stack_ref, small_ref, keep_ref, sent_ref, x_ref, mid_grad_ref, fs_ref, gain_ref, mid_ref,
    ret_ref, sel_ref, kept_g, kept_u, kept_d, got_g, got_u, got_d,
    out_ref, small_out_ref, input_ref, layer_ref, mine_g, mine_u, mine_d, other_g, other_u, other_d,
    own_s, ret_s, recv1, buf1, recv2, buf2, recv3, small_in, got, out_sent, out_got, go, back, out_go, out_back,
    mean_in, kb, gb, nb, kd, gd, far_g, far_u, far_d, ss, rs, sss, srs, ts, tr, ws, ls,
):
    dp = lax.axis_index("dp")
    t = lax.axis_index("tensor")
    y = lax.rem(dp, 4)
    xh = lax.rem(dp // 4, 2)
    z = dp // 8
    core = lax.rem(t, 2)
    first_core = core == 0
    low_x = t < 2
    half = stack_ref.shape[0] // 2
    size = half // 2
    n1, n2, n3 = size // 4, size // 16, size // 32
    quarter = x_ref.shape[1]
    ret_load = pltpu.make_async_copy(ret_ref, ret_s, ls.at[4])
    ret_load.start()

    def at_z(k):
        return ((lax.rem(z + k, 4) * 2 + xh) * 4 + y, t)

    def at_y(k):
        return ((z * 2 + xh) * 4 + lax.rem(y + k, 4), t)

    at_x = ((z * 2 + 1 - xh) * 4 + y, t)
    at_swap = (dp, t + 1 - 2 * core)
    at_cross = (dp, lax.rem(t + 2, 4))
    at_diag = (dp, lax.rem(t + 2, 4) + 1 - 2 * core)

    barrier = pltpu.get_barrier_semaphore()
    for k in range(1, 4):
        pl.semaphore_signal(barrier, inc=1, device_id=at_z(k), device_id_type=MESH)
        pl.semaphore_signal(barrier, inc=1, device_id=at_y(k), device_id_type=MESH)
    for there in (at_x, at_swap, at_cross, at_diag):
        pl.semaphore_signal(barrier, inc=1, device_id=there, device_id_type=MESH)
    pl.semaphore_wait(barrier, 10)

    def send(source, target, sems, device):
        c = pltpu.make_async_remote_copy(
            src_ref=source,
            dst_ref=target,
            send_sem=sems[0],
            recv_sem=sems[1],
            device_id=device,
            device_id_type=MESH,
        )
        c.start()
        return c

    def copy(source, target, phase, h, k, device):
        return send(source, target, (ss.at[phase, h, k], rs.at[phase, h, k]), device)

    def small_copy(slot, k, device):
        return send(small_in.at[slot], small_in.at[slot], (sss.at[k], srs.at[k]), device)

    def near(source, target, k, device):
        return send(source, target, (ts.at[k], tr.at[k]), device)

    def rows_at(start, size):
        return pl.ds(pl.multiple_of(start, 64), size)

    ways = (((z, at_z), (y, at_y)), ((y, at_y), (z, at_z)))
    streams = [(ways[h], h * half + s * size) for s in range(2) for h in range(2)]
    first, second, third, ahead, later, ended, own_loads, bases = [], [], [], [], [], [], [], []
    for n, (((pos, at), _), start) in enumerate(streams):
        for k in range(1, 4):
            there = rows_at(start + lax.rem(pos + k, 4) * n1, n1)
            first.append(copy(stack_ref.at[there], recv1.at[n, k - 1], 0, n, k - 1, at(k)))
        bases.append(start + pos * n1)
    for n, base in enumerate(bases):
        own_loads.append(
            pltpu.make_async_copy(stack_ref.at[rows_at(base, n1)], own_s.at[n], ls.at[n])
        )
        own_loads[-1].start()

    swapped = near(sent_ref, got, 0, at_swap)
    ret_load.wait()
    part = tn(sel_ref[...], ret_s[...])
    p = [part[:, i * quarter : (i + 1) * quarter] for i in range(4)]
    out_sent[:, :quarter] = jnp.where(first_core, p[1], p[0]).astype(BF16)
    out_sent[:, quarter:] = jnp.where(first_core, p[3], p[2]).astype(BF16)
    out_low = jnp.where(first_core, p[0], p[1])
    out_high = jnp.where(first_core, p[2], p[3])
    out_swapped = near(out_sent, out_got, 1, at_swap)
    swapped.wait()
    low_half = keep_ref[:, :quarter] + got[:, :quarter].astype(F32)
    high_half = keep_ref[:, quarter:] + got[:, quarter:].astype(F32)
    go[...] = jnp.where(low_x, high_half, low_half).astype(BF16)
    crossed = near(go, back, 2, at_cross)
    in_mine = jnp.where(low_x, low_half, high_half)
    out_swapped.wait()
    out_low = out_low + out_got[:, :quarter].astype(F32)
    out_high = out_high + out_got[:, quarter:].astype(F32)
    out_go[...] = jnp.where(low_x, out_high, out_low).astype(BF16)
    crossed.wait()
    in_grad = in_mine + back[...].astype(F32)
    x = x_ref[...]
    fs = fs_ref[...]
    weighted = in_grad * gain_ref[...]
    mean = jnp.sum(weighted * x, axis=1, keepdims=True)
    mean_in[0] = jnp.broadcast_to(mean, mean_in.shape[1:])
    mean_swap = near(mean_in.at[0], mean_in.at[1], 3, at_swap)
    row = lax.broadcasted_iota(jnp.int32, (16, quarter), 0)
    norm_row = jnp.sum(in_grad * x * fs, axis=0, keepdims=True)
    small_in[z] = small_ref[...]
    last = small_ref.shape[0] - 16
    small_in[z, last:, :] = jnp.where(
        row == 0, jnp.broadcast_to(norm_row, (16, quarter)), small_ref[last:, :].astype(F32)
    ).astype(BF16)
    small = [small_copy(z, k - 1, at_z(k)) for k in range(1, 4)]
    mean_swap.wait()
    mean_in[2] = mean_in[0] + mean_in[1]
    mean_cross = near(mean_in.at[2], mean_in.at[3], 4, at_cross)
    out_crossed = near(out_go, out_back, 5, at_cross)
    mean_cross.wait()
    mean = (mean_in[2] + mean_in[3])[:, 0:1] / (4 * quarter)
    input_ref[...] = mid_grad_ref[...] + fs * weighted - x * (fs * fs * fs * mean)
    out_crossed.wait()
    layer_ref[...] = mid_ref[...] + (jnp.where(low_x, out_low, out_high) + out_back[...].astype(F32))

    block = kb.shape[1]
    span = far_d.shape[0]

    def column_sums(kept, gotten, far, mine):
        loads, stores = [], []
        count = kept.shape[0] // block
        for i in range(count):
            at = slice(i * block, (i + 1) * block)
            loads.append(
                (
                    pltpu.make_async_copy(kept.at[at], kb.at[i % 2], ws.at[i % 2, 0]),
                    pltpu.make_async_copy(gotten.at[at], gb.at[i % 2], ws.at[i % 2, 1]),
                )
            )
        for c in loads[0]:
            c.start()
        for i in range(count):
            if i + 1 < count:
                for c in loads[i + 1]:
                    c.start()
            for c in loads[i]:
                c.wait()
            slot = i % 2
            at = slice(i * block, (i + 1) * block)
            total = kb[slot] + gb[slot].astype(F32)
            if i >= 2:
                stores[i - 2].wait()
            nb[slot] = total[:, :span]
            far[at, :] = total[:, span:].astype(BF16)
            stores.append(pltpu.make_async_copy(nb.at[slot], mine.at[at], ws.at[slot, 2]))
            stores[-1].start()
        for c in stores[-2:]:
            c.wait()

    def row_sums():
        loads = [
            (
                pltpu.make_async_copy(kept_d.at[at], kd.at[i], ws.at[2 + i, 0]),
                pltpu.make_async_copy(got_d.at[at], gd.at[i], ws.at[2 + i, 1]),
            )
            for i, at in enumerate((slice(span, 2 * span), slice(0, span)))
        ]
        for pair in loads:
            for c in pair:
                c.start()
        for c in loads[0]:
            c.wait()
        far_d[...] = (kd[0] + gd[0].astype(F32)).astype(BF16)
        others.append(near(far_d, other_d, 8, at_cross))
        for c in loads[1]:
            c.wait()
        kd[1] = kd[1] + gd[1].astype(F32)
        store = pltpu.make_async_copy(kd.at[1], mine_d, ws.at[2, 2])
        store.start()
        return store

    def small_total(start, count):
        total = small_in[start].astype(F32)
        for i in range(start + 1, start + count):
            total = total + small_in[i].astype(F32)
        return total.astype(BF16)

    def first_sum(n):
        for c in first[3 * n : 3 * n + 3]:
            c.wait()
        own_loads[n].wait()
        total = own_s[n].astype(F32)
        for k in range(3):
            total = total + recv1[n, k].astype(F32)
        buf1[n] = total.astype(BF16)
        _, (pos, at) = streams[n][0]
        for k in range(1, 4):
            there = rows_at(lax.rem(pos + k, 4) * n2, n2)
            second.append(copy(buf1.at[n, there], recv2.at[n, k - 1], 1, n, k - 1, at(k)))
        bases[n] = bases[n] + pos * n2

    def second_sum(n):
        for c in second[3 * n : 3 * n + 3]:
            c.wait()
        _, (pos, _) = streams[n][0]
        total = buf1[n, rows_at(pos * n2, n2), :].astype(F32)
        for k in range(3):
            total = total + recv2[n, k].astype(F32)
        buf2[n] = total.astype(BF16)
        third.append(
            copy(buf2.at[n, rows_at((1 - xh) * n3, n3)], recv3.at[n], 2, n, 0, at_x)
        )

    def third_sum(n):
        third[n].wait()
        total = buf2[n, rows_at(xh * n3, n3), :].astype(F32) + recv3[n].astype(F32)
        here = rows_at(bases[n] + xh * n3, n3)
        out_ref[here, :] = total.astype(BF16)
        ahead.append(copy(out_ref.at[here], out_ref.at[here], 3, n, 0, at_x))

    def share_second(n):
        ahead[n].wait()
        here = rows_at(bases[n], n2)
        _, (_, at) = streams[n][0]
        for k in range(1, 4):
            later.append(copy(out_ref.at[here], out_ref.at[here], 4, n, k - 1, at(k)))

    def share_first(n):
        for c in later[3 * n : 3 * n + 3]:
            c.wait()
        ((pos, at), _), start = streams[n]
        here = rows_at(start + pos * n1, n1)
        for k in range(1, 4):
            ended.append(copy(out_ref.at[here], out_ref.at[here], 5, n, k - 1, at(k)))

    column_sums(kept_g, got_g, far_g, mine_g)
    others = [near(far_g, other_g, 6, at_cross)]
    first_sum(0)
    first_sum(1)
    column_sums(kept_u, got_u, far_u, mine_u)
    first_sum(2)
    first_sum(3)
    for c in small:
        c.wait()
    small_in[4 + y] = small_total(0, 4)
    small = [small_copy(4 + y, 3 + k - 1, at_y(k)) for k in range(1, 4)]
    second_sum(0)
    second_sum(1)
    third_sum(0)
    third_sum(1)
    second_sum(2)
    second_sum(3)
    for c in small:
        c.wait()
    small_in[8 + xh] = small_total(4, 4)
    small = small_copy(8 + xh, 6, at_x)
    share_second(0)
    share_second(1)
    third_sum(2)
    third_sum(3)
    share_first(0)
    share_first(1)
    share_second(2)
    share_second(3)
    others.append(near(far_u, other_u, 7, at_cross))
    share_first(2)
    share_first(3)
    small.wait()
    small_out_ref[t] = small_total(8, 2)
    small = [
        near(small_out_ref.at[t], small_out_ref.at[t], 9 + i, there)
        for i, there in enumerate((at_swap, at_cross, at_diag))
    ]
    row_sums().wait()
    for c in small + others + ended:
        c.wait()


def run_tail(
    stack, small, keep, sent, x, mid_grad, fs, gain, mid, returned, select, pieces
):
    rows, cols = stack.shape
    half = rows // 2
    length = x.shape[0]
    deep, wide_half = pieces[0].shape
    span = wide_half // 2
    shapes = [(deep, span), (deep, span), (span, deep)]
    whole = pl.BlockSpec(memory_space=pltpu.VMEM)
    free = pl.BlockSpec(memory_space=pl.ANY)
    f = jax.ShapeDtypeStruct
    vm = pltpu.VMEM
    return pl.pallas_call(
        tail_body,
        in_specs=[free] + [whole] * 8 + [free, whole] + [free] * 6,
        out_specs=[whole] * 4 + [free] * 6,
        out_shape=[
            f(stack.shape, BF16),
            f((4,) + small.shape, BF16),
            f(x.shape, F32),
            f(x.shape, F32),
        ]
        + [f(shape, F32) for shape in shapes]
        + [f(shape, BF16) for shape in shapes],
        scratch_shapes=[
            vm((4, half // 8, cols), BF16),
            vm(returned.shape, BF16),
            vm((4, 3, half // 8, cols), BF16),
            vm((4, half // 8, cols), BF16),
            vm((4, 3, half // 32, cols), BF16),
            vm((4, half // 32, cols), BF16),
            vm((4, half // 64, cols), BF16),
            vm((10,) + small.shape, BF16),
            vm((length, 2 * cols), BF16),
            vm((length, 2 * cols), BF16),
            vm((length, 2 * cols), BF16),
            vm((length, cols), BF16),
            vm((length, cols), BF16),
            vm((length, cols), BF16),
            vm((length, cols), BF16),
            vm((4, length, LANES), F32),
            vm((2, 512, wide_half), F32),
            vm((2, 512, wide_half), BF16),
            vm((2, 512, span), F32),
            vm((2, span, deep), F32),
            vm((2, span, deep), BF16),
            vm((deep, span), BF16),
            vm((deep, span), BF16),
            vm((span, deep), BF16),
            pltpu.SemaphoreType.DMA((6, 4, 3)),
            pltpu.SemaphoreType.DMA((6, 4, 3)),
            pltpu.SemaphoreType.DMA((7,)),
            pltpu.SemaphoreType.DMA((7,)),
            pltpu.SemaphoreType.DMA((12,)),
            pltpu.SemaphoreType.DMA((12,)),
            pltpu.SemaphoreType.DMA((4, 3)),
            pltpu.SemaphoreType.DMA((5,)),
        ],
        compiler_params=pltpu.CompilerParams(
            collective_id=0, has_side_effects=True, vmem_limit_bytes=62 << 20
        ),
        cost_estimate=pl.CostEstimate(flops=0, bytes_accessed=500_000_000, transcendentals=0),
        name="sum_over_dp",
    )(stack, small, keep, sent, x, mid_grad, fs, gain, mid, returned, select, *pieces)


def per_device(
    layer_input,
    attn_norm,
    w_query,
    w_key,
    w_value,
    query_norm,
    key_norm,
    w_output,
    moe_norm,
    w_router,
    w_gate,
    w_up,
    w_down,
    segments,
    positions,
    routes,
    out_grad,
):
    length, quarter = layer_input.shape
    width = 4 * quarter
    rank_t = lax.axis_index("tensor")
    core = rank_t % 2
    low_x = rank_t // 2 == 0
    high_group = (lax.axis_index("dp") // 4) % 2 == 1
    first_side = jnp.logical_xor(low_x, high_group)
    groups = lax.axis_size("dp")
    experts = 2 * groups

    def own(vector):
        return lax.dynamic_slice_in_dim(vector, rank_t * quarter, quarter, 0)

    cosine, sine = rope_angles(positions[0])
    labels = segments[0]
    gain_q = query_norm[None, :]
    gain_k = key_norm[None, :]
    gain_1 = attn_norm[None, :]
    gain_2 = moe_norm[None, :]
    by_side = jnp.arange(experts, dtype=jnp.int32).reshape(groups, 2).T.reshape(experts, 1)
    router_by_side = w_router.reshape(width, groups, 2).transpose(2, 1, 0).reshape(experts, width)
    (
        normed_in, first_scale, qpre, kpre, query, key, values, mixed, mid, mids, grads_full, normed_mid, gates,
        place, rows, late_rows, grad_rows, *expert_weights,
    ) = run_front(
        layer_input, out_grad, gain_1, gain_2, w_query, w_key, w_value, w_output, gain_q, gain_k,
        cosine, sine, labels, routes.T, by_side, router_by_side, w_gate, w_up, w_down, groups,
    )

    gates_side = jnp.where(first_side, gates[:groups], gates[groups:])
    spots = core * HALF + jnp.arange(HALF, dtype=jnp.int32)
    select_gated = (
        jnp.where(place[:, None, :] == spots[None, :, None], gates_side[:, None, :], 0.0)
        .astype(BF16)
        .reshape(groups * HALF, length)
    )

    expert_out, back_rows, *pieces = run_experts(rows, late_rows, grad_rows, expert_weights)

    stack, small, mid_grad, keep, sent, returned = run_middle(
        back_rows, expert_out, place, gates, normed_mid, router_by_side, mid, out_grad, mids,
        grads_full, gain_2, normed_in, w_query, w_key, w_value, w_output, gain_q, gain_k, cosine,
        sine, labels, qpre, kpre, query, key, values, mixed,
    )

    big, everywhere, input_grad, layer_output, *halves = run_tail(
        stack, small, keep, sent, layer_input, mid_grad, first_scale, own(attn_norm)[None, :], mid,
        returned.reshape(groups * HALF, width), select_gated, pieces,
    )
    kept, others = halves[:3], halves[3:]
    expert_grads = []
    for mine, other in zip(kept, others):
        other = other.astype(F32)
        expert_grads.append(
            jnp.stack([jnp.where(first_side, mine, other), jnp.where(first_side, other, mine)])
        )
    small = lax.dynamic_index_in_dim(everywhere, rank_t, 0, keepdims=False)
    everywhere = everywhere.astype(F32)
    rows_w = w_query.shape[0]
    rows_o = w_output.shape[0]
    summed = [big[width + i * rows_w : width + (i + 1) * rows_w].astype(F32) for i in range(3)]
    output_grad = jnp.concatenate(
        [big[i * rows_o : (i + 1) * rows_o] for i in range(4)], axis=1
    ).astype(F32)
    return (
        layer_output,
        input_grad,
        everywhere[:, experts].reshape(width),
        summed[0],
        summed[1],
        summed[2],
        small[experts + 2].astype(F32),
        small[experts + 3].astype(F32),
        output_grad,
        everywhere[:, experts + 1].reshape(width),
        everywhere[:, :experts]
        .reshape(4, 2, groups, quarter)
        .transpose(0, 3, 2, 1)
        .reshape(width, experts),
        expert_grads[0],
        expert_grads[1],
        expert_grads[2],
    )


def solution(mesh):
    placed = (
        P("dp", "tensor"),
        P(),
        P(None, "tensor"),
        P(None, "tensor"),
        P(None, "tensor"),
        P("tensor"),
        P("tensor"),
        P("tensor", None),
        P(),
        P(),
        P("dp", None, "tensor"),
        P("dp", None, "tensor"),
        P("dp", "tensor", None),
        P("dp", None),
        P("dp", None),
        P("dp", None),
        P("dp", "tensor"),
    )
    return jax.shard_map(
        per_device,
        mesh=mesh,
        in_specs=placed,
        out_specs=(
            P("dp", "tensor"),
            P("dp", "tensor"),
            P(),
            P(None, "tensor"),
            P(None, "tensor"),
            P(None, "tensor"),
            P("tensor"),
            P("tensor"),
            P("tensor", None),
            P(),
            P(),
            P("dp", None, "tensor"),
            P("dp", None, "tensor"),
            P("dp", "tensor", None),
        ),
        check_vma=False,
    )
```

```python
import math

import jax
import jax.numpy as jnp
from jax import lax
from jax.experimental import pallas as pl
from jax.experimental.pallas import tpu as pltpu
from jax.sharding import PartitionSpec as P

HDIM = 128
TOP = 8
SLOTS = 64
HALF = SLOTS // 2
EPS = 1e-06
HIGH = lax.Precision.HIGHEST
F32 = jnp.float32
BF16 = jnp.bfloat16
MESH = pl.DeviceIdType.MESH
SMALL = 80
LANES = 128
LATE = 8


def dot(a, b, dims, **kw):
    return lax.dot_general(a, b, (dims, ((), ())), preferred_element_type=F32, **kw)


def nn(a, b):
    return dot(a, b, ((1,), (0,)))


def nt(a, b):
    return dot(a, b, ((1,), (1,)))


def tn(a, b):
    return dot(a, b, ((0,), (0,)))


def two_parts(column):
    high = column.astype(BF16)
    rest = (column - high.astype(F32)).astype(BF16)
    lane = lax.broadcasted_iota(jnp.int32, (column.shape[0], LANES), 1)
    return jnp.where(
        lane == 0, high.astype(F32), jnp.where(lane == 1, rest.astype(F32), 0.0)
    ).astype(BF16)


def one_column(pair):
    wide = pair.astype(F32)
    return wide[:, 0:1] + wide[:, 1:2]


def expert_body(
    rows_in, rows_late, og_in, wg_all, wu_all, wd_all,
    out_ref, back_in, kept_g, kept_u, kept_d, got_g, got_u, got_d,
    rows_s, og_s, wgu_s, wd_s, back_s, gu_s, hid_s, keep_s, move_s, down_keep, down_move,
    rs_sem, og_sem, w_sem, bs, br, ls, ks, ms, mr, late_s, late_r,
):
    plane = Plane()
    swap = (plane.dp, lax.axis_index("tensor") + 1 - 2 * plane.core)
    groups, slots, more = rows_s.shape
    width = og_s.shape[2]
    hidden = hid_s.shape[1]
    span = hidden // 4
    per = groups // 4
    tile = per * slots

    late = rows_late.shape[0]
    early = groups - late

    def load(e, _):
        g = plane.source(e)

        @pl.when(e < early)
        def _():
            pltpu.make_async_copy(rows_in.at[g], rows_s.at[e], rs_sem.at[e // per]).start()

        pltpu.make_async_copy(og_in.at[g], og_s.at[e], og_sem.at[e // per]).start()
        return 0

    lax.fori_loop(0, per, load, 0)
    w_copies = []
    for i in range(4):
        at = slice(i * span, (i + 1) * span)
        high = slice(hidden + i * span, hidden + (i + 1) * span)
        w_copies.append(pltpu.make_async_copy(wg_all.at[i], wgu_s.at[:, at], w_sem.at[0, i]))
        w_copies.append(pltpu.make_async_copy(wu_all.at[i], wgu_s.at[:, high], w_sem.at[1, i]))
    for i in range(4):
        at = slice(i * span, (i + 1) * span)
        w_copies.append(pltpu.make_async_copy(wd_all.at[i], wd_s.at[at], w_sem.at[2, i]))
    for c in w_copies:
        c.start()
    lax.fori_loop(per, groups, load, 0)

    barrier = pltpu.get_barrier_semaphore()

    plane.greet(barrier)
    pl.semaphore_signal(barrier, inc=1, device_id=swap, device_id_type=MESH)
    pl.semaphore_wait(barrier, groups)

    def late_copy(i):
        return pltpu.make_async_remote_copy(
            src_ref=rows_late.at[i],
            dst_ref=rows_s.at[early + i],
            send_sem=late_s.at[i],
            recv_sem=late_r.at[i],
            device_id=plane.device(plane.entry(early + i)),
            device_id_type=MESH,
        )

    def late_start(i, _):
        late_copy(i).start()
        return 0

    lax.fori_loop(0, late - 1, late_start, 0)
    own_rows = pltpu.make_async_copy(rows_late.at[late - 1], rows_s.at[groups - 1], ls.at[3])
    own_rows.start()

    def back_copy(e):
        g = plane.source(e)
        return pltpu.make_async_remote_copy(
            src_ref=back_s.at[e],
            dst_ref=back_in.at[plane.dp],
            send_sem=bs.at[e],
            recv_sem=br.at[e],
            device_id=plane.device(g),
            device_id_type=MESH,
        )

    own_back = pltpu.make_async_copy(back_s.at[groups - 1], back_in.at[plane.dp], ls.at[0])

    def one_tile(k, _):
        first = pl.multiple_of(k * per, per)
        here = pl.ds(pl.multiple_of(k * tile, tile), tile)
        part = pl.ds(first, per)

        @pl.when(k < early // per)
        def _():
            pltpu.make_async_copy(rows_in.at[pl.ds(0, per)], rows_s.at[part], rs_sem.at[k]).wait()

        @pl.when(k >= early // per)
        def _():
            def arrive(j, _):
                i = first + j - early

                @pl.when(i < late - 1)
                def _():
                    late_copy(i).wait()

                @pl.when(i == late - 1)
                def _():
                    own_rows.wait()

                return 0

            lax.fori_loop(0, per, arrive, 0)

        @pl.when(k == 0)
        def _():
            for c in w_copies[:8]:
                c.wait()

        mine = rows_s[part].reshape(tile, more)
        rows = mine[:, :width]
        gate = one_column(mine[:, width:])
        both = nn(rows, wgu_s[...])
        gp = both[:, :hidden]
        up = both[:, hidden:]
        sig = jax.nn.sigmoid(gp)
        act = gp * sig
        hid = act * up
        hid_s[here, :] = (gate * hid).astype(BF16)

        @pl.when(k == 0)
        def _():
            for c in w_copies[8:]:
                c.wait()

        low = nn(hid.astype(BF16), wd_s[...]).astype(BF16)
        out_ref[part] = low.reshape(per, slots, width)
        pltpu.make_async_copy(og_in.at[pl.ds(0, per)], og_s.at[part], og_sem.at[k]).wait()
        grads = og_s[part].reshape(tile, width)
        slot = jnp.sum(grads.astype(F32) * low.astype(F32), axis=1, keepdims=True)
        back_s[part, :, width:] = two_parts(slot).reshape(per, slots, more - width)
        hidden_grad = gate * nt(grads, wd_s[...])
        gu_s[here, :hidden] = (hidden_grad * up * sig * (1.0 + gp * (1.0 - sig))).astype(BF16)
        gu_s[here, hidden:] = (hidden_grad * act).astype(BF16)
        back = nt(gu_s[here, :], wgu_s[...]).astype(BF16)
        back_s[part, :, :width] = back.reshape(per, slots, width)

        def send(j, _):
            e = first + j

            @pl.when(e < groups - 1)
            def _():
                back_copy(e).start()

            @pl.when(e == groups - 1)
            def _():
                own_back.start()

            return 0

        lax.fori_loop(0, per, send, 0)
        return 0

    lax.fori_loop(0, 4, one_tile, 0)

    half = hidden // 2
    wide_block = keep_s.shape[1]

    def column_copies(i, slot):
        at = pl.ds(pl.multiple_of(i * wide_block, wide_block), wide_block)
        local = [
            pltpu.make_async_copy(keep_s.at[slot, :, :half], kept_g.at[at], ks.at[slot, 0]),
            pltpu.make_async_copy(keep_s.at[slot, :, half:], kept_u.at[at], ks.at[slot, 1]),
        ]
        far = [
            pltpu.make_async_remote_copy(
                src_ref=move_s.at[slot, :, side],
                dst_ref=target.at[at],
                send_sem=ms.at[slot, n],
                recv_sem=mr.at[i, n],
                device_id=swap,
                device_id_type=MESH,
            )
            for n, (side, target) in enumerate(
                ((slice(0, half), got_g), (slice(half, hidden), got_u))
            )
        ]
        return local + far

    def columns(i, _):
        slot = lax.rem(i, 2)

        @pl.when(i >= 2)
        def _():
            for c in column_copies(i - 2, slot):
                c.wait()

        at = pl.ds(pl.multiple_of(i * wide_block, wide_block), wide_block)
        rows = rows_s[:, :, at].reshape(groups * slots, wide_block)
        grad = tn(rows, gu_s[...])
        keep_s[slot, :, :half] = grad[:, :half]
        keep_s[slot, :, half:] = grad[:, hidden : hidden + half]
        move_s[slot, :, :half] = grad[:, half:hidden].astype(BF16)
        move_s[slot, :, half:] = grad[:, hidden + half :].astype(BF16)
        for c in column_copies(i, slot):
            c.start()
        return 0

    steps = width // wide_block
    lax.fori_loop(0, steps, columns, 0)
    downs = []
    for i in range(4):
        at = slice(i * span, (i + 1) * span)
        grad = tn(hid_s[:, at], og_s[...].reshape(groups * slots, width))
        if i < 2:
            down_keep[at] = grad
            downs.append(pltpu.make_async_copy(down_keep.at[at], kept_d.at[at], ls.at[1 + i]))
        else:
            at = slice((i - 2) * span, (i - 1) * span)
            down_move[at] = grad.astype(BF16)
            downs.append(
                pltpu.make_async_remote_copy(
                    src_ref=down_move.at[at],
                    dst_ref=got_d.at[at],
                    send_sem=ms.at[2, i - 2],
                    recv_sem=mr.at[steps, i - 2],
                    device_id=swap,
                    device_id_type=MESH,
                )
            )
        downs[-1].start()
    for i in (steps - 2, steps - 1):
        for c in column_copies(i, i % 2):
            c.wait()
    for c in downs:
        c.wait()

    def finish(e, _):
        back_copy(e).wait()
        return 0

    lax.fori_loop(0, groups - 1, finish, 0)
    own_back.wait()


def run_experts(rows, late, grads, weights):
    groups, slots, more = rows.shape
    width = grads.shape[2]
    hidden = 4 * weights[0].shape[2]
    half = hidden // 2
    count = groups * slots
    block = 256
    whole = pl.BlockSpec(memory_space=pltpu.VMEM)
    free = pl.BlockSpec(memory_space=pl.ANY)
    f = jax.ShapeDtypeStruct
    vm = pltpu.VMEM
    dma = pltpu.SemaphoreType.DMA
    return pl.pallas_call(
        expert_body,
        in_specs=[free] * 6,
        out_specs=[whole] + [free] * 7,
        out_shape=[
            f((groups, slots, width), BF16),
            f((groups, slots, more), BF16),
            f((width, half), F32),
            f((width, half), F32),
            f((half, width), F32),
            f((width, half), BF16),
            f((width, half), BF16),
            f((half, width), BF16),
        ],
        scratch_shapes=[
            vm((groups, slots, more), BF16),
            vm((groups, slots, width), BF16),
            vm((width, 2 * hidden), BF16),
            vm((hidden, width), BF16),
            vm((groups, slots, more), BF16),
            vm((count, 2 * hidden), BF16),
            vm((count, hidden), BF16),
            vm((2, block, hidden), F32),
            vm((2, block, hidden), BF16),
            vm((half, width), F32),
            vm((half, width), BF16),
            dma((4,)),
            dma((4,)),
            dma((3, 4)),
            dma((31,)),
            dma((31,)),
            dma((4,)),
            dma((2, 2)),
            dma((3, 2)),
            dma((width // block + 1, 2)),
            dma((late.shape[0],)),
            dma((late.shape[0],)),
        ],
        compiler_params=pltpu.CompilerParams(
            collective_id=2, has_side_effects=True, vmem_limit_bytes=61 << 20
        ),
        name="experts",
    )(rows, late, grads, *weights)


def head_scale(pre):
    return lax.rsqrt(jnp.mean(pre * pre, axis=1, keepdims=True) + EPS)


def turn(value, cosine, sine):
    return value * cosine + pltpu.roll(value, HDIM // 2, 1) * sine


def softmax_rows(query, key, same):
    raw = nt(query, key) * HDIM ** (-0.5)
    raw = jnp.where(same, raw, -1e30)
    powered = jnp.exp(raw - jnp.max(raw, axis=1, keepdims=True))
    return powered / jnp.sum(powered, axis=1, keepdims=True)


class Near:
    def __init__(self, send_sems, recv_sems):
        self.dp = lax.axis_index("dp")
        self.t = lax.axis_index("tensor")
        self.core = lax.rem(self.t, 2)
        self.first_core = self.core == 0
        self.low_x = self.t < 2
        self.far = lax.rem(self.t + 2, 4)
        self.swap = (self.dp, self.t + 1 - 2 * self.core)
        self.cross = (self.dp, self.far)
        self.diag = (self.dp, self.far + 1 - 2 * self.core)
        self.sems = (send_sems, recv_sems)
        self.used = 0

    def send(self, source, target, device):
        k = self.used
        self.used = k + 1
        c = pltpu.make_async_remote_copy(
            src_ref=source,
            dst_ref=target,
            send_sem=self.sems[0].at[k],
            recv_sem=self.sems[1].at[k],
            device_id=device,
            device_id_type=MESH,
        )
        c.start()
        return c

    def gather_start(self, buf):
        here = buf.at[self.t]
        return [self.send(here, here, self.cross), self.send(here, here, self.swap)]

    def gather_relay(self, buf, copies):
        copies[0].wait()
        there = buf.at[self.far]
        copies.append(self.send(there, there, self.swap))

    def split(self, part, low_s, high_s, sent):
        quarter = part.shape[1] // 4
        p = [part[:, i * quarter : (i + 1) * quarter] for i in range(4)]
        low_s[...] = jnp.where(self.first_core, p[0], p[1])
        high_s[...] = jnp.where(self.first_core, p[2], p[3])
        sent[:, :quarter] = jnp.where(self.first_core, p[1], p[0]).astype(BF16)
        sent[:, quarter:] = jnp.where(self.first_core, p[3], p[2]).astype(BF16)

    def sum_parts(self, low_s, high_s, sent, got, go, back):
        quarter = go.shape[1]
        self.send(sent, got, self.swap).wait()
        low = low_s[...] + got[:, :quarter].astype(F32)
        high = high_s[...] + got[:, quarter:].astype(F32)
        go[...] = jnp.where(self.low_x, high, low).astype(BF16)
        self.send(go, back, self.cross).wait()
        return jnp.where(self.low_x, low, high) + back[...].astype(F32)


class Plane:
    def __init__(self):
        self.dp = lax.axis_index("dp")
        t = lax.axis_index("tensor")
        self.y = lax.rem(self.dp, 4)
        self.xh = lax.rem(self.dp // 4, 2)
        self.z = self.dp // 8
        self.core = lax.rem(t, 2)
        self.side = lax.rem(t // 2 + self.xh, 2)

    def at(self, dz, dx, dy):
        return (lax.rem(self.z + dz, 4) * 2 + lax.rem(self.xh + dx, 2)) * 4 + lax.rem(
            self.y + dy, 4
        )

    def device(self, group):
        return (group, lax.rem(self.side + lax.rem(group // 4, 2), 2) * 2 + self.core)

    def offset(self, e):
        dz = 3 - lax.rem(e, 4)
        dx = 1 - lax.rem(e // 4, 2)
        dy = lax.rem(e // 8 + 1 + dz, 4)
        return dz, dx, dy

    def entry(self, e):
        return self.at(*self.offset(e))

    def source(self, e):
        dz, dx, dy = self.offset(e)
        return self.at(4 - dz, 2 - dx, 4 - dy)

    def greet(self, barrier):
        def one(e, _):
            pl.semaphore_signal(
                barrier, inc=1, device_id=self.device(self.entry(e)), device_id_type=MESH
            )
            return 0

        lax.fori_loop(0, 31, one, 0)

    def exchange(self, source, target, send_sems, recv_sems, local_sem, back, count=32):
        def copy(e):
            group = self.source(e) if back else self.entry(e)
            return pltpu.make_async_remote_copy(
                src_ref=source.at[e if back else group],
                dst_ref=target.at[self.dp],
                send_sem=send_sems.at[e],
                recv_sem=recv_sems.at[e],
                device_id=self.device(group),
                device_id_type=MESH,
            )

        def start(e, _):
            copy(e).start()
            return 0

        def finish(e, _):
            copy(e).wait()
            return 0

        lax.fori_loop(0, min(count, 31), start, 0)
        if count == 32:
            own = pltpu.make_async_copy(
                source.at[31 if back else self.dp], target.at[self.dp], local_sem
            )
            own.start()

        def wait():
            lax.fori_loop(0, min(count, 31), finish, 0)
            if count == 32:
                own.wait()

        return wait


def wide(buf):
    return jnp.concatenate([buf[i] for i in range(4)], axis=1)


def as_column(row):
    return jnp.broadcast_to(row.astype(F32), (LANES, row.shape[1])).T[:, :1]


def by_side(experts):
    half = experts // 2
    r = lax.broadcasted_iota(jnp.int32, (experts, experts), 0)
    e = lax.broadcasted_iota(jnp.int32, (experts, experts), 1)
    return jnp.where(e == 2 * lax.rem(r, half) + r // half, 1.0, 0.0)


def front_body(
    x_ref, og_ref, gain1_ref, gain2_ref, wq_ref, wk_ref, wv_ref, wo_ref, qn_ref, kn_ref, places_ref,
    row_ref, routes_ref, router_ref, wg_ref, wu_ref, wd_ref,
    cos_ref, sin_ref, normed_ref, fs_ref, qpre_ref, kpre_ref, q_ref, k_ref, v_ref, mixed_ref, mid_ref, mids_ref, ogs_ref,
    nm_ref, gates_ref, place_ref, rows_in, rows_late, og_in, wg_all, wu_all, wd_all,
    xs, low_s, high_s, sent, got, go, back, og_out, rows_out,
    ts, tr, as_, ar, bs, br, ls, late_sem,
):
    near = Near(ts, tr)
    plane = Plane()
    side = plane.side
    barrier = pltpu.get_barrier_semaphore()
    plane.greet(barrier)
    pl.semaphore_signal(barrier, inc=1, device_id=near.swap, device_id_type=MESH)
    pl.semaphore_signal(barrier, inc=1, device_id=near.cross, device_id_type=MESH)
    pl.semaphore_wait(barrier, 33)
    t = near.t
    length = x_ref.shape[0]
    quarter = x_ref.shape[1]
    width = 4 * quarter

    ogs_ref[t] = og_ref[...].astype(BF16)
    og_copies = near.gather_start(ogs_ref)
    xs[t] = x_ref[...].astype(BF16)
    x_copies = near.gather_start(xs)
    weights = ((wg_ref, wg_all), (wu_ref, wu_all), (wd_ref, wd_all))
    kept = [
        pltpu.make_async_copy(w.at[side], w_all.at[0], ls.at[2 + i])
        for i, (w, w_all) in enumerate(weights)
    ]
    w_cross = [near.send(wg_ref.at[1 - side], wg_all.at[1], near.cross)]

    experts_all = router_ref.shape[1]
    number = lax.broadcasted_iota(jnp.int32, (experts_all, length), 0)
    number = 2 * lax.rem(number, experts_all // 2) + number // (experts_all // 2)
    chosen = routes_ref[0:1, :] == number
    for k in range(1, TOP):
        chosen = jnp.logical_or(chosen, routes_ref[k : k + 1, :] == number)
    mask = jnp.where(chosen, 1.0, 0.0)
    earlier = lax.broadcasted_iota(jnp.int32, (length, length), 0) < lax.broadcasted_iota(
        jnp.int32, (length, length), 1
    )
    rank = nn(mask.astype(BF16), jnp.where(earlier, 1.0, 0.0).astype(BF16))
    rank = jnp.where(chosen, rank, -1.0).astype(jnp.int32)
    experts = rank.shape[0] // 2
    place_ref[...] = jnp.where(side == 0, rank[:experts], rank[experts:])
    base = near.core * HALF

    def hits(i):
        place = place_ref[i * 8 : (i + 1) * 8, :]
        spots = lax.broadcasted_iota(jnp.int32, (8, HALF, length), 1) + base
        return jnp.broadcast_to(place[:, None, :], (8, HALF, length)) == spots

    near.gather_relay(ogs_ref, og_copies)
    near.gather_relay(xs, x_copies)
    for c in og_copies[1:]:
        c.wait()
    og = wide(ogs_ref)
    for i in range(experts // 8):
        select = jnp.where(hits(i), 1.0, 0.0).reshape(8 * HALF, length).astype(BF16)
        og_out[i * 8 : (i + 1) * 8] = nn(select, og).astype(BF16).reshape(8, HALF, width)
    og_wait = plane.exchange(og_out, og_in, as_, ar, ls.at[0], False)
    for c in kept:
        c.start()
    w_swap = [near.send(w.at[side], w_all.at[2], near.swap) for w, w_all in weights]

    for c in x_copies[1:]:
        c.wait()
    x = wide(xs).astype(F32)
    scale = lax.rsqrt(jnp.mean(x * x, axis=1, keepdims=True) + EPS)
    fs_ref[...] = scale
    normed = (x * scale * gain1_ref[...]).astype(BF16)
    normed_ref[...] = normed
    qpre = nn(normed, wq_ref[...])
    kpre = nn(normed, wk_ref[...])
    qpre_ref[...] = qpre
    kpre_ref[...] = kpre
    v_ref[...] = nn(normed, wv_ref[...]).astype(BF16)
    lane = lax.broadcasted_iota(jnp.int32, (1, HDIM), 1)
    half = HDIM // 2
    step = lax.rem(lane, half).astype(F32) * (-2.0 * math.log(10000.0) / HDIM)
    angle = as_column(places_ref[...]) * jnp.exp(step)
    cosine = jnp.cos(angle)
    sine = jnp.sin(angle) * jnp.where(lane < half, -1.0, 1.0)
    cos_ref[...] = cosine
    sin_ref[...] = sine
    same = as_column(row_ref[...]) == row_ref[...].astype(F32)
    for h in range(q_ref.shape[1] // HDIM):
        at = slice(h * HDIM, (h + 1) * HDIM)
        qh = qpre[:, at]
        kh = kpre[:, at]
        query = turn(qh * head_scale(qh) * qn_ref[:, at], cosine, sine).astype(BF16)
        key = turn(kh * head_scale(kh) * kn_ref[:, at], cosine, sine).astype(BF16)
        q_ref[:, at] = query
        k_ref[:, at] = key
        probs = softmax_rows(query, key, same).astype(BF16)
        mixed_ref[:, at] = nn(probs, v_ref[:, at]).astype(BF16)
    near.split(nn(mixed_ref[...], wo_ref[...]), low_s, high_s, sent)
    mid = x_ref[...] + near.sum_parts(low_s, high_s, sent, got, go, back)
    mid_ref[...] = mid
    mids_ref[t] = mid.astype(BF16)
    mid_copies = near.gather_start(mids_ref)
    w_cross.append(near.send(wu_ref.at[1 - side], wu_all.at[1], near.cross))
    w_cross.append(near.send(wd_ref.at[1 - side], wd_all.at[1], near.cross))
    near.gather_relay(mids_ref, mid_copies)
    for c in mid_copies[1:]:
        c.wait()
    mid = wide(mids_ref).astype(F32)
    scale = lax.rsqrt(jnp.mean(mid * mid, axis=1, keepdims=True) + EPS)
    normed = (mid * scale * gain2_ref[...]).astype(BF16)
    nm_ref[...] = normed

    logits = dot(
        by_side(experts_all), nn(normed, router_ref[...]), ((1,), (1,)), precision=HIGH
    )
    masked = jnp.where(chosen, logits, -1e30)
    raised = jnp.where(chosen, jnp.exp(masked - jnp.max(masked, axis=0, keepdims=True)), 0.0)
    gates = raised / jnp.sum(raised, axis=0, keepdims=True)
    gates_ref[...] = gates
    gates_side = jnp.where(side == 0, gates[:experts], gates[experts:])
    for i in range(experts // 8):
        hit = hits(i)
        select = jnp.where(hit, 1.0, 0.0).reshape(8 * HALF, length).astype(BF16)
        rows_out[i * 8 : (i + 1) * 8, :, :width] = (
            nn(select, normed).astype(BF16).reshape(8, HALF, width)
        )
        gate = jnp.broadcast_to(gates_side[i * 8 : (i + 1) * 8][:, None, :], (8, HALF, length))
        column = jnp.sum(
            jnp.where(hit, gate, 0.0).reshape(8 * HALF, length), axis=1, keepdims=True
        )
        rows_out[i * 8 : (i + 1) * 8, :, width:] = two_parts(column).reshape(8, HALF, LANES)
    early = 32 - rows_late.shape[0]
    rows_wait = plane.exchange(rows_out, rows_in, bs, br, ls.at[1], False, early)

    def late_copy(i):
        return pltpu.make_async_copy(
            rows_out.at[plane.entry(early + i)], rows_late.at[i], late_sem.at[i]
        )

    def late_start(i, _):
        late_copy(i).start()
        return 0

    def late_wait(i, _):
        late_copy(i).wait()
        return 0

    lax.fori_loop(0, 32 - early, late_start, 0)
    for c, (w, w_all) in zip(w_cross, weights):
        c.wait()
        w_swap.append(near.send(w_all.at[1], w_all.at[3], near.swap))
    og_wait()
    rows_wait()
    lax.fori_loop(0, 32 - early, late_wait, 0)
    for c in w_swap + kept:
        c.wait()


def run_front(
    x, og, gain1, gain2, wq, wk, wv, wo, qn, kn, places, labels, routes, router, wg, wu, wd, groups
):
    length, quarter = x.shape
    width = 4 * quarter
    inner = wq.shape[1]
    whole = pl.BlockSpec(memory_space=pltpu.VMEM)
    free = pl.BlockSpec(memory_space=pl.ANY)
    f = jax.ShapeDtypeStruct
    vm = pltpu.VMEM
    dma = pltpu.SemaphoreType.DMA
    return pl.pallas_call(
        front_body,
        in_specs=[whole] * 14 + [free] * 3,
        out_specs=[whole] * 16 + [free] * 6,
        out_shape=[
            f((length, HDIM), F32),
            f((length, HDIM), F32),
            f((length, width), BF16),
            f((length, 1), F32),
            f((length, inner), F32),
            f((length, inner), F32),
            f((length, inner), BF16),
            f((length, inner), BF16),
            f((length, inner), BF16),
            f((length, inner), BF16),
            f((length, quarter), F32),
            f((4, length, quarter), BF16),
            f((4, length, quarter), BF16),
            f((length, width), BF16),
            f((2 * groups, length), F32),
            f((groups, length), jnp.int32),
            f((groups, HALF, width + LANES), BF16),
            f((LATE, HALF, width + LANES), BF16),
            f((groups, HALF, width), BF16),
            f((4,) + wg.shape[1:], BF16),
            f((4,) + wu.shape[1:], BF16),
            f((4,) + wd.shape[1:], BF16),
        ],
        scratch_shapes=[
            vm((4, length, quarter), BF16),
            vm((length, quarter), F32),
            vm((length, quarter), F32),
            vm((length, 2 * quarter), BF16),
            vm((length, 2 * quarter), BF16),
            vm((length, quarter), BF16),
            vm((length, quarter), BF16),
            vm((groups, HALF, width), BF16),
            vm((groups, HALF, width + LANES), BF16),
            dma((20,)),
            dma((20,)),
            dma((31,)),
            dma((31,)),
            dma((31,)),
            dma((31,)),
            dma((5,)),
            dma((LATE,)),
        ],
        compiler_params=pltpu.CompilerParams(
            collective_id=1, has_side_effects=True, vmem_limit_bytes=60 << 20
        ),
        name="front",
    )(
        x, og, gain1, gain2, wq, wk, wv, wo, qn, kn, places, labels, routes, router, wg, wu, wd
    )


def middle_body(
    rows_ref, out_rows, place_ref, gates_ref, nm_ref, router_ref, mid_ref, og_ref, mids_ref, ogs_ref,
    gain_ref, normed_in, wq_in, wk_in, wv_in, wo_in, qn_ref, kn_ref, cos_ref, sin_ref,
    row_ref, qpre_ref, kpre_ref, q_ref, k_ref, v_ref, mixed_ref,
    stack_ref, small_ref, mid_grad_ref, keep_ref, sent_ref, returned,
    low_s, low_f, high_f, sent, got, go, back, ngs, gg_s, probs_s, normed_ref, wq_ref, wk_ref, wv_ref,
    wo_ref, ts, tr, os, orr, ls,
):
    near = Near(ts, tr)
    plane = Plane()
    loads = [
        pltpu.make_async_copy(source, target, ls.at[1 + i])
        for i, (source, target) in enumerate(
            (
                (wo_in, wo_ref),
                (wq_in, wq_ref),
                (wk_in, wk_ref),
                (wv_in, wv_ref),
                (normed_in, normed_ref),
            )
        )
    ]
    for c in loads:
        c.start()
    side = plane.side
    t = near.t
    groups, slots, more = rows_ref.shape
    length, width = normed_ref.shape
    quarter = width // 4
    inner = q_ref.shape[1]

    barrier = pltpu.get_barrier_semaphore()

    plane.greet(barrier)
    pl.semaphore_signal(barrier, inc=1, device_id=near.swap, device_id_type=MESH)
    pl.semaphore_signal(barrier, inc=1, device_id=near.cross, device_id_type=MESH)
    pl.semaphore_wait(barrier, groups + 1)

    out_wait = plane.exchange(out_rows, returned, os, orr, ls.at[0], True)

    base = near.core * slots
    part = None
    for i in range(groups // 8):
        at = slice(i * 8, (i + 1) * 8)
        spots = lax.broadcasted_iota(jnp.int32, (8, slots, length), 1) + base
        hit = jnp.broadcast_to(place_ref[at, :][:, None, :], (8, slots, length)) == spots
        select = jnp.where(hit, 1.0, 0.0).reshape(8 * slots, length)
        tile = rows_ref[at].reshape(8 * slots, more)
        column = one_column(tile[:, width:])
        gg_s[0, at] = jnp.sum((select * column).reshape(8, slots, length), axis=1)
        term = tn(select.astype(BF16), tile[:, :width])
        part = term if part is None else part + term
    gate_swap = near.send(gg_s.at[0], gg_s.at[1], near.swap)
    near.split(part, low_f, high_f, sent)
    swapped = near.send(sent, got, near.swap)
    gate_swap.wait()
    gg_s[2] = gg_s[0] + gg_s[1]
    gate_cross = near.send(gg_s.at[2], gg_s.at[3], near.cross)
    swapped.wait()
    low = low_f[...] + got[:, :quarter].astype(F32)
    high = high_f[...] + got[:, quarter:].astype(F32)
    go[...] = jnp.where(near.low_x, high, low).astype(BF16)
    crossed = near.send(go, back, near.cross)
    gate_cross.wait()
    own, other = gg_s[2], gg_s[3]
    gate_grad = jnp.concatenate(
        [jnp.where(side == 0, own, other), jnp.where(side == 0, other, own)], axis=0
    )
    gates = gates_ref[...]
    logit_grad = gates * (gate_grad - jnp.sum(gates * gate_grad, axis=0, keepdims=True))
    mine = pl.ds(pl.multiple_of(t * quarter, quarter), quarter)
    experts = gates.shape[0]
    router = dot(
        by_side(experts), router_ref[mine, :].astype(F32), ((1,), (1,)), precision=HIGH
    )
    router_back = dot(logit_grad, router, ((0,), (0,)), precision=HIGH)
    small_ref[:experts, :] = dot(
        logit_grad, nm_ref[:, mine].astype(F32), ((1,), (0,)), precision=HIGH
    ).astype(BF16)
    mid = wide(mids_ref).astype(F32)
    scale = lax.rsqrt(jnp.mean(mid * mid, axis=1, keepdims=True) + EPS)
    mid_own = mid_ref[...]
    same = as_column(row_ref[...]) == row_ref[...].astype(F32)
    heads = inner // HDIM

    def attention_probs(h):
        at = slice(h * HDIM, (h + 1) * HDIM)
        probs_s[h] = softmax_rows(q_ref[:, at], k_ref[:, at], same)

    for h in range(heads // 2):
        attention_probs(h)
    crossed.wait()
    ng = jnp.where(near.low_x, low, high) + back[...].astype(F32) + router_back
    ngs[t] = ng.astype(BF16)
    ng_copies = near.gather_start(ngs)
    moe = jnp.sum(ng * mid_own * scale, axis=0, keepdims=True)
    for h in range(heads // 2, heads):
        attention_probs(h)
    near.gather_relay(ngs, ng_copies)
    for c in ng_copies[1:]:
        c.wait()

    weighted = wide(ngs).astype(F32) * gain_ref[...]
    shrink = scale * scale * scale * jnp.mean(weighted * mid, axis=1, keepdims=True)
    mid_grad_ref[...] = og_ref[...] + scale * (ng * gain_ref[:, mine]) - mid_own * shrink
    attn_grad = (wide(ogs_ref).astype(F32) + scale * weighted - mid * shrink).astype(BF16)

    for c in loads:
        c.wait()
    wo_grad = tn(mixed_ref[...], attn_grad).astype(BF16)
    for i in range(4):
        stack_ref[i * inner : (i + 1) * inner, :] = wo_grad[:, i * quarter : (i + 1) * quarter]
    mixed_grad = nt(attn_grad, wo_ref[...]).astype(BF16)
    cosine = cos_ref[...]
    sine = sin_ref[...]
    factor = HDIM ** (-0.5)

    def norm_back(pre, gain, rotated):
        grad = rotated * cosine - pltpu.roll(rotated, HDIM // 2, 1) * sine
        head = head_scale(pre)
        weighted = grad * gain
        mean = jnp.mean(weighted * pre, axis=1, keepdims=True)
        low = (head * weighted - pre * (head * head * head * mean)).astype(BF16)
        return low, jnp.sum(grad * pre * head, axis=0, keepdims=True)

    q_sums, k_sums = [], []
    for h in range(inner // HDIM):
        at = slice(h * HDIM, (h + 1) * HDIM)
        query = q_ref[:, at]
        key = k_ref[:, at]
        mg = mixed_grad[:, at]
        probs = probs_s[h]
        low_s[:, 2 * inner + h * HDIM : 2 * inner + (h + 1) * HDIM] = tn(
            probs.astype(BF16), mg
        ).astype(BF16)
        prob_grad = nt(mg, v_ref[:, at])
        weighted_p = probs * prob_grad
        score = (weighted_p - probs * jnp.sum(weighted_p, axis=1, keepdims=True)).astype(BF16)
        low_q, total = norm_back(qpre_ref[:, at], qn_ref[:, at], nn(score, key) * factor)
        low_s[:, h * HDIM : (h + 1) * HDIM] = low_q
        q_sums.append(total)
        low_k, total = norm_back(kpre_ref[:, at], kn_ref[:, at], tn(score, query) * factor)
        low_s[:, inner + h * HDIM : inner + (h + 1) * HDIM] = low_k
        k_sums.append(total)
    row = lax.broadcasted_iota(jnp.int32, (small_ref.shape[0] - experts, quarter), 0)
    rest = jnp.zeros(row.shape, F32)
    for i, value in enumerate(
        (moe, jnp.concatenate(q_sums, axis=1), jnp.concatenate(k_sums, axis=1))
    ):
        rest = jnp.where(row == i + 1, jnp.broadcast_to(value, row.shape), rest)
    small_ref[experts:, :] = rest.astype(BF16)
    part = None
    for i, w in enumerate((wq_ref, wk_ref, wv_ref)):
        term = nt(low_s[:, i * inner : (i + 1) * inner], w[...])
        part = term if part is None else part + term
    near.split(part, low_f, high_f, sent_ref)
    keep_ref[:, :quarter] = low_f[...]
    keep_ref[:, quarter:] = high_f[...]
    normed = normed_ref[...]
    for i in range(3):
        stack_ref[(i + 1) * width : (i + 2) * width, :] = tn(
            normed, low_s[:, i * inner : (i + 1) * inner]
        ).astype(BF16)

    out_wait()


def run_middle(
    rows, out_rows, place, gates, nm, router, mid, og, mids, ogs, gain, normed, wq, wk, wv, wo, qn,
    kn, cosine, sine, labels, qpre, kpre, q, k, v, mixed,
):
    length, width = normed.shape
    quarter = width // 4
    groups = place.shape[0]
    inner = wq.shape[1]
    whole = pl.BlockSpec(memory_space=pltpu.VMEM)
    free = pl.BlockSpec(memory_space=pl.ANY)
    f = jax.ShapeDtypeStruct
    vm = pltpu.VMEM
    dma = pltpu.SemaphoreType.DMA
    return pl.pallas_call(
        middle_body,
        in_specs=[whole, free] + [whole] * 9 + [free] * 5 + [whole] * 11,
        out_specs=[whole] * 5 + [free],
        out_shape=[
            f((4 * width, quarter), BF16),
            f((SMALL, quarter), BF16),
            f((length, quarter), F32),
            f((length, 2 * quarter), F32),
            f((length, 2 * quarter), BF16),
            f(out_rows.shape, BF16),
        ],
        scratch_shapes=[
            vm((length, 3 * inner), BF16),
            vm((length, quarter), F32),
            vm((length, quarter), F32),
            vm((length, 2 * quarter), BF16),
            vm((length, 2 * quarter), BF16),
            vm((length, quarter), BF16),
            vm((length, quarter), BF16),
            vm((4, length, quarter), BF16),
            vm((4, groups, length), F32),
            vm((inner // HDIM, length, length), F32),
            vm(normed.shape, BF16),
            vm(wq.shape, BF16),
            vm(wk.shape, BF16),
            vm(wv.shape, BF16),
            vm(wo.shape, BF16),
            dma((8,)),
            dma((8,)),
            dma((31,)),
            dma((31,)),
            dma((6,)),
        ],
        compiler_params=pltpu.CompilerParams(
            collective_id=3, has_side_effects=True, vmem_limit_bytes=61 << 20
        ),
        name="middle",
    )(
        rows, out_rows, place, gates, nm, router, mid, og, mids, ogs, gain, normed, wq, wk, wv, wo,
        qn, kn, cosine, sine, labels, qpre, kpre, q, k, v, mixed,
    )


def tail_body(
    stack_ref, small_ref, keep_ref, sent_ref, x_ref, mid_grad_ref, fs_ref, gain_ref, mid_ref,
    ret_ref, place_ref, gates_ref, kept_g, kept_u, kept_d, got_g, got_u, got_d,
    out_ref, small_out_ref, input_ref, layer_ref, full_g, full_u, full_d,
    own_s, ret_s, recv1, buf1, recv2, buf2, recv3, small_in, got, out_sent, out_got, go, back, out_go, out_back,
    mean_in, kb, gb, nb, kd, gd, far_g, far_u, far_d, other_g, other_u,
    other_d, ss, rs, sss, srs, ts, tr, ws, ls,
):
    dp = lax.axis_index("dp")
    t = lax.axis_index("tensor")
    y = lax.rem(dp, 4)
    xh = lax.rem(dp // 4, 2)
    z = dp // 8
    core = lax.rem(t, 2)
    first_core = core == 0
    low_x = t < 2
    half = stack_ref.shape[0] // 2
    size = half // 2
    n1, n2, n3 = size // 4, size // 16, size // 32
    quarter = x_ref.shape[1]
    ret_load = pltpu.make_async_copy(ret_ref, ret_s, ls.at[4])
    ret_load.start()

    def at_z(k):
        return ((lax.rem(z + k, 4) * 2 + xh) * 4 + y, t)

    def at_y(k):
        return ((z * 2 + xh) * 4 + lax.rem(y + k, 4), t)

    at_x = ((z * 2 + 1 - xh) * 4 + y, t)
    at_swap = (dp, t + 1 - 2 * core)
    at_cross = (dp, lax.rem(t + 2, 4))
    at_diag = (dp, lax.rem(t + 2, 4) + 1 - 2 * core)

    barrier = pltpu.get_barrier_semaphore()
    for k in range(1, 4):
        pl.semaphore_signal(barrier, inc=1, device_id=at_z(k), device_id_type=MESH)
        pl.semaphore_signal(barrier, inc=1, device_id=at_y(k), device_id_type=MESH)
    for there in (at_x, at_swap, at_cross, at_diag):
        pl.semaphore_signal(barrier, inc=1, device_id=there, device_id_type=MESH)
    pl.semaphore_wait(barrier, 10)

    def send(source, target, sems, device):
        c = pltpu.make_async_remote_copy(
            src_ref=source,
            dst_ref=target,
            send_sem=sems[0],
            recv_sem=sems[1],
            device_id=device,
            device_id_type=MESH,
        )
        c.start()
        return c

    def copy(source, target, phase, h, k, device):
        return send(source, target, (ss.at[phase, h, k], rs.at[phase, h, k]), device)

    def small_copy(slot, k, device):
        return send(small_in.at[slot], small_in.at[slot], (sss.at[k], srs.at[k]), device)

    def near(source, target, k, device):
        return send(source, target, (ts.at[k], tr.at[k]), device)

    def rows_at(start, size):
        return pl.ds(pl.multiple_of(start, 64), size)

    ways = (((z, at_z), (y, at_y)), ((y, at_y), (z, at_z)))
    streams = [(ways[h], h * half + s * size) for s in range(2) for h in range(2)]
    first, second, third, ahead, later, ended, own_loads, bases = [], [], [], [], [], [], [], []
    for n, (((pos, at), _), start) in enumerate(streams):
        for k in range(1, 4):
            there = rows_at(start + lax.rem(pos + k, 4) * n1, n1)
            first.append(copy(stack_ref.at[there], recv1.at[n, k - 1], 0, n, k - 1, at(k)))
        bases.append(start + pos * n1)
    for n, base in enumerate(bases):
        own_loads.append(
            pltpu.make_async_copy(stack_ref.at[rows_at(base, n1)], own_s.at[n], ls.at[n])
        )
        own_loads[-1].start()

    swapped = near(sent_ref, got, 0, at_swap)
    side = lax.rem(t // 2 + xh, 2)
    groups, slots, width = ret_ref.shape
    length = x_ref.shape[0]
    gates = jnp.where(side == 0, gates_ref[:groups, :], gates_ref[groups:, :])
    ret_load.wait()
    part = None
    for i in range(groups // 8):
        at = slice(i * 8, (i + 1) * 8)
        spots = lax.broadcasted_iota(jnp.int32, (8, slots, length), 1) + core * slots
        hit = jnp.broadcast_to(place_ref[at, :][:, None, :], (8, slots, length)) == spots
        gate = jnp.broadcast_to(gates[at][:, None, :], (8, slots, length))
        select = jnp.where(hit, gate, 0.0).reshape(8 * slots, length).astype(BF16)
        term = tn(select, ret_s[at].reshape(8 * slots, width))
        part = term if part is None else part + term
    p = [part[:, i * quarter : (i + 1) * quarter] for i in range(4)]
    out_sent[:, :quarter] = jnp.where(first_core, p[1], p[0]).astype(BF16)
    out_sent[:, quarter:] = jnp.where(first_core, p[3], p[2]).astype(BF16)
    out_low = jnp.where(first_core, p[0], p[1])
    out_high = jnp.where(first_core, p[2], p[3])
    out_swapped = near(out_sent, out_got, 1, at_swap)
    swapped.wait()
    low_half = keep_ref[:, :quarter] + got[:, :quarter].astype(F32)
    high_half = keep_ref[:, quarter:] + got[:, quarter:].astype(F32)
    go[...] = jnp.where(low_x, high_half, low_half).astype(BF16)
    crossed = near(go, back, 2, at_cross)
    in_mine = jnp.where(low_x, low_half, high_half)
    out_swapped.wait()
    out_low = out_low + out_got[:, :quarter].astype(F32)
    out_high = out_high + out_got[:, quarter:].astype(F32)
    out_go[...] = jnp.where(low_x, out_high, out_low).astype(BF16)
    crossed.wait()
    in_grad = in_mine + back[...].astype(F32)
    x = x_ref[...]
    fs = fs_ref[...]
    weighted = in_grad * gain_ref[:, pl.ds(pl.multiple_of(t * quarter, quarter), quarter)]
    mean = jnp.sum(weighted * x, axis=1, keepdims=True)
    mean_in[0] = jnp.broadcast_to(mean, mean_in.shape[1:])
    mean_swap = near(mean_in.at[0], mean_in.at[1], 3, at_swap)
    row = lax.broadcasted_iota(jnp.int32, (16, quarter), 0)
    norm_row = jnp.sum(in_grad * x * fs, axis=0, keepdims=True)
    small_in[z] = small_ref[...]
    last = small_ref.shape[0] - 16
    small_in[z, last:, :] = jnp.where(
        row == 0, jnp.broadcast_to(norm_row, (16, quarter)), small_ref[last:, :].astype(F32)
    ).astype(BF16)
    small = [small_copy(z, k - 1, at_z(k)) for k in range(1, 4)]
    mean_swap.wait()
    mean_in[2] = mean_in[0] + mean_in[1]
    mean_cross = near(mean_in.at[2], mean_in.at[3], 4, at_cross)
    out_crossed = near(out_go, out_back, 5, at_cross)
    mean_cross.wait()
    mean = (mean_in[2] + mean_in[3])[:, 0:1] / (4 * quarter)
    input_ref[...] = mid_grad_ref[...] + fs * weighted - x * (fs * fs * fs * mean)
    out_crossed.wait()
    layer_ref[...] = mid_ref[...] + (jnp.where(low_x, out_low, out_high) + out_back[...].astype(F32))

    block = kb.shape[1]
    span = far_d.shape[0]

    def column_sums(kept, gotten, far, mine):
        loads, stores = [], []
        count = kept.shape[0] // block
        for i in range(count):
            at = slice(i * block, (i + 1) * block)
            loads.append(
                (
                    pltpu.make_async_copy(kept.at[at], kb.at[i % 2], ws.at[i % 2, 0]),
                    pltpu.make_async_copy(gotten.at[at], gb.at[i % 2], ws.at[i % 2, 1]),
                )
            )
        for c in loads[0]:
            c.start()
        for i in range(count):
            if i + 1 < count:
                for c in loads[i + 1]:
                    c.start()
            for c in loads[i]:
                c.wait()
            slot = i % 2
            at = slice(i * block, (i + 1) * block)
            total = kb[slot] + gb[slot].astype(F32)
            if i >= 2:
                stores[i - 2].wait()
            nb[slot] = total[:, :span]
            far[at, :] = total[:, span:].astype(BF16)
            stores.append(pltpu.make_async_copy(nb.at[slot], mine.at[side, at], ws.at[slot, 2]))
            stores[-1].start()
        for c in stores[-2:]:
            c.wait()

    def arrived(copy, other, full):
        copy.wait()
        stores = []
        for i in range(other.shape[0] // block):
            slot = i % 2
            at = slice(i * block, (i + 1) * block)
            if i >= 2:
                stores[i - 2].wait()
            nb[slot] = other[at, :].astype(F32)
            stores.append(pltpu.make_async_copy(nb.at[slot], full.at[1 - side, at], ws.at[slot, 2]))
            stores[-1].start()
        for c in stores[-2:]:
            c.wait()

    def row_sums():
        loads = [
            (
                pltpu.make_async_copy(kept_d.at[at], kd.at[i], ws.at[2 + i, 0]),
                pltpu.make_async_copy(got_d.at[at], gd.at[i], ws.at[2 + i, 1]),
            )
            for i, at in enumerate((slice(span, 2 * span), slice(0, span)))
        ]
        for pair in loads:
            for c in pair:
                c.start()
        for c in loads[0]:
            c.wait()
        far_d[...] = (kd[0] + gd[0].astype(F32)).astype(BF16)
        others.append(near(far_d, other_d, 8, at_cross))
        for c in loads[1]:
            c.wait()
        kd[1] = kd[1] + gd[1].astype(F32)
        store = pltpu.make_async_copy(kd.at[1], full_d.at[side], ws.at[2, 2])
        store.start()
        return store

    def small_total(start, count):
        total = small_in[start].astype(F32)
        for i in range(start + 1, start + count):
            total = total + small_in[i].astype(F32)
        return total.astype(BF16)

    def first_sum(n):
        for c in first[3 * n : 3 * n + 3]:
            c.wait()
        own_loads[n].wait()
        total = own_s[n].astype(F32)
        for k in range(3):
            total = total + recv1[n, k].astype(F32)
        buf1[n] = total.astype(BF16)
        _, (pos, at) = streams[n][0]
        for k in range(1, 4):
            there = rows_at(lax.rem(pos + k, 4) * n2, n2)
            second.append(copy(buf1.at[n, there], recv2.at[n, k - 1], 1, n, k - 1, at(k)))
        bases[n] = bases[n] + pos * n2

    def second_sum(n):
        for c in second[3 * n : 3 * n + 3]:
            c.wait()
        _, (pos, _) = streams[n][0]
        total = buf1[n, rows_at(pos * n2, n2), :].astype(F32)
        for k in range(3):
            total = total + recv2[n, k].astype(F32)
        buf2[n] = total.astype(BF16)
        third.append(
            copy(buf2.at[n, rows_at((1 - xh) * n3, n3)], recv3.at[n], 2, n, 0, at_x)
        )

    def third_sum(n):
        third[n].wait()
        total = buf2[n, rows_at(xh * n3, n3), :].astype(F32) + recv3[n].astype(F32)
        here = rows_at(bases[n] + xh * n3, n3)
        out_ref[here, :] = total.astype(BF16)
        ahead.append(copy(out_ref.at[here], out_ref.at[here], 3, n, 0, at_x))

    def share_second(n):
        ahead[n].wait()
        here = rows_at(bases[n], n2)
        _, (_, at) = streams[n][0]
        for k in range(1, 4):
            later.append(copy(out_ref.at[here], out_ref.at[here], 4, n, k - 1, at(k)))

    def share_first(n):
        for c in later[3 * n : 3 * n + 3]:
            c.wait()
        ((pos, at), _), start = streams[n]
        here = rows_at(start + pos * n1, n1)
        for k in range(1, 4):
            ended.append(copy(out_ref.at[here], out_ref.at[here], 5, n, k - 1, at(k)))

    column_sums(kept_g, got_g, far_g, full_g)
    others = [near(far_g, other_g, 6, at_cross)]
    first_sum(0)
    first_sum(1)
    column_sums(kept_u, got_u, far_u, full_u)
    first_sum(2)
    first_sum(3)
    for c in small:
        c.wait()
    small_in[4 + y] = small_total(0, 4)
    small = [small_copy(4 + y, 3 + k - 1, at_y(k)) for k in range(1, 4)]
    second_sum(0)
    second_sum(1)
    third_sum(0)
    third_sum(1)
    second_sum(2)
    second_sum(3)
    for c in small:
        c.wait()
    small_in[8 + xh] = small_total(4, 4)
    small = small_copy(8 + xh, 6, at_x)
    share_second(0)
    share_second(1)
    third_sum(2)
    third_sum(3)
    share_first(0)
    share_first(1)
    share_second(2)
    share_second(3)
    others.append(near(far_u, other_u, 7, at_cross))
    share_first(2)
    share_first(3)
    small.wait()
    small_out_ref[t] = small_total(8, 2)
    small = [
        near(small_out_ref.at[t], small_out_ref.at[t], 9 + i, there)
        for i, there in enumerate((at_swap, at_cross, at_diag))
    ]
    row_sums().wait()
    arrived(others[0], other_g, full_g)
    arrived(others[1], other_u, full_u)
    others[2].wait()
    kd[0] = other_d[...].astype(F32)
    store = pltpu.make_async_copy(kd.at[0], full_d.at[1 - side], ws.at[2, 2])
    store.start()
    store.wait()
    for c in small + ended:
        c.wait()


def run_tail(
    stack, small, keep, sent, x, mid_grad, fs, gain, mid, returned, place, gates, pieces
):
    rows, cols = stack.shape
    half = rows // 2
    length = x.shape[0]
    deep, wide_half = pieces[0].shape
    span = wide_half // 2
    shapes = [(deep, span), (deep, span), (span, deep)]
    whole = pl.BlockSpec(memory_space=pltpu.VMEM)
    free = pl.BlockSpec(memory_space=pl.ANY)
    f = jax.ShapeDtypeStruct
    vm = pltpu.VMEM
    return pl.pallas_call(
        tail_body,
        in_specs=[free] + [whole] * 8 + [free, whole, whole] + [free] * 6,
        out_specs=[whole] * 4 + [free] * 3,
        out_shape=[
            f(stack.shape, BF16),
            f((4,) + small.shape, BF16),
            f(x.shape, F32),
            f(x.shape, F32),
        ]
        + [f((2,) + shape, F32) for shape in shapes],
        scratch_shapes=[
            vm((4, half // 8, cols), BF16),
            vm(returned.shape, BF16),
            vm((4, 3, half // 8, cols), BF16),
            vm((4, half // 8, cols), BF16),
            vm((4, 3, half // 32, cols), BF16),
            vm((4, half // 32, cols), BF16),
            vm((4, half // 64, cols), BF16),
            vm((10,) + small.shape, BF16),
            vm((length, 2 * cols), BF16),
            vm((length, 2 * cols), BF16),
            vm((length, 2 * cols), BF16),
            vm((length, cols), BF16),
            vm((length, cols), BF16),
            vm((length, cols), BF16),
            vm((length, cols), BF16),
            vm((4, length, LANES), F32),
            vm((2, 512, wide_half), F32),
            vm((2, 512, wide_half), BF16),
            vm((2, 512, span), F32),
            vm((2, span, deep), F32),
            vm((2, span, deep), BF16),
            vm((deep, span), BF16),
            vm((deep, span), BF16),
            vm((span, deep), BF16),
        ]
        + [vm(shape, BF16) for shape in shapes]
        + [
            pltpu.SemaphoreType.DMA((6, 4, 3)),
            pltpu.SemaphoreType.DMA((6, 4, 3)),
            pltpu.SemaphoreType.DMA((7,)),
            pltpu.SemaphoreType.DMA((7,)),
            pltpu.SemaphoreType.DMA((12,)),
            pltpu.SemaphoreType.DMA((12,)),
            pltpu.SemaphoreType.DMA((4, 3)),
            pltpu.SemaphoreType.DMA((5,)),
        ],
        compiler_params=pltpu.CompilerParams(
            collective_id=0, has_side_effects=True, vmem_limit_bytes=62 << 20
        ),
        cost_estimate=pl.CostEstimate(flops=0, bytes_accessed=500_000_000, transcendentals=0),
        name="sum_over_dp",
    )(stack, small, keep, sent, x, mid_grad, fs, gain, mid, returned, place, gates, *pieces)


def per_device(
    layer_input,
    attn_norm,
    w_query,
    w_key,
    w_value,
    query_norm,
    key_norm,
    w_output,
    moe_norm,
    w_router,
    w_gate,
    w_up,
    w_down,
    segments,
    positions,
    routes,
    out_grad,
):
    length, quarter = layer_input.shape
    width = 4 * quarter
    rank_t = lax.axis_index("tensor")
    groups = lax.axis_size("dp")
    experts = 2 * groups

    labels = segments
    gain_q = query_norm[None, :]
    gain_k = key_norm[None, :]
    gain_1 = attn_norm[None, :]
    gain_2 = moe_norm[None, :]
    (
        cosine, sine, normed_in, first_scale, qpre, kpre, query, key, values, mixed, mid, mids, grads_full, normed_mid, gates,
        place, rows, late_rows, grad_rows, *expert_weights,
    ) = run_front(
        layer_input, out_grad, gain_1, gain_2, w_query, w_key, w_value, w_output, gain_q, gain_k,
        positions, labels, routes.T, w_router, w_gate, w_up, w_down, groups,
    )

    expert_out, back_rows, *pieces = run_experts(rows, late_rows, grad_rows, expert_weights)

    stack, small, mid_grad, keep, sent, returned = run_middle(
        back_rows, expert_out, place, gates, normed_mid, w_router, mid, out_grad, mids,
        grads_full, gain_2, normed_in, w_query, w_key, w_value, w_output, gain_q, gain_k, cosine,
        sine, labels, qpre, kpre, query, key, values, mixed,
    )

    big, everywhere, input_grad, layer_output, *expert_grads = run_tail(
        stack, small, keep, sent, layer_input, mid_grad, first_scale, gain_1, mid,
        returned, place, gates, pieces,
    )
    small = lax.dynamic_index_in_dim(everywhere, rank_t, 0, keepdims=False)
    everywhere = everywhere.astype(F32)
    rows_w = w_query.shape[0]
    rows_o = w_output.shape[0]
    summed = [big[width + i * rows_w : width + (i + 1) * rows_w].astype(F32) for i in range(3)]
    output_grad = jnp.concatenate(
        [big[i * rows_o : (i + 1) * rows_o] for i in range(4)], axis=1
    ).astype(F32)
    return (
        layer_output,
        input_grad,
        everywhere[:, experts].reshape(width),
        summed[0],
        summed[1],
        summed[2],
        small[experts + 2].astype(F32),
        small[experts + 3].astype(F32),
        output_grad,
        everywhere[:, experts + 1].reshape(width),
        everywhere[:, :experts]
        .reshape(4, 2, groups, quarter)
        .transpose(0, 3, 2, 1)
        .reshape(width, experts),
        expert_grads[0],
        expert_grads[1],
        expert_grads[2],
    )


def solution(mesh):
    placed = (
        P("dp", "tensor"),
        P(),
        P(None, "tensor"),
        P(None, "tensor"),
        P(None, "tensor"),
        P("tensor"),
        P("tensor"),
        P("tensor", None),
        P(),
        P(),
        P("dp", None, "tensor"),
        P("dp", None, "tensor"),
        P("dp", "tensor", None),
        P("dp", None),
        P("dp", None),
        P("dp", None),
        P("dp", "tensor"),
    )
    return jax.shard_map(
        per_device,
        mesh=mesh,
        in_specs=placed,
        out_specs=(
            P("dp", "tensor"),
            P("dp", "tensor"),
            P(),
            P(None, "tensor"),
            P(None, "tensor"),
            P(None, "tensor"),
            P("tensor"),
            P("tensor"),
            P("tensor", None),
            P(),
            P(),
            P("dp", None, "tensor"),
            P("dp", None, "tensor"),
            P("dp", "tensor", None),
        ),
        check_vma=False,
    )
```

```python
import math

import jax
import jax.numpy as jnp
from jax import lax
from jax.experimental import pallas as pl
from jax.experimental.pallas import tpu as pltpu
from jax.sharding import PartitionSpec as P

HDIM = 128
TOP = 8
SLOTS = 64
HALF = SLOTS // 2
EPS = 1e-06
HIGH = lax.Precision.HIGHEST
F32 = jnp.float32
BF16 = jnp.bfloat16
MESH = pl.DeviceIdType.MESH
SMALL = 80
LANES = 128
LATE = 8


def dot(a, b, dims, **kw):
    return lax.dot_general(a, b, (dims, ((), ())), preferred_element_type=F32, **kw)


def nn(a, b):
    return dot(a, b, ((1,), (0,)))


def nt(a, b):
    return dot(a, b, ((1,), (1,)))


def tn(a, b):
    return dot(a, b, ((0,), (0,)))


def two_parts(column):
    high = column.astype(BF16)
    rest = (column - high.astype(F32)).astype(BF16)
    lane = lax.broadcasted_iota(jnp.int32, (column.shape[0], LANES), 1)
    return jnp.where(
        lane == 0, high.astype(F32), jnp.where(lane == 1, rest.astype(F32), 0.0)
    ).astype(BF16)


def one_column(pair):
    wide = pair.astype(F32)
    return wide[:, 0:1] + wide[:, 1:2]


def expert_body(
    rows_in, rows_late, og_in, wg_all, wu_all, wd_all,
    out_rows, back_in, kept_g, kept_u, kept_d, got_g, got_u, got_d,
    rows_s, og_s, wgu_s, wd_s, back_s, gu_s, hid_s, keep_s, move_s, down_keep, down_move,
    rs_sem, og_sem, w_sem, bs, br, ls, ks, ms, mr, late_s, late_r, out_ref, out_sem,
):
    plane = Plane()
    swap = (plane.dp, lax.axis_index("tensor") + 1 - 2 * plane.core)
    groups, slots, more = rows_s.shape
    width = og_s.shape[2]
    hidden = hid_s.shape[1]
    span = hidden // 4
    per = groups // 4
    tile = per * slots

    late = rows_late.shape[0]
    early = groups - late

    def load(e, _):
        g = plane.source(e)

        @pl.when(e < early)
        def _():
            pltpu.make_async_copy(rows_in.at[g], rows_s.at[e], rs_sem.at[e // per]).start()

        pltpu.make_async_copy(og_in.at[g], og_s.at[e], og_sem.at[e // per]).start()
        return 0

    lax.fori_loop(0, per, load, 0)
    w_copies = []
    for i in range(4):
        at = slice(i * span, (i + 1) * span)
        high = slice(hidden + i * span, hidden + (i + 1) * span)
        w_copies.append(pltpu.make_async_copy(wg_all.at[i], wgu_s.at[:, at], w_sem.at[0, i]))
        w_copies.append(pltpu.make_async_copy(wu_all.at[i], wgu_s.at[:, high], w_sem.at[1, i]))
    for i in range(4):
        at = slice(i * span, (i + 1) * span)
        w_copies.append(pltpu.make_async_copy(wd_all.at[i], wd_s.at[at], w_sem.at[2, i]))
    for c in w_copies:
        c.start()
    lax.fori_loop(per, groups, load, 0)

    barrier = pltpu.get_barrier_semaphore()

    plane.greet(barrier)
    pl.semaphore_signal(barrier, inc=1, device_id=swap, device_id_type=MESH)
    pl.semaphore_wait(barrier, groups)

    def late_copy(i):
        return pltpu.make_async_remote_copy(
            src_ref=rows_late.at[i],
            dst_ref=rows_s.at[early + i],
            send_sem=late_s.at[i],
            recv_sem=late_r.at[i],
            device_id=plane.device(plane.entry(early + i)),
            device_id_type=MESH,
        )

    def late_start(i, _):
        late_copy(i).start()
        return 0

    lax.fori_loop(0, late - 1, late_start, 0)
    own_rows = pltpu.make_async_copy(rows_late.at[late - 1], rows_s.at[groups - 1], ls.at[3])
    own_rows.start()

    def back_copy(e):
        g = plane.source(e)
        return pltpu.make_async_remote_copy(
            src_ref=back_s.at[e],
            dst_ref=back_in.at[plane.dp],
            send_sem=bs.at[e],
            recv_sem=br.at[e],
            device_id=plane.device(g),
            device_id_type=MESH,
        )

    own_back = pltpu.make_async_copy(back_s.at[groups - 1], back_in.at[plane.dp], ls.at[0])

    def one_tile(k, _):
        first = pl.multiple_of(k * per, per)
        here = pl.ds(pl.multiple_of(k * tile, tile), tile)
        part = pl.ds(first, per)

        @pl.when(k < early // per)
        def _():
            pltpu.make_async_copy(rows_in.at[pl.ds(0, per)], rows_s.at[part], rs_sem.at[k]).wait()

        @pl.when(k >= early // per)
        def _():
            def arrive(j, _):
                i = first + j - early

                @pl.when(i < late - 1)
                def _():
                    late_copy(i).wait()

                @pl.when(i == late - 1)
                def _():
                    own_rows.wait()

                return 0

            lax.fori_loop(0, per, arrive, 0)

        @pl.when(k == 0)
        def _():
            for c in w_copies[:8]:
                c.wait()

        mine = rows_s[part].reshape(tile, more)
        rows = mine[:, :width]
        gate = one_column(mine[:, width:])
        both = nn(rows, wgu_s[...])
        gp = both[:, :hidden]
        up = both[:, hidden:]
        sig = jax.nn.sigmoid(gp)
        act = gp * sig
        hid = act * up
        hid_s[here, :] = (gate * hid).astype(BF16)

        @pl.when(k == 0)
        def _():
            for c in w_copies[8:]:
                c.wait()

        low = nn(hid.astype(BF16), wd_s[...]).astype(BF16)
        out_ref[part] = low.reshape(per, slots, width)
        pltpu.make_async_copy(out_ref.at[part], out_rows.at[part], out_sem.at[k]).start()
        pltpu.make_async_copy(og_in.at[pl.ds(0, per)], og_s.at[part], og_sem.at[k]).wait()
        grads = og_s[part].reshape(tile, width)
        slot = jnp.sum(grads.astype(F32) * low.astype(F32), axis=1, keepdims=True)
        back_s[part, :, width:] = two_parts(slot).reshape(per, slots, more - width)
        hidden_grad = gate * nt(grads, wd_s[...])
        gu_s[here, :hidden] = (hidden_grad * up * sig * (1.0 + gp * (1.0 - sig))).astype(BF16)
        gu_s[here, hidden:] = (hidden_grad * act).astype(BF16)
        back = nt(gu_s[here, :], wgu_s[...]).astype(BF16)
        back_s[part, :, :width] = back.reshape(per, slots, width)

        def send(j, _):
            e = first + j

            @pl.when(e < groups - 1)
            def _():
                back_copy(e).start()

            @pl.when(e == groups - 1)
            def _():
                own_back.start()

            return 0

        lax.fori_loop(0, per, send, 0)
        return 0

    lax.fori_loop(0, 4, one_tile, 0)

    half = hidden // 2
    wide_block = keep_s.shape[1]

    def column_copies(i, slot):
        at = pl.ds(pl.multiple_of(i * wide_block, wide_block), wide_block)
        local = [
            pltpu.make_async_copy(keep_s.at[slot, :, :half], kept_g.at[at], ks.at[slot, 0]),
            pltpu.make_async_copy(keep_s.at[slot, :, half:], kept_u.at[at], ks.at[slot, 1]),
        ]
        far = [
            pltpu.make_async_remote_copy(
                src_ref=move_s.at[slot, :, side],
                dst_ref=target.at[at],
                send_sem=ms.at[slot, n],
                recv_sem=mr.at[i, n],
                device_id=swap,
                device_id_type=MESH,
            )
            for n, (side, target) in enumerate(
                ((slice(0, half), got_g), (slice(half, hidden), got_u))
            )
        ]
        return local + far

    def columns(i, _):
        slot = lax.rem(i, 2)

        @pl.when(i >= 2)
        def _():
            for c in column_copies(i - 2, slot):
                c.wait()

        at = pl.ds(pl.multiple_of(i * wide_block, wide_block), wide_block)
        rows = rows_s[:, :, at].reshape(groups * slots, wide_block)
        grad = tn(rows, gu_s[...])
        keep_s[slot, :, :half] = grad[:, :half]
        keep_s[slot, :, half:] = grad[:, hidden : hidden + half]
        move_s[slot, :, :half] = grad[:, half:hidden].astype(BF16)
        move_s[slot, :, half:] = grad[:, hidden + half :].astype(BF16)
        for c in column_copies(i, slot):
            c.start()
        return 0

    steps = width // wide_block
    lax.fori_loop(0, steps, columns, 0)
    downs = []
    for i in range(4):
        at = slice(i * span, (i + 1) * span)
        grad = tn(hid_s[:, at], og_s[...].reshape(groups * slots, width))
        if i < 2:
            down_keep[at] = grad
            downs.append(pltpu.make_async_copy(down_keep.at[at], kept_d.at[at], ls.at[1 + i]))
        else:
            at = slice((i - 2) * span, (i - 1) * span)
            down_move[at] = grad.astype(BF16)
            downs.append(
                pltpu.make_async_remote_copy(
                    src_ref=down_move.at[at],
                    dst_ref=got_d.at[at],
                    send_sem=ms.at[2, i - 2],
                    recv_sem=mr.at[steps, i - 2],
                    device_id=swap,
                    device_id_type=MESH,
                )
            )
        downs[-1].start()
    for i in (steps - 2, steps - 1):
        for c in column_copies(i, i % 2):
            c.wait()
    for c in downs:
        c.wait()

    def finish(e, _):
        back_copy(e).wait()
        return 0

    lax.fori_loop(0, groups - 1, finish, 0)
    own_back.wait()

    def stored(k, _):
        part = pl.ds(pl.multiple_of(k * per, per), per)
        pltpu.make_async_copy(out_ref.at[part], out_rows.at[part], out_sem.at[k]).wait()
        return 0

    lax.fori_loop(0, 4, stored, 0)


def run_experts(rows, late, grads, weights):
    groups, slots, more = rows.shape
    width = grads.shape[2]
    hidden = 4 * weights[0].shape[2]
    half = hidden // 2
    count = groups * slots
    block = 256
    free = pl.BlockSpec(memory_space=pl.ANY)
    f = jax.ShapeDtypeStruct
    vm = pltpu.VMEM
    dma = pltpu.SemaphoreType.DMA
    return pl.pallas_call(
        expert_body,
        in_specs=[free] * 6,
        out_specs=[free] * 8,
        out_shape=[
            f((groups, slots, width), BF16),
            f((groups, slots, more), BF16),
            f((width, half), F32),
            f((width, half), F32),
            f((half, width), F32),
            f((width, half), BF16),
            f((width, half), BF16),
            f((half, width), BF16),
        ],
        scratch_shapes=[
            vm((groups, slots, more), BF16),
            vm((groups, slots, width), BF16),
            vm((width, 2 * hidden), BF16),
            vm((hidden, width), BF16),
            vm((groups, slots, more), BF16),
            vm((count, 2 * hidden), BF16),
            vm((count, hidden), BF16),
            vm((2, block, hidden), F32),
            vm((2, block, hidden), BF16),
            vm((half, width), F32),
            vm((half, width), BF16),
            dma((4,)),
            dma((4,)),
            dma((3, 4)),
            dma((31,)),
            dma((31,)),
            dma((4,)),
            dma((2, 2)),
            dma((3, 2)),
            dma((width // block + 1, 2)),
            dma((late.shape[0],)),
            dma((late.shape[0],)),
            vm((groups, slots, width), BF16),
            dma((4,)),
        ],
        compiler_params=pltpu.CompilerParams(
            collective_id=2, has_side_effects=True, vmem_limit_bytes=61 << 20
        ),
        name="experts",
    )(rows, late, grads, *weights)


def head_scale(pre):
    return lax.rsqrt(jnp.mean(pre * pre, axis=1, keepdims=True) + EPS)


def turn(value, cosine, sine):
    return value * cosine + pltpu.roll(value, HDIM // 2, 1) * sine


def softmax_rows(query, key, same):
    raw = nt(query, key) * HDIM ** (-0.5)
    raw = jnp.where(same, raw, -1e30)
    powered = jnp.exp(raw - jnp.max(raw, axis=1, keepdims=True))
    return powered / jnp.sum(powered, axis=1, keepdims=True)


class Near:
    def __init__(self, send_sems, recv_sems):
        self.dp = lax.axis_index("dp")
        self.t = lax.axis_index("tensor")
        self.core = lax.rem(self.t, 2)
        self.first_core = self.core == 0
        self.low_x = self.t < 2
        self.far = lax.rem(self.t + 2, 4)
        self.swap = (self.dp, self.t + 1 - 2 * self.core)
        self.cross = (self.dp, self.far)
        self.diag = (self.dp, self.far + 1 - 2 * self.core)
        self.sems = (send_sems, recv_sems)
        self.used = 0

    def send(self, source, target, device):
        k = self.used
        self.used = k + 1
        c = pltpu.make_async_remote_copy(
            src_ref=source,
            dst_ref=target,
            send_sem=self.sems[0].at[k],
            recv_sem=self.sems[1].at[k],
            device_id=device,
            device_id_type=MESH,
        )
        c.start()
        return c

    def gather_start(self, buf):
        here = buf.at[self.t]
        return [self.send(here, here, self.cross), self.send(here, here, self.swap)]

    def gather_relay(self, buf, copies):
        copies[0].wait()
        there = buf.at[self.far]
        copies.append(self.send(there, there, self.swap))

    def split(self, part, low_s, high_s, sent):
        quarter = part.shape[1] // 4
        p = [part[:, i * quarter : (i + 1) * quarter] for i in range(4)]
        low_s[...] = jnp.where(self.first_core, p[0], p[1])
        high_s[...] = jnp.where(self.first_core, p[2], p[3])
        sent[:, :quarter] = jnp.where(self.first_core, p[1], p[0]).astype(BF16)
        sent[:, quarter:] = jnp.where(self.first_core, p[3], p[2]).astype(BF16)

    def sum_parts(self, low_s, high_s, sent, got, go, back):
        quarter = go.shape[1]
        self.send(sent, got, self.swap).wait()
        low = low_s[...] + got[:, :quarter].astype(F32)
        high = high_s[...] + got[:, quarter:].astype(F32)
        go[...] = jnp.where(self.low_x, high, low).astype(BF16)
        self.send(go, back, self.cross).wait()
        return jnp.where(self.low_x, low, high) + back[...].astype(F32)


class Plane:
    def __init__(self):
        self.dp = lax.axis_index("dp")
        t = lax.axis_index("tensor")
        self.y = lax.rem(self.dp, 4)
        self.xh = lax.rem(self.dp // 4, 2)
        self.z = self.dp // 8
        self.core = lax.rem(t, 2)
        self.side = lax.rem(t // 2 + self.xh, 2)

    def at(self, dz, dx, dy):
        return (lax.rem(self.z + dz, 4) * 2 + lax.rem(self.xh + dx, 2)) * 4 + lax.rem(
            self.y + dy, 4
        )

    def device(self, group):
        return (group, lax.rem(self.side + lax.rem(group // 4, 2), 2) * 2 + self.core)

    def offset(self, e):
        dz = 3 - lax.rem(e, 4)
        dx = 1 - lax.rem(e // 4, 2)
        dy = lax.rem(e // 8 + 1 + dz, 4)
        return dz, dx, dy

    def entry(self, e):
        return self.at(*self.offset(e))

    def source(self, e):
        dz, dx, dy = self.offset(e)
        return self.at(4 - dz, 2 - dx, 4 - dy)

    def greet(self, barrier):
        def one(e, _):
            pl.semaphore_signal(
                barrier, inc=1, device_id=self.device(self.entry(e)), device_id_type=MESH
            )
            return 0

        lax.fori_loop(0, 31, one, 0)

    def exchange(self, source, target, send_sems, recv_sems, local_sem, back, count=32):
        def copy(e):
            group = self.source(e) if back else self.entry(e)
            return pltpu.make_async_remote_copy(
                src_ref=source.at[e if back else group],
                dst_ref=target.at[self.dp],
                send_sem=send_sems.at[e],
                recv_sem=recv_sems.at[e],
                device_id=self.device(group),
                device_id_type=MESH,
            )

        def start(e, _):
            copy(e).start()
            return 0

        def finish(e, _):
            copy(e).wait()
            return 0

        lax.fori_loop(0, min(count, 31), start, 0)
        if count == 32:
            own = pltpu.make_async_copy(
                source.at[31 if back else self.dp], target.at[self.dp], local_sem
            )
            own.start()

        def wait():
            lax.fori_loop(0, min(count, 31), finish, 0)
            if count == 32:
                own.wait()

        return wait


def wide(buf):
    return jnp.concatenate([buf[i] for i in range(4)], axis=1)


def as_column(row):
    return jnp.broadcast_to(row.astype(F32), (LANES, row.shape[1])).T[:, :1]


def by_side(experts):
    half = experts // 2
    r = lax.broadcasted_iota(jnp.int32, (experts, experts), 0)
    e = lax.broadcasted_iota(jnp.int32, (experts, experts), 1)
    return jnp.where(e == 2 * lax.rem(r, half) + r // half, 1.0, 0.0)


def front_body(
    x_ref, og_ref, gain1_ref, gain2_ref, wq_in, wk_in, wv_in, wo_in, qn_ref, kn_ref, places_ref,
    row_ref, routes_ref, router_ref, wg_ref, wu_ref, wd_ref,
    *rest,
):
    cos_ref, sin_ref, fs_ref, gates_ref, place_ref = rest[:5]
    outs, (rows_in, rows_late, og_in, wg_all, wu_all, wd_all), rest = rest[5:16], rest[16:22], rest[22:]
    held, rest = rest[:11], rest[11:]
    normed_ref, qpre_ref, kpre_ref, q_ref, k_ref, v_ref, mixed_ref, mid_ref, mids_ref, ogs_ref, nm_ref = held
    wq_ref, wk_ref, wv_ref, wo_ref, w_sem, out_sem, *rest = rest
    (
        xs, low_s, high_s, sent, got, go, back, og_out, rows_out, ts, tr, as_, ar, bs, br, ls, late_sem,
    ) = rest
    loads = [
        pltpu.make_async_copy(source, target, w_sem.at[i])
        for i, (source, target) in enumerate(
            ((wq_in, wq_ref), (wk_in, wk_ref), (wv_in, wv_ref), (wo_in, wo_ref))
        )
    ]
    saves = [
        pltpu.make_async_copy(source, target, out_sem.at[i])
        for i, (source, target) in enumerate(zip(held, outs))
    ]

    def save(*which):
        for i in which:
            saves[i].start()

    near = Near(ts, tr)
    plane = Plane()
    side = plane.side
    barrier = pltpu.get_barrier_semaphore()
    plane.greet(barrier)
    pl.semaphore_signal(barrier, inc=1, device_id=near.swap, device_id_type=MESH)
    pl.semaphore_signal(barrier, inc=1, device_id=near.cross, device_id_type=MESH)
    pl.semaphore_wait(barrier, 33)
    t = near.t
    length = x_ref.shape[0]
    quarter = x_ref.shape[1]
    width = 4 * quarter

    ogs_ref[t] = og_ref[...].astype(BF16)
    og_copies = near.gather_start(ogs_ref)
    xs[t] = x_ref[...].astype(BF16)
    x_copies = near.gather_start(xs)
    weights = ((wg_ref, wg_all), (wu_ref, wu_all), (wd_ref, wd_all))
    kept = [
        pltpu.make_async_copy(w.at[side], w_all.at[0], ls.at[2 + i])
        for i, (w, w_all) in enumerate(weights)
    ]
    w_cross = [near.send(wg_ref.at[1 - side], wg_all.at[1], near.cross)]
    for c in loads:
        c.start()

    experts_all = router_ref.shape[1]
    number = lax.broadcasted_iota(jnp.int32, (experts_all, length), 0)
    number = 2 * lax.rem(number, experts_all // 2) + number // (experts_all // 2)
    chosen = routes_ref[0:1, :] == number
    for k in range(1, TOP):
        chosen = jnp.logical_or(chosen, routes_ref[k : k + 1, :] == number)
    mask = jnp.where(chosen, 1.0, 0.0)
    earlier = lax.broadcasted_iota(jnp.int32, (length, length), 0) < lax.broadcasted_iota(
        jnp.int32, (length, length), 1
    )
    rank = nn(mask.astype(BF16), jnp.where(earlier, 1.0, 0.0).astype(BF16))
    rank = jnp.where(chosen, rank, -1.0).astype(jnp.int32)
    experts = rank.shape[0] // 2
    place_ref[...] = jnp.where(side == 0, rank[:experts], rank[experts:])
    base = near.core * HALF

    def hits(i):
        place = place_ref[i * 8 : (i + 1) * 8, :]
        spots = lax.broadcasted_iota(jnp.int32, (8, HALF, length), 1) + base
        return jnp.broadcast_to(place[:, None, :], (8, HALF, length)) == spots

    near.gather_relay(ogs_ref, og_copies)
    near.gather_relay(xs, x_copies)
    for c in og_copies[1:]:
        c.wait()
    og = wide(ogs_ref)
    save(9)
    for i in range(experts // 8):
        select = jnp.where(hits(i), 1.0, 0.0).reshape(8 * HALF, length).astype(BF16)
        og_out[i * 8 : (i + 1) * 8] = nn(select, og).astype(BF16).reshape(8, HALF, width)
    og_wait = plane.exchange(og_out, og_in, as_, ar, ls.at[0], False)
    for c in kept:
        c.start()
    w_swap = [near.send(w.at[side], w_all.at[2], near.swap) for w, w_all in weights]

    for c in x_copies[1:]:
        c.wait()
    x = wide(xs).astype(F32)
    scale = lax.rsqrt(jnp.mean(x * x, axis=1, keepdims=True) + EPS)
    fs_ref[...] = scale
    normed = (x * scale * gain1_ref[...]).astype(BF16)
    normed_ref[...] = normed
    for c in loads:
        c.wait()
    save(0)
    qpre = nn(normed, wq_ref[...])
    kpre = nn(normed, wk_ref[...])
    qpre_ref[...] = qpre
    kpre_ref[...] = kpre
    v_ref[...] = nn(normed, wv_ref[...]).astype(BF16)
    lane = lax.broadcasted_iota(jnp.int32, (1, HDIM), 1)
    half = HDIM // 2
    step = lax.rem(lane, half).astype(F32) * (-2.0 * math.log(10000.0) / HDIM)
    angle = as_column(places_ref[...]) * jnp.exp(step)
    cosine = jnp.cos(angle)
    sine = jnp.sin(angle) * jnp.where(lane < half, -1.0, 1.0)
    cos_ref[...] = cosine
    sin_ref[...] = sine
    same = as_column(row_ref[...]) == row_ref[...].astype(F32)
    for h in range(q_ref.shape[1] // HDIM):
        at = slice(h * HDIM, (h + 1) * HDIM)
        qh = qpre[:, at]
        kh = kpre[:, at]
        query = turn(qh * head_scale(qh) * qn_ref[:, at], cosine, sine).astype(BF16)
        key = turn(kh * head_scale(kh) * kn_ref[:, at], cosine, sine).astype(BF16)
        q_ref[:, at] = query
        k_ref[:, at] = key
        probs = softmax_rows(query, key, same).astype(BF16)
        mixed_ref[:, at] = nn(probs, v_ref[:, at]).astype(BF16)
    near.split(nn(mixed_ref[...], wo_ref[...]), low_s, high_s, sent)
    save(1, 2, 3, 4, 5, 6)
    mid = x_ref[...] + near.sum_parts(low_s, high_s, sent, got, go, back)
    mid_ref[...] = mid
    mids_ref[t] = mid.astype(BF16)
    mid_copies = near.gather_start(mids_ref)
    w_cross.append(near.send(wu_ref.at[1 - side], wu_all.at[1], near.cross))
    w_cross.append(near.send(wd_ref.at[1 - side], wd_all.at[1], near.cross))
    near.gather_relay(mids_ref, mid_copies)
    for c in mid_copies[1:]:
        c.wait()
    save(7, 8)
    mid = wide(mids_ref).astype(F32)
    scale = lax.rsqrt(jnp.mean(mid * mid, axis=1, keepdims=True) + EPS)
    normed = (mid * scale * gain2_ref[...]).astype(BF16)
    nm_ref[...] = normed
    save(10)

    logits = dot(
        by_side(experts_all), nn(normed, router_ref[...]), ((1,), (1,)), precision=HIGH
    )
    masked = jnp.where(chosen, logits, -1e30)
    raised = jnp.where(chosen, jnp.exp(masked - jnp.max(masked, axis=0, keepdims=True)), 0.0)
    gates = raised / jnp.sum(raised, axis=0, keepdims=True)
    gates_ref[...] = gates
    gates_side = jnp.where(side == 0, gates[:experts], gates[experts:])
    for i in range(experts // 8):
        hit = hits(i)
        select = jnp.where(hit, 1.0, 0.0).reshape(8 * HALF, length).astype(BF16)
        rows_out[i * 8 : (i + 1) * 8, :, :width] = (
            nn(select, normed).astype(BF16).reshape(8, HALF, width)
        )
        gate = jnp.broadcast_to(gates_side[i * 8 : (i + 1) * 8][:, None, :], (8, HALF, length))
        column = jnp.sum(
            jnp.where(hit, gate, 0.0).reshape(8 * HALF, length), axis=1, keepdims=True
        )
        rows_out[i * 8 : (i + 1) * 8, :, width:] = two_parts(column).reshape(8, HALF, LANES)
    early = 32 - rows_late.shape[0]
    rows_wait = plane.exchange(rows_out, rows_in, bs, br, ls.at[1], False, early)

    def late_copy(i):
        return pltpu.make_async_copy(
            rows_out.at[plane.entry(early + i)], rows_late.at[i], late_sem.at[i]
        )

    def late_start(i, _):
        late_copy(i).start()
        return 0

    def late_wait(i, _):
        late_copy(i).wait()
        return 0

    lax.fori_loop(0, 32 - early, late_start, 0)
    for c, (w, w_all) in zip(w_cross, weights):
        c.wait()
        w_swap.append(near.send(w_all.at[1], w_all.at[3], near.swap))
    og_wait()
    rows_wait()
    lax.fori_loop(0, 32 - early, late_wait, 0)
    for c in w_swap + kept + saves:
        c.wait()


def run_front(
    x, og, gain1, gain2, wq, wk, wv, wo, qn, kn, places, labels, routes, router, wg, wu, wd, groups
):
    length, quarter = x.shape
    width = 4 * quarter
    inner = wq.shape[1]
    whole = pl.BlockSpec(memory_space=pltpu.VMEM)
    free = pl.BlockSpec(memory_space=pl.ANY)
    f = jax.ShapeDtypeStruct
    vm = pltpu.VMEM
    dma = pltpu.SemaphoreType.DMA
    held = [
        f((length, width), BF16),
        f((length, inner), F32),
        f((length, inner), F32),
        f((length, inner), BF16),
        f((length, inner), BF16),
        f((length, inner), BF16),
        f((length, inner), BF16),
        f((length, quarter), F32),
        f((4, length, quarter), BF16),
        f((4, length, quarter), BF16),
        f((length, width), BF16),
    ]
    return pl.pallas_call(
        front_body,
        in_specs=[whole] * 4 + [free] * 4 + [whole] * 6 + [free] * 3,
        out_specs=[whole] * 5 + [free] * 17,
        out_shape=[
            f((length, HDIM), F32),
            f((length, HDIM), F32),
            f((length, 1), F32),
            f((2 * groups, length), F32),
            f((groups, length), jnp.int32),
        ]
        + held
        + [
            f((groups, HALF, width + LANES), BF16),
            f((LATE, HALF, width + LANES), BF16),
            f((groups, HALF, width), BF16),
            f((4,) + wg.shape[1:], BF16),
            f((4,) + wu.shape[1:], BF16),
            f((4,) + wd.shape[1:], BF16),
        ],
        scratch_shapes=[vm(h.shape, h.dtype) for h in held]
        + [vm(w.shape, BF16) for w in (wq, wk, wv, wo)]
        + [
            dma((4,)),
            dma((11,)),
            vm((4, length, quarter), BF16),
            vm((length, quarter), F32),
            vm((length, quarter), F32),
            vm((length, 2 * quarter), BF16),
            vm((length, 2 * quarter), BF16),
            vm((length, quarter), BF16),
            vm((length, quarter), BF16),
            vm((groups, HALF, width), BF16),
            vm((groups, HALF, width + LANES), BF16),
            dma((20,)),
            dma((20,)),
            dma((31,)),
            dma((31,)),
            dma((31,)),
            dma((31,)),
            dma((5,)),
            dma((LATE,)),
        ],
        compiler_params=pltpu.CompilerParams(
            collective_id=1, has_side_effects=True, vmem_limit_bytes=60 << 20
        ),
        name="front",
    )(
        x, og, gain1, gain2, wq, wk, wv, wo, qn, kn, places, labels, routes, router, wg, wu, wd
    )


def middle_body(
    rows_ref, out_rows, place_ref, gates_ref, nm_ref, router_ref, mid_ref, og_ref, mids_ref, ogs_ref,
    gain_ref, normed_in, wq_in, wk_in, wv_in, wo_in, qn_ref, kn_ref, cos_ref, sin_ref,
    row_ref, qpre_ref, kpre_ref, q_ref, k_ref, v_ref, mixed_ref,
    stack_out, small_ref, mid_grad_ref, keep_ref, sent_ref, returned,
    low_s, low_f, high_f, sent, got, go, back, ngs, gg_s, stack_ref, probs_s, normed_ref, wq_ref, wk_ref, wv_ref,
    wo_ref, ts, tr, os, orr, ls,
):
    near = Near(ts, tr)
    plane = Plane()
    loads = [
        pltpu.make_async_copy(source, target, ls.at[1 + i])
        for i, (source, target) in enumerate(
            (
                (wo_in, wo_ref),
                (wq_in, wq_ref),
                (wk_in, wk_ref),
                (wv_in, wv_ref),
                (normed_in, normed_ref),
            )
        )
    ]
    for c in loads:
        c.start()
    side = plane.side
    t = near.t
    groups, slots, more = rows_ref.shape
    length, width = normed_ref.shape
    quarter = width // 4
    inner = q_ref.shape[1]

    barrier = pltpu.get_barrier_semaphore()

    plane.greet(barrier)
    pl.semaphore_signal(barrier, inc=1, device_id=near.swap, device_id_type=MESH)
    pl.semaphore_signal(barrier, inc=1, device_id=near.cross, device_id_type=MESH)
    pl.semaphore_wait(barrier, groups + 1)

    out_wait = plane.exchange(out_rows, returned, os, orr, ls.at[0], True)

    base = near.core * slots
    part = None
    for i in range(groups // 8):
        at = slice(i * 8, (i + 1) * 8)
        spots = lax.broadcasted_iota(jnp.int32, (8, slots, length), 1) + base
        hit = jnp.broadcast_to(place_ref[at, :][:, None, :], (8, slots, length)) == spots
        select = jnp.where(hit, 1.0, 0.0).reshape(8 * slots, length)
        tile = rows_ref[at].reshape(8 * slots, more)
        column = one_column(tile[:, width:])
        gg_s[0, at] = jnp.sum((select * column).reshape(8, slots, length), axis=1)
        term = tn(select.astype(BF16), tile[:, :width])
        part = term if part is None else part + term
    gate_swap = near.send(gg_s.at[0], gg_s.at[1], near.swap)
    near.split(part, low_f, high_f, sent)
    swapped = near.send(sent, got, near.swap)
    gate_swap.wait()
    gg_s[2] = gg_s[0] + gg_s[1]
    gate_cross = near.send(gg_s.at[2], gg_s.at[3], near.cross)
    swapped.wait()
    low = low_f[...] + got[:, :quarter].astype(F32)
    high = high_f[...] + got[:, quarter:].astype(F32)
    go[...] = jnp.where(near.low_x, high, low).astype(BF16)
    crossed = near.send(go, back, near.cross)
    gate_cross.wait()
    own, other = gg_s[2], gg_s[3]
    gate_grad = jnp.concatenate(
        [jnp.where(side == 0, own, other), jnp.where(side == 0, other, own)], axis=0
    )
    gates = gates_ref[...]
    logit_grad = gates * (gate_grad - jnp.sum(gates * gate_grad, axis=0, keepdims=True))
    mine = pl.ds(pl.multiple_of(t * quarter, quarter), quarter)
    experts = gates.shape[0]
    router = dot(
        by_side(experts), router_ref[mine, :].astype(F32), ((1,), (1,)), precision=HIGH
    )
    router_back = dot(logit_grad, router, ((0,), (0,)), precision=HIGH)
    small_ref[:experts, :] = dot(
        logit_grad, nm_ref[:, mine].astype(F32), ((1,), (0,)), precision=HIGH
    ).astype(BF16)
    mid = wide(mids_ref).astype(F32)
    scale = lax.rsqrt(jnp.mean(mid * mid, axis=1, keepdims=True) + EPS)
    mid_own = mid_ref[...]
    same = as_column(row_ref[...]) == row_ref[...].astype(F32)
    heads = inner // HDIM

    def attention_probs(h):
        at = slice(h * HDIM, (h + 1) * HDIM)
        probs_s[h] = softmax_rows(q_ref[:, at], k_ref[:, at], same)

    for h in range(heads // 2):
        attention_probs(h)
    crossed.wait()
    ng = jnp.where(near.low_x, low, high) + back[...].astype(F32) + router_back
    ngs[t] = ng.astype(BF16)
    ng_copies = near.gather_start(ngs)
    moe = jnp.sum(ng * mid_own * scale, axis=0, keepdims=True)
    for h in range(heads // 2, heads):
        attention_probs(h)
    near.gather_relay(ngs, ng_copies)
    for c in ng_copies[1:]:
        c.wait()

    weighted = wide(ngs).astype(F32) * gain_ref[...]
    shrink = scale * scale * scale * jnp.mean(weighted * mid, axis=1, keepdims=True)
    mid_grad_ref[...] = og_ref[...] + scale * (ng * gain_ref[:, mine]) - mid_own * shrink
    attn_grad = (wide(ogs_ref).astype(F32) + scale * weighted - mid * shrink).astype(BF16)

    for c in loads:
        c.wait()
    wo_grad = tn(mixed_ref[...], attn_grad).astype(BF16)
    for i in range(4):
        stack_ref[i * inner : (i + 1) * inner, :] = wo_grad[:, i * quarter : (i + 1) * quarter]
    saves = [
        pltpu.make_async_copy(
            stack_ref.at[i * width : (i + 1) * width],
            stack_out.at[i * width : (i + 1) * width],
            ls.at[6 + i],
        )
        for i in range(4)
    ]
    saves[0].start()
    mixed_grad = nt(attn_grad, wo_ref[...]).astype(BF16)
    cosine = cos_ref[...]
    sine = sin_ref[...]
    factor = HDIM ** (-0.5)

    def norm_back(pre, gain, rotated):
        grad = rotated * cosine - pltpu.roll(rotated, HDIM // 2, 1) * sine
        head = head_scale(pre)
        weighted = grad * gain
        mean = jnp.mean(weighted * pre, axis=1, keepdims=True)
        low = (head * weighted - pre * (head * head * head * mean)).astype(BF16)
        return low, jnp.sum(grad * pre * head, axis=0, keepdims=True)

    q_sums, k_sums = [], []
    for h in range(inner // HDIM):
        at = slice(h * HDIM, (h + 1) * HDIM)
        query = q_ref[:, at]
        key = k_ref[:, at]
        mg = mixed_grad[:, at]
        probs = probs_s[h]
        low_s[:, 2 * inner + h * HDIM : 2 * inner + (h + 1) * HDIM] = tn(
            probs.astype(BF16), mg
        ).astype(BF16)
        prob_grad = nt(mg, v_ref[:, at])
        weighted_p = probs * prob_grad
        score = (weighted_p - probs * jnp.sum(weighted_p, axis=1, keepdims=True)).astype(BF16)
        low_q, total = norm_back(qpre_ref[:, at], qn_ref[:, at], nn(score, key) * factor)
        low_s[:, h * HDIM : (h + 1) * HDIM] = low_q
        q_sums.append(total)
        low_k, total = norm_back(kpre_ref[:, at], kn_ref[:, at], tn(score, query) * factor)
        low_s[:, inner + h * HDIM : inner + (h + 1) * HDIM] = low_k
        k_sums.append(total)
    row = lax.broadcasted_iota(jnp.int32, (small_ref.shape[0] - experts, quarter), 0)
    rest = jnp.zeros(row.shape, F32)
    for i, value in enumerate(
        (moe, jnp.concatenate(q_sums, axis=1), jnp.concatenate(k_sums, axis=1))
    ):
        rest = jnp.where(row == i + 1, jnp.broadcast_to(value, row.shape), rest)
    small_ref[experts:, :] = rest.astype(BF16)
    part = None
    for i, w in enumerate((wq_ref, wk_ref, wv_ref)):
        term = nt(low_s[:, i * inner : (i + 1) * inner], w[...])
        part = term if part is None else part + term
    near.split(part, low_f, high_f, sent_ref)
    keep_ref[:, :quarter] = low_f[...]
    keep_ref[:, quarter:] = high_f[...]
    normed = normed_ref[...]
    for i in range(3):
        stack_ref[(i + 1) * width : (i + 2) * width, :] = tn(
            normed, low_s[:, i * inner : (i + 1) * inner]
        ).astype(BF16)
        saves[i + 1].start()

    out_wait()
    for c in saves:
        c.wait()


def run_middle(
    rows, out_rows, place, gates, nm, router, mid, og, mids, ogs, gain, normed, wq, wk, wv, wo, qn,
    kn, cosine, sine, labels, qpre, kpre, q, k, v, mixed,
):
    length, width = normed.shape
    quarter = width // 4
    groups = place.shape[0]
    inner = wq.shape[1]
    whole = pl.BlockSpec(memory_space=pltpu.VMEM)
    free = pl.BlockSpec(memory_space=pl.ANY)
    f = jax.ShapeDtypeStruct
    vm = pltpu.VMEM
    dma = pltpu.SemaphoreType.DMA
    return pl.pallas_call(
        middle_body,
        in_specs=[whole, free] + [whole] * 9 + [free] * 5 + [whole] * 11,
        out_specs=[free] + [whole] * 4 + [free],
        out_shape=[
            f((4 * width, quarter), BF16),
            f((SMALL, quarter), BF16),
            f((length, quarter), F32),
            f((length, 2 * quarter), F32),
            f((length, 2 * quarter), BF16),
            f(out_rows.shape, BF16),
        ],
        scratch_shapes=[
            vm((length, 3 * inner), BF16),
            vm((length, quarter), F32),
            vm((length, quarter), F32),
            vm((length, 2 * quarter), BF16),
            vm((length, 2 * quarter), BF16),
            vm((length, quarter), BF16),
            vm((length, quarter), BF16),
            vm((4, length, quarter), BF16),
            vm((4, groups, length), F32),
            vm((4 * width, quarter), BF16),
            vm((inner // HDIM, length, length), F32),
            vm(normed.shape, BF16),
            vm(wq.shape, BF16),
            vm(wk.shape, BF16),
            vm(wv.shape, BF16),
            vm(wo.shape, BF16),
            dma((8,)),
            dma((8,)),
            dma((31,)),
            dma((31,)),
            dma((10,)),
        ],
        compiler_params=pltpu.CompilerParams(
            collective_id=3, has_side_effects=True, vmem_limit_bytes=61 << 20
        ),
        name="middle",
    )(
        rows, out_rows, place, gates, nm, router, mid, og, mids, ogs, gain, normed, wq, wk, wv, wo,
        qn, kn, cosine, sine, labels, qpre, kpre, q, k, v, mixed,
    )


def tail_body(
    stack_ref, small_ref, keep_ref, sent_ref, x_ref, mid_grad_ref, fs_ref, gain_ref, mid_ref,
    ret_ref, place_ref, gates_ref, kept_g, kept_u, kept_d, got_g, got_u, got_d,
    out_ref, small_out_ref, input_ref, layer_ref, full_g, full_u, full_d,
    own_s, ret_s, recv1, buf1, recv2, buf2, recv3, small_in, got, out_sent, out_got, go, back, out_go, out_back,
    mean_in, kb, gb, nb, kd, gd, far_g, far_u, far_d, other_g, other_u,
    other_d, ss, rs, sss, srs, ts, tr, ws, ls,
):
    dp = lax.axis_index("dp")
    t = lax.axis_index("tensor")
    y = lax.rem(dp, 4)
    xh = lax.rem(dp // 4, 2)
    z = dp // 8
    core = lax.rem(t, 2)
    first_core = core == 0
    low_x = t < 2
    half = stack_ref.shape[0] // 2
    size = half // 2
    n1, n2, n3 = size // 4, size // 16, size // 32
    quarter = x_ref.shape[1]
    ret_load = pltpu.make_async_copy(ret_ref, ret_s, ls.at[4])
    ret_load.start()

    def at_z(k):
        return ((lax.rem(z + k, 4) * 2 + xh) * 4 + y, t)

    def at_y(k):
        return ((z * 2 + xh) * 4 + lax.rem(y + k, 4), t)

    at_x = ((z * 2 + 1 - xh) * 4 + y, t)
    at_swap = (dp, t + 1 - 2 * core)
    at_cross = (dp, lax.rem(t + 2, 4))
    at_diag = (dp, lax.rem(t + 2, 4) + 1 - 2 * core)

    barrier = pltpu.get_barrier_semaphore()
    for k in range(1, 4):
        pl.semaphore_signal(barrier, inc=1, device_id=at_z(k), device_id_type=MESH)
        pl.semaphore_signal(barrier, inc=1, device_id=at_y(k), device_id_type=MESH)
    for there in (at_x, at_swap, at_cross, at_diag):
        pl.semaphore_signal(barrier, inc=1, device_id=there, device_id_type=MESH)
    pl.semaphore_wait(barrier, 10)

    def send(source, target, sems, device):
        c = pltpu.make_async_remote_copy(
            src_ref=source,
            dst_ref=target,
            send_sem=sems[0],
            recv_sem=sems[1],
            device_id=device,
            device_id_type=MESH,
        )
        c.start()
        return c

    def copy(source, target, phase, h, k, device):
        return send(source, target, (ss.at[phase, h, k], rs.at[phase, h, k]), device)

    def small_copy(slot, k, device):
        return send(small_in.at[slot], small_in.at[slot], (sss.at[k], srs.at[k]), device)

    def near(source, target, k, device):
        return send(source, target, (ts.at[k], tr.at[k]), device)

    def rows_at(start, size):
        return pl.ds(pl.multiple_of(start, 64), size)

    ways = (((z, at_z), (y, at_y)), ((y, at_y), (z, at_z)))
    streams = [(ways[h], h * half + s * size) for s in range(2) for h in range(2)]
    first, second, third, ahead, later, ended, own_loads, bases = [], [], [], [], [], [], [], []
    for n, (((pos, at), _), start) in enumerate(streams):
        for k in range(1, 4):
            there = rows_at(start + lax.rem(pos + k, 4) * n1, n1)
            first.append(copy(stack_ref.at[there], recv1.at[n, k - 1], 0, n, k - 1, at(k)))
        bases.append(start + pos * n1)
    for n, base in enumerate(bases):
        own_loads.append(
            pltpu.make_async_copy(stack_ref.at[rows_at(base, n1)], own_s.at[n], ls.at[n])
        )
        own_loads[-1].start()

    swapped = near(sent_ref, got, 0, at_swap)
    side = lax.rem(t // 2 + xh, 2)
    groups, slots, width = ret_ref.shape
    length = x_ref.shape[0]
    gates = jnp.where(side == 0, gates_ref[:groups, :], gates_ref[groups:, :])
    ret_load.wait()
    part = None
    for i in range(groups // 8):
        at = slice(i * 8, (i + 1) * 8)
        spots = lax.broadcasted_iota(jnp.int32, (8, slots, length), 1) + core * slots
        hit = jnp.broadcast_to(place_ref[at, :][:, None, :], (8, slots, length)) == spots
        gate = jnp.broadcast_to(gates[at][:, None, :], (8, slots, length))
        select = jnp.where(hit, gate, 0.0).reshape(8 * slots, length).astype(BF16)
        term = tn(select, ret_s[at].reshape(8 * slots, width))
        part = term if part is None else part + term
    p = [part[:, i * quarter : (i + 1) * quarter] for i in range(4)]
    out_sent[:, :quarter] = jnp.where(first_core, p[1], p[0]).astype(BF16)
    out_sent[:, quarter:] = jnp.where(first_core, p[3], p[2]).astype(BF16)
    out_low = jnp.where(first_core, p[0], p[1])
    out_high = jnp.where(first_core, p[2], p[3])
    out_swapped = near(out_sent, out_got, 1, at_swap)
    swapped.wait()
    low_half = keep_ref[:, :quarter] + got[:, :quarter].astype(F32)
    high_half = keep_ref[:, quarter:] + got[:, quarter:].astype(F32)
    go[...] = jnp.where(low_x, high_half, low_half).astype(BF16)
    crossed = near(go, back, 2, at_cross)
    in_mine = jnp.where(low_x, low_half, high_half)
    out_swapped.wait()
    out_low = out_low + out_got[:, :quarter].astype(F32)
    out_high = out_high + out_got[:, quarter:].astype(F32)
    out_go[...] = jnp.where(low_x, out_high, out_low).astype(BF16)
    crossed.wait()
    in_grad = in_mine + back[...].astype(F32)
    x = x_ref[...]
    fs = fs_ref[...]
    weighted = in_grad * gain_ref[:, pl.ds(pl.multiple_of(t * quarter, quarter), quarter)]
    mean = jnp.sum(weighted * x, axis=1, keepdims=True)
    mean_in[0] = jnp.broadcast_to(mean, mean_in.shape[1:])
    mean_swap = near(mean_in.at[0], mean_in.at[1], 3, at_swap)
    row = lax.broadcasted_iota(jnp.int32, (16, quarter), 0)
    norm_row = jnp.sum(in_grad * x * fs, axis=0, keepdims=True)
    small_in[z] = small_ref[...]
    last = small_ref.shape[0] - 16
    small_in[z, last:, :] = jnp.where(
        row == 0, jnp.broadcast_to(norm_row, (16, quarter)), small_ref[last:, :].astype(F32)
    ).astype(BF16)
    small = [small_copy(z, k - 1, at_z(k)) for k in range(1, 4)]
    mean_swap.wait()
    mean_in[2] = mean_in[0] + mean_in[1]
    mean_cross = near(mean_in.at[2], mean_in.at[3], 4, at_cross)
    out_crossed = near(out_go, out_back, 5, at_cross)
    mean_cross.wait()
    mean = (mean_in[2] + mean_in[3])[:, 0:1] / (4 * quarter)
    input_ref[...] = mid_grad_ref[...] + fs * weighted - x * (fs * fs * fs * mean)
    out_crossed.wait()
    layer_ref[...] = mid_ref[...] + (jnp.where(low_x, out_low, out_high) + out_back[...].astype(F32))

    block = kb.shape[1]
    span = far_d.shape[0]

    def column_sums(kept, gotten, far, mine):
        loads, stores = [], []
        count = kept.shape[0] // block
        for i in range(count):
            at = slice(i * block, (i + 1) * block)
            loads.append(
                (
                    pltpu.make_async_copy(kept.at[at], kb.at[i % 2], ws.at[i % 2, 0]),
                    pltpu.make_async_copy(gotten.at[at], gb.at[i % 2], ws.at[i % 2, 1]),
                )
            )
        for c in loads[0]:
            c.start()
        for i in range(count):
            if i + 1 < count:
                for c in loads[i + 1]:
                    c.start()
            for c in loads[i]:
                c.wait()
            slot = i % 2
            at = slice(i * block, (i + 1) * block)
            total = kb[slot] + gb[slot].astype(F32)
            if i >= 2:
                stores[i - 2].wait()
            nb[slot] = total[:, :span]
            far[at, :] = total[:, span:].astype(BF16)
            stores.append(pltpu.make_async_copy(nb.at[slot], mine.at[side, at], ws.at[slot, 2]))
            stores[-1].start()
        for c in stores[-2:]:
            c.wait()

    def arrived(copy, other, full):
        copy.wait()
        stores = []
        for i in range(other.shape[0] // block):
            slot = i % 2
            at = slice(i * block, (i + 1) * block)
            if i >= 2:
                stores[i - 2].wait()
            nb[slot] = other[at, :].astype(F32)
            stores.append(pltpu.make_async_copy(nb.at[slot], full.at[1 - side, at], ws.at[slot, 2]))
            stores[-1].start()
        for c in stores[-2:]:
            c.wait()

    def row_sums():
        loads = [
            (
                pltpu.make_async_copy(kept_d.at[at], kd.at[i], ws.at[2 + i, 0]),
                pltpu.make_async_copy(got_d.at[at], gd.at[i], ws.at[2 + i, 1]),
            )
            for i, at in enumerate((slice(span, 2 * span), slice(0, span)))
        ]
        for pair in loads:
            for c in pair:
                c.start()
        for c in loads[0]:
            c.wait()
        far_d[...] = (kd[0] + gd[0].astype(F32)).astype(BF16)
        others.append(near(far_d, other_d, 8, at_cross))
        for c in loads[1]:
            c.wait()
        kd[1] = kd[1] + gd[1].astype(F32)
        store = pltpu.make_async_copy(kd.at[1], full_d.at[side], ws.at[2, 2])
        store.start()
        return store

    def small_total(start, count):
        total = small_in[start].astype(F32)
        for i in range(start + 1, start + count):
            total = total + small_in[i].astype(F32)
        return total.astype(BF16)

    def first_sum(n):
        for c in first[3 * n : 3 * n + 3]:
            c.wait()
        own_loads[n].wait()
        total = own_s[n].astype(F32)
        for k in range(3):
            total = total + recv1[n, k].astype(F32)
        buf1[n] = total.astype(BF16)
        _, (pos, at) = streams[n][0]
        for k in range(1, 4):
            there = rows_at(lax.rem(pos + k, 4) * n2, n2)
            second.append(copy(buf1.at[n, there], recv2.at[n, k - 1], 1, n, k - 1, at(k)))
        bases[n] = bases[n] + pos * n2

    def second_sum(n):
        for c in second[3 * n : 3 * n + 3]:
            c.wait()
        _, (pos, _) = streams[n][0]
        total = buf1[n, rows_at(pos * n2, n2), :].astype(F32)
        for k in range(3):
            total = total + recv2[n, k].astype(F32)
        buf2[n] = total.astype(BF16)
        third.append(
            copy(buf2.at[n, rows_at((1 - xh) * n3, n3)], recv3.at[n], 2, n, 0, at_x)
        )

    def third_sum(n):
        third[n].wait()
        total = buf2[n, rows_at(xh * n3, n3), :].astype(F32) + recv3[n].astype(F32)
        here = rows_at(bases[n] + xh * n3, n3)
        out_ref[here, :] = total.astype(BF16)
        ahead.append(copy(out_ref.at[here], out_ref.at[here], 3, n, 0, at_x))

    def share_second(n):
        ahead[n].wait()
        here = rows_at(bases[n], n2)
        _, (_, at) = streams[n][0]
        for k in range(1, 4):
            later.append(copy(out_ref.at[here], out_ref.at[here], 4, n, k - 1, at(k)))

    def share_first(n):
        for c in later[3 * n : 3 * n + 3]:
            c.wait()
        ((pos, at), _), start = streams[n]
        here = rows_at(start + pos * n1, n1)
        for k in range(1, 4):
            ended.append(copy(out_ref.at[here], out_ref.at[here], 5, n, k - 1, at(k)))

    column_sums(kept_g, got_g, far_g, full_g)
    others = [near(far_g, other_g, 6, at_cross)]
    first_sum(0)
    first_sum(1)
    column_sums(kept_u, got_u, far_u, full_u)
    first_sum(2)
    first_sum(3)
    for c in small:
        c.wait()
    small_in[4 + y] = small_total(0, 4)
    small = [small_copy(4 + y, 3 + k - 1, at_y(k)) for k in range(1, 4)]
    second_sum(0)
    second_sum(1)
    third_sum(0)
    third_sum(1)
    second_sum(2)
    second_sum(3)
    for c in small:
        c.wait()
    small_in[8 + xh] = small_total(4, 4)
    small = small_copy(8 + xh, 6, at_x)
    share_second(0)
    share_second(1)
    third_sum(2)
    third_sum(3)
    share_first(0)
    share_first(1)
    share_second(2)
    share_second(3)
    others.append(near(far_u, other_u, 7, at_cross))
    share_first(2)
    share_first(3)
    small.wait()
    small_out_ref[t] = small_total(8, 2)
    small = [
        near(small_out_ref.at[t], small_out_ref.at[t], 9 + i, there)
        for i, there in enumerate((at_swap, at_cross, at_diag))
    ]
    row_sums().wait()
    arrived(others[0], other_g, full_g)
    arrived(others[1], other_u, full_u)
    others[2].wait()
    kd[0] = other_d[...].astype(F32)
    store = pltpu.make_async_copy(kd.at[0], full_d.at[1 - side], ws.at[2, 2])
    store.start()
    store.wait()
    for c in small + ended:
        c.wait()


def run_tail(
    stack, small, keep, sent, x, mid_grad, fs, gain, mid, returned, place, gates, pieces
):
    rows, cols = stack.shape
    half = rows // 2
    length = x.shape[0]
    deep, wide_half = pieces[0].shape
    span = wide_half // 2
    shapes = [(deep, span), (deep, span), (span, deep)]
    whole = pl.BlockSpec(memory_space=pltpu.VMEM)
    free = pl.BlockSpec(memory_space=pl.ANY)
    f = jax.ShapeDtypeStruct
    vm = pltpu.VMEM
    return pl.pallas_call(
        tail_body,
        in_specs=[free] + [whole] * 8 + [free, whole, whole] + [free] * 6,
        out_specs=[whole] * 4 + [free] * 3,
        out_shape=[
            f(stack.shape, BF16),
            f((4,) + small.shape, BF16),
            f(x.shape, F32),
            f(x.shape, F32),
        ]
        + [f((2,) + shape, F32) for shape in shapes],
        scratch_shapes=[
            vm((4, half // 8, cols), BF16),
            vm(returned.shape, BF16),
            vm((4, 3, half // 8, cols), BF16),
            vm((4, half // 8, cols), BF16),
            vm((4, 3, half // 32, cols), BF16),
            vm((4, half // 32, cols), BF16),
            vm((4, half // 64, cols), BF16),
            vm((10,) + small.shape, BF16),
            vm((length, 2 * cols), BF16),
            vm((length, 2 * cols), BF16),
            vm((length, 2 * cols), BF16),
            vm((length, cols), BF16),
            vm((length, cols), BF16),
            vm((length, cols), BF16),
            vm((length, cols), BF16),
            vm((4, length, LANES), F32),
            vm((2, 512, wide_half), F32),
            vm((2, 512, wide_half), BF16),
            vm((2, 512, span), F32),
            vm((2, span, deep), F32),
            vm((2, span, deep), BF16),
            vm((deep, span), BF16),
            vm((deep, span), BF16),
            vm((span, deep), BF16),
        ]
        + [vm(shape, BF16) for shape in shapes]
        + [
            pltpu.SemaphoreType.DMA((6, 4, 3)),
            pltpu.SemaphoreType.DMA((6, 4, 3)),
            pltpu.SemaphoreType.DMA((7,)),
            pltpu.SemaphoreType.DMA((7,)),
            pltpu.SemaphoreType.DMA((12,)),
            pltpu.SemaphoreType.DMA((12,)),
            pltpu.SemaphoreType.DMA((4, 3)),
            pltpu.SemaphoreType.DMA((5,)),
        ],
        compiler_params=pltpu.CompilerParams(
            collective_id=0, has_side_effects=True, vmem_limit_bytes=62 << 20
        ),
        cost_estimate=pl.CostEstimate(flops=0, bytes_accessed=500_000_000, transcendentals=0),
        name="sum_over_dp",
    )(stack, small, keep, sent, x, mid_grad, fs, gain, mid, returned, place, gates, *pieces)


def per_device(
    layer_input,
    attn_norm,
    w_query,
    w_key,
    w_value,
    query_norm,
    key_norm,
    w_output,
    moe_norm,
    w_router,
    w_gate,
    w_up,
    w_down,
    segments,
    positions,
    routes,
    out_grad,
):
    length, quarter = layer_input.shape
    width = 4 * quarter
    rank_t = lax.axis_index("tensor")
    groups = lax.axis_size("dp")
    experts = 2 * groups

    labels = segments
    gain_q = query_norm[None, :]
    gain_k = key_norm[None, :]
    gain_1 = attn_norm[None, :]
    gain_2 = moe_norm[None, :]
    (
        cosine, sine, first_scale, gates, place, normed_in, qpre, kpre, query, key, values, mixed, mid,
        mids, grads_full, normed_mid, rows, late_rows, grad_rows, *expert_weights,
    ) = run_front(
        layer_input, out_grad, gain_1, gain_2, w_query, w_key, w_value, w_output, gain_q, gain_k,
        positions, labels, routes.T, w_router, w_gate, w_up, w_down, groups,
    )

    expert_out, back_rows, *pieces = run_experts(rows, late_rows, grad_rows, expert_weights)

    stack, small, mid_grad, keep, sent, returned = run_middle(
        back_rows, expert_out, place, gates, normed_mid, w_router, mid, out_grad, mids,
        grads_full, gain_2, normed_in, w_query, w_key, w_value, w_output, gain_q, gain_k, cosine,
        sine, labels, qpre, kpre, query, key, values, mixed,
    )

    big, everywhere, input_grad, layer_output, *expert_grads = run_tail(
        stack, small, keep, sent, layer_input, mid_grad, first_scale, gain_1, mid,
        returned, place, gates, pieces,
    )
    small = lax.dynamic_index_in_dim(everywhere, rank_t, 0, keepdims=False)
    everywhere = everywhere.astype(F32)
    rows_w = w_query.shape[0]
    rows_o = w_output.shape[0]
    summed = [big[width + i * rows_w : width + (i + 1) * rows_w].astype(F32) for i in range(3)]
    output_grad = jnp.concatenate(
        [big[i * rows_o : (i + 1) * rows_o] for i in range(4)], axis=1
    ).astype(F32)
    return (
        layer_output,
        input_grad,
        everywhere[:, experts].reshape(width),
        summed[0],
        summed[1],
        summed[2],
        small[experts + 2].astype(F32),
        small[experts + 3].astype(F32),
        output_grad,
        everywhere[:, experts + 1].reshape(width),
        everywhere[:, :experts]
        .reshape(4, 2, groups, quarter)
        .transpose(0, 3, 2, 1)
        .reshape(width, experts),
        expert_grads[0],
        expert_grads[1],
        expert_grads[2],
    )


def solution(mesh):
    placed = (
        P("dp", "tensor"),
        P(),
        P(None, "tensor"),
        P(None, "tensor"),
        P(None, "tensor"),
        P("tensor"),
        P("tensor"),
        P("tensor", None),
        P(),
        P(),
        P("dp", None, "tensor"),
        P("dp", None, "tensor"),
        P("dp", "tensor", None),
        P("dp", None),
        P("dp", None),
        P("dp", None),
        P("dp", "tensor"),
    )
    return jax.shard_map(
        per_device,
        mesh=mesh,
        in_specs=placed,
        out_specs=(
            P("dp", "tensor"),
            P("dp", "tensor"),
            P(),
            P(None, "tensor"),
            P(None, "tensor"),
            P(None, "tensor"),
            P("tensor"),
            P("tensor"),
            P("tensor", None),
            P(),
            P(),
            P("dp", None, "tensor"),
            P("dp", None, "tensor"),
            P("dp", "tensor", None),
        ),
        check_vma=False,
    )
```

```python
import math

import jax
import jax.numpy as jnp
from jax import lax
from jax.experimental import pallas as pl
from jax.experimental.pallas import tpu as pltpu
from jax.sharding import PartitionSpec as P

HDIM = 128
TOP = 8
SLOTS = 64
HALF = SLOTS // 2
EPS = 1e-06
HIGH = lax.Precision.HIGHEST
F32 = jnp.float32
BF16 = jnp.bfloat16
MESH = pl.DeviceIdType.MESH
SMALL = 80
LANES = 128
LATE = 8


def dot(a, b, dims, **kw):
    return lax.dot_general(a, b, (dims, ((), ())), preferred_element_type=F32, **kw)


def nn(a, b):
    return dot(a, b, ((1,), (0,)))


def nt(a, b):
    return dot(a, b, ((1,), (1,)))


def tn(a, b):
    return dot(a, b, ((0,), (0,)))


def two_parts(column):
    high = column.astype(BF16)
    rest = (column - high.astype(F32)).astype(BF16)
    lane = lax.broadcasted_iota(jnp.int32, (column.shape[0], LANES), 1)
    return jnp.where(
        lane == 0, high.astype(F32), jnp.where(lane == 1, rest.astype(F32), 0.0)
    ).astype(BF16)


def one_column(pair):
    wide = pair.astype(F32)
    return wide[:, 0:1] + wide[:, 1:2]


def expert_body(
    rows_in, rows_late, og_in, wg_all, wu_all, wd_all,
    out_rows, back_in, kept_g, kept_u, kept_d, got_g, got_u, got_d,
    rows_s, og_s, wgu_s, wd_s, back_s, gu_s, hid_s, keep_s, move_s, down_keep, down_move,
    rs_sem, og_sem, w_sem, bs, br, ls, ks, ms, mr, late_s, late_r, out_ref, out_sem,
):
    plane = Plane()
    swap = (plane.dp, lax.axis_index("tensor") + 1 - 2 * plane.core)
    groups, slots, more = rows_s.shape
    width = og_s.shape[2]
    hidden = hid_s.shape[1]
    span = hidden // 4
    per = groups // 4
    tile = per * slots

    late = rows_late.shape[0]
    early = groups - late

    def load(e, _):
        g = plane.source(e)

        @pl.when(e < early)
        def _():
            pltpu.make_async_copy(rows_in.at[g], rows_s.at[e], rs_sem.at[e // per]).start()

        pltpu.make_async_copy(og_in.at[g], og_s.at[e], og_sem.at[e // per]).start()
        return 0

    lax.fori_loop(0, per, load, 0)
    w_copies = []
    for i in range(4):
        at = slice(i * span, (i + 1) * span)
        high = slice(hidden + i * span, hidden + (i + 1) * span)
        w_copies.append(pltpu.make_async_copy(wg_all.at[i], wgu_s.at[:, at], w_sem.at[0, i]))
        w_copies.append(pltpu.make_async_copy(wu_all.at[i], wgu_s.at[:, high], w_sem.at[1, i]))
    for i in range(4):
        at = slice(i * span, (i + 1) * span)
        w_copies.append(pltpu.make_async_copy(wd_all.at[i], wd_s.at[at], w_sem.at[2, i]))
    for c in w_copies:
        c.start()
    lax.fori_loop(per, groups, load, 0)

    barrier = pltpu.get_barrier_semaphore()

    plane.greet(barrier)
    pl.semaphore_signal(barrier, inc=1, device_id=swap, device_id_type=MESH)
    pl.semaphore_wait(barrier, groups)

    def late_copy(i):
        return pltpu.make_async_remote_copy(
            src_ref=rows_late.at[i],
            dst_ref=rows_s.at[early + i],
            send_sem=late_s.at[i],
            recv_sem=late_r.at[i],
            device_id=plane.device(plane.entry(early + i)),
            device_id_type=MESH,
        )

    def late_start(i, _):
        late_copy(i).start()
        return 0

    lax.fori_loop(0, late - 1, late_start, 0)
    own_rows = pltpu.make_async_copy(rows_late.at[late - 1], rows_s.at[groups - 1], ls.at[3])
    own_rows.start()

    def back_copy(e):
        g = plane.source(e)
        return pltpu.make_async_remote_copy(
            src_ref=back_s.at[e],
            dst_ref=back_in.at[plane.dp],
            send_sem=bs.at[e],
            recv_sem=br.at[e],
            device_id=plane.device(g),
            device_id_type=MESH,
        )

    own_back = pltpu.make_async_copy(back_s.at[groups - 1], back_in.at[plane.dp], ls.at[0])

    def one_tile(k, _):
        first = pl.multiple_of(k * per, per)
        here = pl.ds(pl.multiple_of(k * tile, tile), tile)
        part = pl.ds(first, per)

        @pl.when(k < early // per)
        def _():
            pltpu.make_async_copy(rows_in.at[pl.ds(0, per)], rows_s.at[part], rs_sem.at[k]).wait()

        @pl.when(k >= early // per)
        def _():
            def arrive(j, _):
                i = first + j - early

                @pl.when(i < late - 1)
                def _():
                    late_copy(i).wait()

                @pl.when(i == late - 1)
                def _():
                    own_rows.wait()

                return 0

            lax.fori_loop(0, per, arrive, 0)

        @pl.when(k == 0)
        def _():
            for c in w_copies[:8]:
                c.wait()

        mine = rows_s[part].reshape(tile, more)
        rows = mine[:, :width]
        gate = one_column(mine[:, width:])
        both = nn(rows, wgu_s[...])
        gp = both[:, :hidden]
        up = both[:, hidden:]
        sig = jax.nn.sigmoid(gp)
        act = gp * sig
        hid = act * up
        hid_s[here, :] = (gate * hid).astype(BF16)

        @pl.when(k == 0)
        def _():
            for c in w_copies[8:]:
                c.wait()

        low = nn(hid.astype(BF16), wd_s[...]).astype(BF16)
        out_ref[part] = low.reshape(per, slots, width)
        pltpu.make_async_copy(out_ref.at[part], out_rows.at[part], out_sem.at[k]).start()
        pltpu.make_async_copy(og_in.at[pl.ds(0, per)], og_s.at[part], og_sem.at[k]).wait()
        grads = og_s[part].reshape(tile, width)
        slot = jnp.sum(grads.astype(F32) * low.astype(F32), axis=1, keepdims=True)
        back_s[part, :, width:] = two_parts(slot).reshape(per, slots, more - width)
        hidden_grad = gate * nt(grads, wd_s[...])
        gu_s[here, :hidden] = (hidden_grad * up * sig * (1.0 + gp * (1.0 - sig))).astype(BF16)
        gu_s[here, hidden:] = (hidden_grad * act).astype(BF16)
        back = nt(gu_s[here, :], wgu_s[...]).astype(BF16)
        back_s[part, :, :width] = back.reshape(per, slots, width)

        def send(j, _):
            e = first + j

            @pl.when(e < groups - 1)
            def _():
                back_copy(e).start()

            @pl.when(e == groups - 1)
            def _():
                own_back.start()

            return 0

        lax.fori_loop(0, per, send, 0)
        return 0

    lax.fori_loop(0, 4, one_tile, 0)

    half = hidden // 2
    wide_block = keep_s.shape[1]

    def column_copies(i, slot):
        at = pl.ds(pl.multiple_of(i * wide_block, wide_block), wide_block)
        local = [
            pltpu.make_async_copy(keep_s.at[slot, :, :half], kept_g.at[at], ks.at[slot, 0]),
            pltpu.make_async_copy(keep_s.at[slot, :, half:], kept_u.at[at], ks.at[slot, 1]),
        ]
        far = [
            pltpu.make_async_remote_copy(
                src_ref=move_s.at[slot, :, side],
                dst_ref=target.at[at],
                send_sem=ms.at[slot, n],
                recv_sem=mr.at[i, n],
                device_id=swap,
                device_id_type=MESH,
            )
            for n, (side, target) in enumerate(
                ((slice(0, half), got_g), (slice(half, hidden), got_u))
            )
        ]
        return local + far

    def columns(i, _):
        slot = lax.rem(i, 2)

        @pl.when(i >= 2)
        def _():
            for c in column_copies(i - 2, slot):
                c.wait()

        at = pl.ds(pl.multiple_of(i * wide_block, wide_block), wide_block)
        rows = rows_s[:, :, at].reshape(groups * slots, wide_block)
        grad = tn(rows, gu_s[...])
        keep_s[slot, :, :half] = grad[:, :half]
        keep_s[slot, :, half:] = grad[:, hidden : hidden + half]
        move_s[slot, :, :half] = grad[:, half:hidden].astype(BF16)
        move_s[slot, :, half:] = grad[:, hidden + half :].astype(BF16)
        for c in column_copies(i, slot):
            c.start()
        return 0

    steps = width // wide_block
    lax.fori_loop(0, steps, columns, 0)
    downs = []
    for i in range(4):
        at = slice(i * span, (i + 1) * span)
        grad = tn(hid_s[:, at], og_s[...].reshape(groups * slots, width))
        if i < 2:
            down_keep[at] = grad
            downs.append(pltpu.make_async_copy(down_keep.at[at], kept_d.at[at], ls.at[1 + i]))
        else:
            at = slice((i - 2) * span, (i - 1) * span)
            down_move[at] = grad.astype(BF16)
            downs.append(
                pltpu.make_async_remote_copy(
                    src_ref=down_move.at[at],
                    dst_ref=got_d.at[at],
                    send_sem=ms.at[2, i - 2],
                    recv_sem=mr.at[steps, i - 2],
                    device_id=swap,
                    device_id_type=MESH,
                )
            )
        downs[-1].start()
    for i in (steps - 2, steps - 1):
        for c in column_copies(i, i % 2):
            c.wait()
    for c in downs:
        c.wait()

    def finish(e, _):
        back_copy(e).wait()
        return 0

    lax.fori_loop(0, groups - 1, finish, 0)
    own_back.wait()

    def stored(k, _):
        part = pl.ds(pl.multiple_of(k * per, per), per)
        pltpu.make_async_copy(out_ref.at[part], out_rows.at[part], out_sem.at[k]).wait()
        return 0

    lax.fori_loop(0, 4, stored, 0)


def run_experts(rows, late, grads, weights):
    groups, slots, more = rows.shape
    width = grads.shape[2]
    hidden = 4 * weights[0].shape[2]
    half = hidden // 2
    count = groups * slots
    block = 256
    free = pl.BlockSpec(memory_space=pl.ANY)
    f = jax.ShapeDtypeStruct
    vm = pltpu.VMEM
    dma = pltpu.SemaphoreType.DMA
    return pl.pallas_call(
        expert_body,
        in_specs=[free] * 6,
        out_specs=[free] * 8,
        out_shape=[
            f((groups, slots, width), BF16),
            f((groups, slots, more), BF16),
            f((width, half), F32),
            f((width, half), F32),
            f((half, width), F32),
            f((width, half), BF16),
            f((width, half), BF16),
            f((half, width), BF16),
        ],
        scratch_shapes=[
            vm((groups, slots, more), BF16),
            vm((groups, slots, width), BF16),
            vm((width, 2 * hidden), BF16),
            vm((hidden, width), BF16),
            vm((groups, slots, more), BF16),
            vm((count, 2 * hidden), BF16),
            vm((count, hidden), BF16),
            vm((2, block, hidden), F32),
            vm((2, block, hidden), BF16),
            vm((half, width), F32),
            vm((half, width), BF16),
            dma((4,)),
            dma((4,)),
            dma((3, 4)),
            dma((31,)),
            dma((31,)),
            dma((4,)),
            dma((2, 2)),
            dma((3, 2)),
            dma((width // block + 1, 2)),
            dma((late.shape[0],)),
            dma((late.shape[0],)),
            vm((groups, slots, width), BF16),
            dma((4,)),
        ],
        compiler_params=pltpu.CompilerParams(
            collective_id=2, has_side_effects=True, vmem_limit_bytes=61 << 20
        ),
        name="experts",
    )(rows, late, grads, *weights)


def head_scale(pre):
    return lax.rsqrt(jnp.mean(pre * pre, axis=1, keepdims=True) + EPS)


def turn(value, cosine, sine):
    return value * cosine + pltpu.roll(value, HDIM // 2, 1) * sine


def softmax_rows(query, key, same):
    raw = nt(query, key) * HDIM ** (-0.5)
    raw = jnp.where(same, raw, -1e30)
    powered = jnp.exp(raw - jnp.max(raw, axis=1, keepdims=True))
    return powered / jnp.sum(powered, axis=1, keepdims=True)


class Near:
    def __init__(self, send_sems, recv_sems):
        self.dp = lax.axis_index("dp")
        self.t = lax.axis_index("tensor")
        self.core = lax.rem(self.t, 2)
        self.first_core = self.core == 0
        self.low_x = self.t < 2
        self.far = lax.rem(self.t + 2, 4)
        self.swap = (self.dp, self.t + 1 - 2 * self.core)
        self.cross = (self.dp, self.far)
        self.diag = (self.dp, self.far + 1 - 2 * self.core)
        self.sems = (send_sems, recv_sems)
        self.used = 0

    def send(self, source, target, device):
        k = self.used
        self.used = k + 1
        c = pltpu.make_async_remote_copy(
            src_ref=source,
            dst_ref=target,
            send_sem=self.sems[0].at[k],
            recv_sem=self.sems[1].at[k],
            device_id=device,
            device_id_type=MESH,
        )
        c.start()
        return c

    def gather_start(self, buf):
        here = buf.at[self.t]
        return [self.send(here, here, self.cross), self.send(here, here, self.swap)]

    def gather_relay(self, buf, copies):
        copies[0].wait()
        there = buf.at[self.far]
        copies.append(self.send(there, there, self.swap))

    def split(self, part, low_s, high_s, sent):
        quarter = part.shape[1] // 4
        p = [part[:, i * quarter : (i + 1) * quarter] for i in range(4)]
        low_s[...] = jnp.where(self.first_core, p[0], p[1])
        high_s[...] = jnp.where(self.first_core, p[2], p[3])
        sent[:, :quarter] = jnp.where(self.first_core, p[1], p[0]).astype(BF16)
        sent[:, quarter:] = jnp.where(self.first_core, p[3], p[2]).astype(BF16)

    def sum_parts(self, low_s, high_s, sent, got, go, back):
        quarter = go.shape[1]
        self.send(sent, got, self.swap).wait()
        low = low_s[...] + got[:, :quarter].astype(F32)
        high = high_s[...] + got[:, quarter:].astype(F32)
        go[...] = jnp.where(self.low_x, high, low).astype(BF16)
        self.send(go, back, self.cross).wait()
        return jnp.where(self.low_x, low, high) + back[...].astype(F32)


class Plane:
    def __init__(self):
        self.dp = lax.axis_index("dp")
        t = lax.axis_index("tensor")
        self.y = lax.rem(self.dp, 4)
        self.xh = lax.rem(self.dp // 4, 2)
        self.z = self.dp // 8
        self.core = lax.rem(t, 2)
        self.side = lax.rem(t // 2 + self.xh, 2)

    def at(self, dz, dx, dy):
        return (lax.rem(self.z + dz, 4) * 2 + lax.rem(self.xh + dx, 2)) * 4 + lax.rem(
            self.y + dy, 4
        )

    def device(self, group):
        return (group, lax.rem(self.side + lax.rem(group // 4, 2), 2) * 2 + self.core)

    def offset(self, e):
        dz = 3 - lax.rem(e, 4)
        dx = 1 - lax.rem(e // 4, 2)
        dy = lax.rem(e // 8 + 1 + dz, 4)
        return dz, dx, dy

    def entry(self, e):
        return self.at(*self.offset(e))

    def source(self, e):
        dz, dx, dy = self.offset(e)
        return self.at(4 - dz, 2 - dx, 4 - dy)

    def greet(self, barrier):
        def one(e, _):
            pl.semaphore_signal(
                barrier, inc=1, device_id=self.device(self.entry(e)), device_id_type=MESH
            )
            return 0

        lax.fori_loop(0, 31, one, 0)

    def exchange(self, source, target, send_sems, recv_sems, local_sem, back, count=32):
        def copy(e):
            group = self.source(e) if back else self.entry(e)
            return pltpu.make_async_remote_copy(
                src_ref=source.at[e if back else group],
                dst_ref=target.at[self.dp],
                send_sem=send_sems.at[e],
                recv_sem=recv_sems.at[e],
                device_id=self.device(group),
                device_id_type=MESH,
            )

        def start(e, _):
            copy(e).start()
            return 0

        def finish(e, _):
            copy(e).wait()
            return 0

        lax.fori_loop(0, min(count, 31), start, 0)
        if count == 32:
            own = pltpu.make_async_copy(
                source.at[31 if back else self.dp], target.at[self.dp], local_sem
            )
            own.start()

        def wait():
            lax.fori_loop(0, min(count, 31), finish, 0)
            if count == 32:
                own.wait()

        return wait


def wide(buf):
    return jnp.concatenate([buf[i] for i in range(4)], axis=1)


def as_column(row):
    return jnp.broadcast_to(row.astype(F32), (LANES, row.shape[1])).T[:, :1]


def by_side(experts):
    half = experts // 2
    r = lax.broadcasted_iota(jnp.int32, (experts, experts), 0)
    e = lax.broadcasted_iota(jnp.int32, (experts, experts), 1)
    return jnp.where(e == 2 * lax.rem(r, half) + r // half, 1.0, 0.0)


def front_body(
    x_ref, og_ref, gain1_ref, gain2_ref, wq_in, wk_in, wv_in, wo_in, qn_ref, kn_ref, places_ref,
    row_ref, routes_ref, router_ref, wg_ref, wu_ref, wd_ref,
    *rest,
):
    cos_ref, sin_ref, fs_ref, gates_ref, place_ref = rest[:5]
    outs, (rows_in, rows_late, og_in, wg_all, wu_all, wd_all), rest = rest[5:16], rest[16:22], rest[22:]
    held, rest = rest[:11], rest[11:]
    normed_ref, qpre_ref, kpre_ref, q_ref, k_ref, v_ref, mixed_ref, mid_ref, mids_ref, ogs_ref, nm_ref = held
    wq_ref, wk_ref, wv_ref, wo_ref, w_sem, out_sem, *rest = rest
    (
        xs, low_s, high_s, sent, got, go, back, og_out, rows_out, ts, tr, as_, ar, bs, br, ls, late_sem,
    ) = rest
    loads = [
        pltpu.make_async_copy(source, target, w_sem.at[i])
        for i, (source, target) in enumerate(
            ((wq_in, wq_ref), (wk_in, wk_ref), (wv_in, wv_ref), (wo_in, wo_ref))
        )
    ]
    saves = [
        pltpu.make_async_copy(source, target, out_sem.at[i])
        for i, (source, target) in enumerate(zip(held, outs))
    ]

    def save(*which):
        for i in which:
            saves[i].start()

    near = Near(ts, tr)
    plane = Plane()
    side = plane.side
    barrier = pltpu.get_barrier_semaphore()
    plane.greet(barrier)
    pl.semaphore_signal(barrier, inc=1, device_id=near.swap, device_id_type=MESH)
    pl.semaphore_signal(barrier, inc=1, device_id=near.cross, device_id_type=MESH)
    pl.semaphore_wait(barrier, 33)
    t = near.t
    length = x_ref.shape[0]
    quarter = x_ref.shape[1]
    width = 4 * quarter

    ogs_ref[t] = og_ref[...].astype(BF16)
    og_copies = near.gather_start(ogs_ref)
    xs[t] = x_ref[...].astype(BF16)
    x_copies = near.gather_start(xs)
    weights = ((wg_ref, wg_all), (wu_ref, wu_all), (wd_ref, wd_all))
    kept = [
        pltpu.make_async_copy(w.at[side], w_all.at[0], ls.at[2 + i])
        for i, (w, w_all) in enumerate(weights)
    ]
    w_cross = [near.send(wg_ref.at[1 - side], wg_all.at[1], near.cross)]
    for c in loads:
        c.start()

    experts_all = router_ref.shape[1]
    number = lax.broadcasted_iota(jnp.int32, (experts_all, length), 0)
    number = 2 * lax.rem(number, experts_all // 2) + number // (experts_all // 2)
    chosen = routes_ref[0:1, :] == number
    for k in range(1, TOP):
        chosen = jnp.logical_or(chosen, routes_ref[k : k + 1, :] == number)
    mask = jnp.where(chosen, 1.0, 0.0)
    earlier = lax.broadcasted_iota(jnp.int32, (length, length), 0) < lax.broadcasted_iota(
        jnp.int32, (length, length), 1
    )
    rank = nn(mask.astype(BF16), jnp.where(earlier, 1.0, 0.0).astype(BF16))
    rank = jnp.where(chosen, rank, -1.0).astype(jnp.int32)
    experts = rank.shape[0] // 2
    place_ref[...] = jnp.where(side == 0, rank[:experts], rank[experts:])
    base = near.core * HALF

    def hits(i):
        place = place_ref[i * 8 : (i + 1) * 8, :]
        spots = lax.broadcasted_iota(jnp.int32, (8, HALF, length), 1) + base
        return jnp.broadcast_to(place[:, None, :], (8, HALF, length)) == spots

    near.gather_relay(ogs_ref, og_copies)
    near.gather_relay(xs, x_copies)
    for c in og_copies[1:]:
        c.wait()
    og = wide(ogs_ref)
    save(9)
    for i in range(experts // 8):
        select = jnp.where(hits(i), 1.0, 0.0).reshape(8 * HALF, length).astype(BF16)
        og_out[i * 8 : (i + 1) * 8] = nn(select, og).astype(BF16).reshape(8, HALF, width)
    og_wait = plane.exchange(og_out, og_in, as_, ar, ls.at[0], False)
    for c in kept:
        c.start()
    w_swap = [near.send(w.at[side], w_all.at[2], near.swap) for w, w_all in weights]

    for c in x_copies[1:]:
        c.wait()
    x = wide(xs).astype(F32)
    scale = lax.rsqrt(jnp.mean(x * x, axis=1, keepdims=True) + EPS)
    fs_ref[...] = scale
    normed = (x * scale * gain1_ref[...]).astype(BF16)
    normed_ref[...] = normed
    for c in loads:
        c.wait()
    save(0)
    qpre = nn(normed, wq_ref[...])
    kpre = nn(normed, wk_ref[...])
    qpre_ref[...] = qpre
    kpre_ref[...] = kpre
    v_ref[...] = nn(normed, wv_ref[...]).astype(BF16)
    lane = lax.broadcasted_iota(jnp.int32, (1, HDIM), 1)
    half = HDIM // 2
    step = lax.rem(lane, half).astype(F32) * (-2.0 * math.log(10000.0) / HDIM)
    angle = as_column(places_ref[...]) * jnp.exp(step)
    cosine = jnp.cos(angle)
    sine = jnp.sin(angle) * jnp.where(lane < half, -1.0, 1.0)
    cos_ref[...] = cosine
    sin_ref[...] = sine
    same = as_column(row_ref[...]) == row_ref[...].astype(F32)
    for h in range(q_ref.shape[1] // HDIM):
        at = slice(h * HDIM, (h + 1) * HDIM)
        qh = qpre[:, at]
        kh = kpre[:, at]
        query = turn(qh * head_scale(qh) * qn_ref[:, at], cosine, sine).astype(BF16)
        key = turn(kh * head_scale(kh) * kn_ref[:, at], cosine, sine).astype(BF16)
        q_ref[:, at] = query
        k_ref[:, at] = key
        probs = softmax_rows(query, key, same).astype(BF16)
        mixed_ref[:, at] = nn(probs, v_ref[:, at]).astype(BF16)
    near.split(nn(mixed_ref[...], wo_ref[...]), low_s, high_s, sent)
    save(1, 2, 3, 4, 5, 6)
    mid = x_ref[...] + near.sum_parts(low_s, high_s, sent, got, go, back)
    mid_ref[...] = mid
    mids_ref[t] = mid.astype(BF16)
    mid_copies = near.gather_start(mids_ref)
    w_cross.append(near.send(wu_ref.at[1 - side], wu_all.at[1], near.cross))
    w_cross.append(near.send(wd_ref.at[1 - side], wd_all.at[1], near.cross))
    near.gather_relay(mids_ref, mid_copies)
    for c in mid_copies[1:]:
        c.wait()
    save(7, 8)
    mid = wide(mids_ref).astype(F32)
    scale = lax.rsqrt(jnp.mean(mid * mid, axis=1, keepdims=True) + EPS)
    normed = (mid * scale * gain2_ref[...]).astype(BF16)
    nm_ref[...] = normed
    save(10)

    logits = dot(
        by_side(experts_all), nn(normed, router_ref[...]), ((1,), (1,)), precision=HIGH
    )
    masked = jnp.where(chosen, logits, -1e30)
    raised = jnp.where(chosen, jnp.exp(masked - jnp.max(masked, axis=0, keepdims=True)), 0.0)
    gates = raised / jnp.sum(raised, axis=0, keepdims=True)
    gates_ref[...] = gates
    gates_side = jnp.where(side == 0, gates[:experts], gates[experts:])
    for i in range(experts // 8):
        hit = hits(i)
        select = jnp.where(hit, 1.0, 0.0).reshape(8 * HALF, length).astype(BF16)
        rows_out[i * 8 : (i + 1) * 8, :, :width] = (
            nn(select, normed).astype(BF16).reshape(8, HALF, width)
        )
        gate = jnp.broadcast_to(gates_side[i * 8 : (i + 1) * 8][:, None, :], (8, HALF, length))
        column = jnp.sum(
            jnp.where(hit, gate, 0.0).reshape(8 * HALF, length), axis=1, keepdims=True
        )
        rows_out[i * 8 : (i + 1) * 8, :, width:] = two_parts(column).reshape(8, HALF, LANES)
    early = 32 - rows_late.shape[0]
    rows_wait = plane.exchange(rows_out, rows_in, bs, br, ls.at[1], False, early)

    def late_copy(i):
        return pltpu.make_async_copy(
            rows_out.at[plane.entry(early + i)], rows_late.at[i], late_sem.at[i]
        )

    def late_start(i, _):
        late_copy(i).start()
        return 0

    def late_wait(i, _):
        late_copy(i).wait()
        return 0

    lax.fori_loop(0, 32 - early, late_start, 0)
    for c, (w, w_all) in zip(w_cross, weights):
        c.wait()
        w_swap.append(near.send(w_all.at[1], w_all.at[3], near.swap))
    og_wait()
    rows_wait()
    lax.fori_loop(0, 32 - early, late_wait, 0)
    for c in w_swap + kept + saves:
        c.wait()


def run_front(
    x, og, gain1, gain2, wq, wk, wv, wo, qn, kn, places, labels, routes, router, wg, wu, wd, groups
):
    length, quarter = x.shape
    width = 4 * quarter
    inner = wq.shape[1]
    whole = pl.BlockSpec(memory_space=pltpu.VMEM)
    free = pl.BlockSpec(memory_space=pl.ANY)
    f = jax.ShapeDtypeStruct
    vm = pltpu.VMEM
    dma = pltpu.SemaphoreType.DMA
    held = [
        f((length, width), BF16),
        f((length, inner), F32),
        f((length, inner), F32),
        f((length, inner), BF16),
        f((length, inner), BF16),
        f((length, inner), BF16),
        f((length, inner), BF16),
        f((length, quarter), F32),
        f((4, length, quarter), BF16),
        f((4, length, quarter), BF16),
        f((length, width), BF16),
    ]
    return pl.pallas_call(
        front_body,
        in_specs=[whole] * 4 + [free] * 4 + [whole] * 6 + [free] * 3,
        out_specs=[whole] * 5 + [free] * 17,
        out_shape=[
            f((length, HDIM), F32),
            f((length, HDIM), F32),
            f((length, 1), F32),
            f((2 * groups, length), F32),
            f((groups, length), jnp.int32),
        ]
        + held
        + [
            f((groups, HALF, width + LANES), BF16),
            f((LATE, HALF, width + LANES), BF16),
            f((groups, HALF, width), BF16),
            f((4,) + wg.shape[1:], BF16),
            f((4,) + wu.shape[1:], BF16),
            f((4,) + wd.shape[1:], BF16),
        ],
        scratch_shapes=[vm(h.shape, h.dtype) for h in held]
        + [vm(w.shape, BF16) for w in (wq, wk, wv, wo)]
        + [
            dma((4,)),
            dma((11,)),
            vm((4, length, quarter), BF16),
            vm((length, quarter), F32),
            vm((length, quarter), F32),
            vm((length, 2 * quarter), BF16),
            vm((length, 2 * quarter), BF16),
            vm((length, quarter), BF16),
            vm((length, quarter), BF16),
            vm((groups, HALF, width), BF16),
            vm((groups, HALF, width + LANES), BF16),
            dma((20,)),
            dma((20,)),
            dma((31,)),
            dma((31,)),
            dma((31,)),
            dma((31,)),
            dma((5,)),
            dma((LATE,)),
        ],
        compiler_params=pltpu.CompilerParams(
            collective_id=1, has_side_effects=True, vmem_limit_bytes=60 << 20
        ),
        name="front",
    )(
        x, og, gain1, gain2, wq, wk, wv, wo, qn, kn, places, labels, routes, router, wg, wu, wd
    )


def middle_body(
    rows_ref, out_rows, place_ref, gates_ref, nm_ref, router_ref, mid_ref, og_ref, mids_ref, ogs_ref,
    gain_ref, normed_in, wq_in, wk_in, wv_in, wo_in, qn_ref, kn_ref, cos_ref, sin_ref,
    row_ref, qpre_ref, kpre_ref, q_ref, k_ref, v_ref, mixed_ref,
    stack_out, small_ref, mid_grad_ref, keep_ref, sent_ref, returned,
    low_s, low_f, high_f, sent, got, go, back, ngs, gg_s, stack_ref, probs_s, normed_ref, wq_ref, wk_ref, wv_ref,
    wo_ref, ts, tr, os, orr, ls,
):
    near = Near(ts, tr)
    plane = Plane()
    loads = [
        pltpu.make_async_copy(source, target, ls.at[1 + i])
        for i, (source, target) in enumerate(
            (
                (wo_in, wo_ref),
                (wq_in, wq_ref),
                (wk_in, wk_ref),
                (wv_in, wv_ref),
                (normed_in, normed_ref),
            )
        )
    ]
    for c in loads:
        c.start()
    side = plane.side
    t = near.t
    groups, slots, more = rows_ref.shape
    length, width = normed_ref.shape
    quarter = width // 4
    inner = q_ref.shape[1]

    barrier = pltpu.get_barrier_semaphore()

    plane.greet(barrier)
    pl.semaphore_signal(barrier, inc=1, device_id=near.swap, device_id_type=MESH)
    pl.semaphore_signal(barrier, inc=1, device_id=near.cross, device_id_type=MESH)
    pl.semaphore_wait(barrier, groups + 1)

    out_wait = plane.exchange(out_rows, returned, os, orr, ls.at[0], True)

    base = near.core * slots
    part = None
    for i in range(groups // 8):
        at = slice(i * 8, (i + 1) * 8)
        spots = lax.broadcasted_iota(jnp.int32, (8, slots, length), 1) + base
        hit = jnp.broadcast_to(place_ref[at, :][:, None, :], (8, slots, length)) == spots
        select = jnp.where(hit, 1.0, 0.0).reshape(8 * slots, length)
        tile = rows_ref[at].reshape(8 * slots, more)
        column = one_column(tile[:, width:])
        gg_s[0, at] = jnp.sum((select * column).reshape(8, slots, length), axis=1)
        term = tn(select.astype(BF16), tile[:, :width])
        part = term if part is None else part + term
    gate_swap = near.send(gg_s.at[0], gg_s.at[1], near.swap)
    near.split(part, low_f, high_f, sent)
    swapped = near.send(sent, got, near.swap)
    gate_swap.wait()
    gg_s[2] = gg_s[0] + gg_s[1]
    gate_cross = near.send(gg_s.at[2], gg_s.at[3], near.cross)
    swapped.wait()
    low = low_f[...] + got[:, :quarter].astype(F32)
    high = high_f[...] + got[:, quarter:].astype(F32)
    go[...] = jnp.where(near.low_x, high, low).astype(BF16)
    crossed = near.send(go, back, near.cross)
    gate_cross.wait()
    own, other = gg_s[2], gg_s[3]
    gate_grad = jnp.concatenate(
        [jnp.where(side == 0, own, other), jnp.where(side == 0, other, own)], axis=0
    )
    gates = gates_ref[...]
    logit_grad = gates * (gate_grad - jnp.sum(gates * gate_grad, axis=0, keepdims=True))
    mine = pl.ds(pl.multiple_of(t * quarter, quarter), quarter)
    experts = gates.shape[0]
    router = dot(
        by_side(experts), router_ref[mine, :].astype(F32), ((1,), (1,)), precision=HIGH
    )
    router_back = dot(logit_grad, router, ((0,), (0,)), precision=HIGH)
    small_ref[:experts, :] = dot(
        logit_grad, nm_ref[:, mine].astype(F32), ((1,), (0,)), precision=HIGH
    ).astype(BF16)
    mid = wide(mids_ref).astype(F32)
    scale = lax.rsqrt(jnp.mean(mid * mid, axis=1, keepdims=True) + EPS)
    mid_own = mid_ref[...]
    same = as_column(row_ref[...]) == row_ref[...].astype(F32)
    heads = inner // HDIM

    def attention_probs(h):
        at = slice(h * HDIM, (h + 1) * HDIM)
        probs_s[h] = softmax_rows(q_ref[:, at], k_ref[:, at], same)

    for h in range(heads // 2):
        attention_probs(h)
    crossed.wait()
    ng = jnp.where(near.low_x, low, high) + back[...].astype(F32) + router_back
    ngs[t] = ng.astype(BF16)
    ng_copies = near.gather_start(ngs)
    moe = jnp.sum(ng * mid_own * scale, axis=0, keepdims=True)
    for h in range(heads // 2, heads):
        attention_probs(h)
    near.gather_relay(ngs, ng_copies)
    for c in ng_copies[1:]:
        c.wait()

    weighted = wide(ngs).astype(F32) * gain_ref[...]
    shrink = scale * scale * scale * jnp.mean(weighted * mid, axis=1, keepdims=True)
    mid_grad_ref[...] = og_ref[...] + scale * (ng * gain_ref[:, mine]) - mid_own * shrink
    attn_grad = (wide(ogs_ref).astype(F32) + scale * weighted - mid * shrink).astype(BF16)

    for c in loads:
        c.wait()
    wo_grad = tn(mixed_ref[...], attn_grad).astype(BF16)
    for i in range(4):
        stack_ref[i * inner : (i + 1) * inner, :] = wo_grad[:, i * quarter : (i + 1) * quarter]
    saves = [
        pltpu.make_async_copy(
            stack_ref.at[i * width : (i + 1) * width],
            stack_out.at[i * width : (i + 1) * width],
            ls.at[6 + i],
        )
        for i in range(4)
    ]
    saves[0].start()
    mixed_grad = nt(attn_grad, wo_ref[...]).astype(BF16)
    cosine = cos_ref[...]
    sine = sin_ref[...]
    factor = HDIM ** (-0.5)

    def norm_back(pre, gain, rotated):
        grad = rotated * cosine - pltpu.roll(rotated, HDIM // 2, 1) * sine
        head = head_scale(pre)
        weighted = grad * gain
        mean = jnp.mean(weighted * pre, axis=1, keepdims=True)
        low = (head * weighted - pre * (head * head * head * mean)).astype(BF16)
        return low, jnp.sum(grad * pre * head, axis=0, keepdims=True)

    q_sums, k_sums = [], []
    for h in range(inner // HDIM):
        at = slice(h * HDIM, (h + 1) * HDIM)
        query = q_ref[:, at]
        key = k_ref[:, at]
        mg = mixed_grad[:, at]
        probs = probs_s[h]
        low_s[:, 2 * inner + h * HDIM : 2 * inner + (h + 1) * HDIM] = tn(
            probs.astype(BF16), mg
        ).astype(BF16)
        prob_grad = nt(mg, v_ref[:, at])
        weighted_p = probs * prob_grad
        score = (weighted_p - probs * jnp.sum(weighted_p, axis=1, keepdims=True)).astype(BF16)
        low_q, total = norm_back(qpre_ref[:, at], qn_ref[:, at], nn(score, key) * factor)
        low_s[:, h * HDIM : (h + 1) * HDIM] = low_q
        q_sums.append(total)
        low_k, total = norm_back(kpre_ref[:, at], kn_ref[:, at], tn(score, query) * factor)
        low_s[:, inner + h * HDIM : inner + (h + 1) * HDIM] = low_k
        k_sums.append(total)
    row = lax.broadcasted_iota(jnp.int32, (small_ref.shape[0] - experts, quarter), 0)
    rest = jnp.zeros(row.shape, F32)
    for i, value in enumerate(
        (moe, jnp.concatenate(q_sums, axis=1), jnp.concatenate(k_sums, axis=1))
    ):
        rest = jnp.where(row == i + 1, jnp.broadcast_to(value, row.shape), rest)
    small_ref[experts:, :] = rest.astype(BF16)
    part = None
    for i, w in enumerate((wq_ref, wk_ref, wv_ref)):
        term = nt(low_s[:, i * inner : (i + 1) * inner], w[...])
        part = term if part is None else part + term
    near.split(part, low_f, high_f, sent_ref)
    keep_ref[:, :quarter] = low_f[...]
    keep_ref[:, quarter:] = high_f[...]
    normed = normed_ref[...]
    for i in range(3):
        stack_ref[(i + 1) * width : (i + 2) * width, :] = tn(
            normed, low_s[:, i * inner : (i + 1) * inner]
        ).astype(BF16)
        saves[i + 1].start()

    out_wait()
    for c in saves:
        c.wait()


def run_middle(
    rows, out_rows, place, gates, nm, router, mid, og, mids, ogs, gain, normed, wq, wk, wv, wo, qn,
    kn, cosine, sine, labels, qpre, kpre, q, k, v, mixed,
):
    length, width = normed.shape
    quarter = width // 4
    groups = place.shape[0]
    inner = wq.shape[1]
    whole = pl.BlockSpec(memory_space=pltpu.VMEM)
    free = pl.BlockSpec(memory_space=pl.ANY)
    f = jax.ShapeDtypeStruct
    vm = pltpu.VMEM
    dma = pltpu.SemaphoreType.DMA
    return pl.pallas_call(
        middle_body,
        in_specs=[whole, free] + [whole] * 9 + [free] * 5 + [whole] * 11,
        out_specs=[free] + [whole] * 4 + [free],
        out_shape=[
            f((4 * width, quarter), BF16),
            f((SMALL, quarter), BF16),
            f((length, quarter), F32),
            f((length, 2 * quarter), F32),
            f((length, 2 * quarter), BF16),
            f(out_rows.shape, BF16),
        ],
        scratch_shapes=[
            vm((length, 3 * inner), BF16),
            vm((length, quarter), F32),
            vm((length, quarter), F32),
            vm((length, 2 * quarter), BF16),
            vm((length, 2 * quarter), BF16),
            vm((length, quarter), BF16),
            vm((length, quarter), BF16),
            vm((4, length, quarter), BF16),
            vm((4, groups, length), F32),
            vm((4 * width, quarter), BF16),
            vm((inner // HDIM, length, length), F32),
            vm(normed.shape, BF16),
            vm(wq.shape, BF16),
            vm(wk.shape, BF16),
            vm(wv.shape, BF16),
            vm(wo.shape, BF16),
            dma((8,)),
            dma((8,)),
            dma((31,)),
            dma((31,)),
            dma((10,)),
        ],
        compiler_params=pltpu.CompilerParams(
            collective_id=3, has_side_effects=True, vmem_limit_bytes=61 << 20
        ),
        name="middle",
    )(
        rows, out_rows, place, gates, nm, router, mid, og, mids, ogs, gain, normed, wq, wk, wv, wo,
        qn, kn, cosine, sine, labels, qpre, kpre, q, k, v, mixed,
    )


def tail_body(
    stack_ref, small_ref, keep_ref, sent_ref, x_ref, mid_grad_ref, fs_ref, gain_ref, mid_ref,
    ret_ref, place_ref, gates_ref, kept_g, kept_u, kept_d, got_g, got_u, got_d,
    out_ref, small_out_ref, input_ref, layer_ref, full_g, full_u, full_d,
    fin_s, own_s, ret_s, recv1, buf1, recv2, buf2, recv3, small_in, got, out_sent, out_got, go, back, out_go, out_back,
    mean_in, kb, gb, nb, kd, gd, far_g, far_u, far_d, other_g, other_u,
    other_d, ss, rs, sss, srs, ts, tr, ws, ls,
):
    dp = lax.axis_index("dp")
    t = lax.axis_index("tensor")
    y = lax.rem(dp, 4)
    xh = lax.rem(dp // 4, 2)
    z = dp // 8
    core = lax.rem(t, 2)
    first_core = core == 0
    low_x = t < 2
    half = stack_ref.shape[0] // 2
    size = half // 2
    n1, n2, n3 = size // 4, size // 16, size // 32
    quarter = x_ref.shape[1]
    ret_load = pltpu.make_async_copy(ret_ref, ret_s, ls.at[4])
    ret_load.start()

    def at_z(k):
        return ((lax.rem(z + k, 4) * 2 + xh) * 4 + y, t)

    def at_y(k):
        return ((z * 2 + xh) * 4 + lax.rem(y + k, 4), t)

    at_x = ((z * 2 + 1 - xh) * 4 + y, t)
    at_swap = (dp, t + 1 - 2 * core)
    at_cross = (dp, lax.rem(t + 2, 4))
    at_diag = (dp, lax.rem(t + 2, 4) + 1 - 2 * core)

    barrier = pltpu.get_barrier_semaphore()
    for k in range(1, 4):
        pl.semaphore_signal(barrier, inc=1, device_id=at_z(k), device_id_type=MESH)
        pl.semaphore_signal(barrier, inc=1, device_id=at_y(k), device_id_type=MESH)
    for there in (at_x, at_swap, at_cross, at_diag):
        pl.semaphore_signal(barrier, inc=1, device_id=there, device_id_type=MESH)
    pl.semaphore_wait(barrier, 10)

    def send(source, target, sems, device):
        c = pltpu.make_async_remote_copy(
            src_ref=source,
            dst_ref=target,
            send_sem=sems[0],
            recv_sem=sems[1],
            device_id=device,
            device_id_type=MESH,
        )
        c.start()
        return c

    def copy(source, target, phase, h, k, device):
        return send(source, target, (ss.at[phase, h, k], rs.at[phase, h, k]), device)

    def small_copy(slot, k, device):
        return send(small_in.at[slot], small_in.at[slot], (sss.at[k], srs.at[k]), device)

    def near(source, target, k, device):
        return send(source, target, (ts.at[k], tr.at[k]), device)

    def rows_at(start, size):
        return pl.ds(pl.multiple_of(start, 64), size)

    ways = (((z, at_z), (y, at_y)), ((y, at_y), (z, at_z)))
    streams = [(ways[h], h * half + s * size) for s in range(2) for h in range(2)]
    first, second, third, ahead, later, ended, own_loads, bases = [], [], [], [], [], [], [], []
    for n, (((pos, at), _), start) in enumerate(streams):
        for k in range(1, 4):
            there = rows_at(start + lax.rem(pos + k, 4) * n1, n1)
            first.append(copy(stack_ref.at[there], recv1.at[n, k - 1], 0, n, k - 1, at(k)))
        bases.append(start + pos * n1)
    for n, base in enumerate(bases):
        own_loads.append(
            pltpu.make_async_copy(stack_ref.at[rows_at(base, n1)], own_s.at[n], ls.at[n])
        )
        own_loads[-1].start()

    swapped = near(sent_ref, got, 0, at_swap)
    side = lax.rem(t // 2 + xh, 2)
    groups, slots, width = ret_ref.shape
    length = x_ref.shape[0]
    gates = jnp.where(side == 0, gates_ref[:groups, :], gates_ref[groups:, :])
    ret_load.wait()
    part = None
    for i in range(groups // 8):
        at = slice(i * 8, (i + 1) * 8)
        spots = lax.broadcasted_iota(jnp.int32, (8, slots, length), 1) + core * slots
        hit = jnp.broadcast_to(place_ref[at, :][:, None, :], (8, slots, length)) == spots
        gate = jnp.broadcast_to(gates[at][:, None, :], (8, slots, length))
        select = jnp.where(hit, gate, 0.0).reshape(8 * slots, length).astype(BF16)
        term = tn(select, ret_s[at].reshape(8 * slots, width))
        part = term if part is None else part + term
    p = [part[:, i * quarter : (i + 1) * quarter] for i in range(4)]
    out_sent[:, :quarter] = jnp.where(first_core, p[1], p[0]).astype(BF16)
    out_sent[:, quarter:] = jnp.where(first_core, p[3], p[2]).astype(BF16)
    out_low = jnp.where(first_core, p[0], p[1])
    out_high = jnp.where(first_core, p[2], p[3])
    out_swapped = near(out_sent, out_got, 1, at_swap)
    swapped.wait()
    low_half = keep_ref[:, :quarter] + got[:, :quarter].astype(F32)
    high_half = keep_ref[:, quarter:] + got[:, quarter:].astype(F32)
    go[...] = jnp.where(low_x, high_half, low_half).astype(BF16)
    crossed = near(go, back, 2, at_cross)
    in_mine = jnp.where(low_x, low_half, high_half)
    out_swapped.wait()
    out_low = out_low + out_got[:, :quarter].astype(F32)
    out_high = out_high + out_got[:, quarter:].astype(F32)
    out_go[...] = jnp.where(low_x, out_high, out_low).astype(BF16)
    crossed.wait()
    in_grad = in_mine + back[...].astype(F32)
    x = x_ref[...]
    fs = fs_ref[...]
    weighted = in_grad * gain_ref[:, pl.ds(pl.multiple_of(t * quarter, quarter), quarter)]
    mean = jnp.sum(weighted * x, axis=1, keepdims=True)
    mean_in[0] = jnp.broadcast_to(mean, mean_in.shape[1:])
    mean_swap = near(mean_in.at[0], mean_in.at[1], 3, at_swap)
    row = lax.broadcasted_iota(jnp.int32, (16, quarter), 0)
    norm_row = jnp.sum(in_grad * x * fs, axis=0, keepdims=True)
    small_in[z] = small_ref[...]
    last = small_ref.shape[0] - 16
    small_in[z, last:, :] = jnp.where(
        row == 0, jnp.broadcast_to(norm_row, (16, quarter)), small_ref[last:, :].astype(F32)
    ).astype(BF16)
    small = [small_copy(z, k - 1, at_z(k)) for k in range(1, 4)]
    mean_swap.wait()
    mean_in[2] = mean_in[0] + mean_in[1]
    mean_cross = near(mean_in.at[2], mean_in.at[3], 4, at_cross)
    out_crossed = near(out_go, out_back, 5, at_cross)
    mean_cross.wait()
    mean = (mean_in[2] + mean_in[3])[:, 0:1] / (4 * quarter)
    input_ref[...] = mid_grad_ref[...] + fs * weighted - x * (fs * fs * fs * mean)
    out_crossed.wait()
    layer_ref[...] = mid_ref[...] + (jnp.where(low_x, out_low, out_high) + out_back[...].astype(F32))

    block = kb.shape[1]
    span = far_d.shape[0]

    def column_sums(kept, gotten, far, mine):
        loads, stores = [], []
        count = kept.shape[0] // block
        for i in range(count):
            at = slice(i * block, (i + 1) * block)
            loads.append(
                (
                    pltpu.make_async_copy(kept.at[at], kb.at[i % 2], ws.at[i % 2, 0]),
                    pltpu.make_async_copy(gotten.at[at], gb.at[i % 2], ws.at[i % 2, 1]),
                )
            )
        for c in loads[0]:
            c.start()
        for i in range(count):
            if i + 1 < count:
                for c in loads[i + 1]:
                    c.start()
            for c in loads[i]:
                c.wait()
            slot = i % 2
            at = slice(i * block, (i + 1) * block)
            total = kb[slot] + gb[slot].astype(F32)
            if i >= 2:
                stores[i - 2].wait()
            nb[slot] = total[:, :span]
            far[at, :] = total[:, span:].astype(BF16)
            stores.append(pltpu.make_async_copy(nb.at[slot], mine.at[side, at], ws.at[slot, 2]))
            stores[-1].start()
        for c in stores[-2:]:
            c.wait()

    def arrived(copy, other, full):
        copy.wait()
        stores = []
        for i in range(other.shape[0] // block):
            slot = i % 2
            at = slice(i * block, (i + 1) * block)
            if i >= 2:
                stores[i - 2].wait()
            nb[slot] = other[at, :].astype(F32)
            stores.append(pltpu.make_async_copy(nb.at[slot], full.at[1 - side, at], ws.at[slot, 2]))
            stores[-1].start()
        for c in stores[-2:]:
            c.wait()

    def row_sums():
        loads = [
            (
                pltpu.make_async_copy(kept_d.at[at], kd.at[i], ws.at[2 + i, 0]),
                pltpu.make_async_copy(got_d.at[at], gd.at[i], ws.at[2 + i, 1]),
            )
            for i, at in enumerate((slice(span, 2 * span), slice(0, span)))
        ]
        for pair in loads:
            for c in pair:
                c.start()
        for c in loads[0]:
            c.wait()
        far_d[...] = (kd[0] + gd[0].astype(F32)).astype(BF16)
        others.append(near(far_d, other_d, 8, at_cross))
        for c in loads[1]:
            c.wait()
        kd[1] = kd[1] + gd[1].astype(F32)
        store = pltpu.make_async_copy(kd.at[1], full_d.at[side], ws.at[2, 2])
        store.start()
        return store

    def small_total(start, count):
        total = small_in[start].astype(F32)
        for i in range(start + 1, start + count):
            total = total + small_in[i].astype(F32)
        return total.astype(BF16)

    def first_sum(n):
        for c in first[3 * n : 3 * n + 3]:
            c.wait()
        own_loads[n].wait()
        total = own_s[n].astype(F32)
        for k in range(3):
            total = total + recv1[n, k].astype(F32)
        buf1[n] = total.astype(BF16)
        _, (pos, at) = streams[n][0]
        for k in range(1, 4):
            there = rows_at(lax.rem(pos + k, 4) * n2, n2)
            second.append(copy(buf1.at[n, there], recv2.at[n, k - 1], 1, n, k - 1, at(k)))
        bases[n] = bases[n] + pos * n2

    def second_sum(n):
        for c in second[3 * n : 3 * n + 3]:
            c.wait()
        _, (pos, _) = streams[n][0]
        total = buf1[n, rows_at(pos * n2, n2), :].astype(F32)
        for k in range(3):
            total = total + recv2[n, k].astype(F32)
        buf2[n] = total.astype(BF16)
        third.append(
            copy(buf2.at[n, rows_at((1 - xh) * n3, n3)], recv3.at[n], 2, n, 0, at_x)
        )

    def third_sum(n):
        third[n].wait()
        total = buf2[n, rows_at(xh * n3, n3), :].astype(F32) + recv3[n].astype(F32)
        here = rows_at(bases[n] + xh * n3, n3)
        fin_s[n] = total.astype(BF16)
        ahead.append(copy(fin_s.at[n], out_ref.at[here], 3, n, 0, at_x))
        own_loads.append(pltpu.make_async_copy(fin_s.at[n], out_ref.at[here], ls.at[n]))
        own_loads[-1].start()

    def share_second(n):
        ahead[n].wait()
        own_loads[4 + n].wait()
        here = rows_at(bases[n], n2)
        _, (_, at) = streams[n][0]
        for k in range(1, 4):
            later.append(copy(out_ref.at[here], out_ref.at[here], 4, n, k - 1, at(k)))

    def share_first(n):
        for c in later[3 * n : 3 * n + 3]:
            c.wait()
        ((pos, at), _), start = streams[n]
        here = rows_at(start + pos * n1, n1)
        for k in range(1, 4):
            ended.append(copy(out_ref.at[here], out_ref.at[here], 5, n, k - 1, at(k)))

    column_sums(kept_g, got_g, far_g, full_g)
    others = [near(far_g, other_g, 6, at_cross)]
    first_sum(0)
    first_sum(1)
    column_sums(kept_u, got_u, far_u, full_u)
    first_sum(2)
    first_sum(3)
    for c in small:
        c.wait()
    small_in[4 + y] = small_total(0, 4)
    small = [small_copy(4 + y, 3 + k - 1, at_y(k)) for k in range(1, 4)]
    second_sum(0)
    second_sum(1)
    third_sum(0)
    third_sum(1)
    second_sum(2)
    second_sum(3)
    for c in small:
        c.wait()
    small_in[8 + xh] = small_total(4, 4)
    small = small_copy(8 + xh, 6, at_x)
    share_second(0)
    share_second(1)
    third_sum(2)
    third_sum(3)
    share_first(0)
    share_first(1)
    share_second(2)
    share_second(3)
    others.append(near(far_u, other_u, 7, at_cross))
    share_first(2)
    share_first(3)
    small.wait()
    small_out_ref[t] = small_total(8, 2)
    small = [
        near(small_out_ref.at[t], small_out_ref.at[t], 9 + i, there)
        for i, there in enumerate((at_swap, at_cross, at_diag))
    ]
    row_sums().wait()
    arrived(others[0], other_g, full_g)
    arrived(others[1], other_u, full_u)
    others[2].wait()
    kd[0] = other_d[...].astype(F32)
    store = pltpu.make_async_copy(kd.at[0], full_d.at[1 - side], ws.at[2, 2])
    store.start()
    store.wait()
    for c in small + ended:
        c.wait()


def run_tail(
    stack, small, keep, sent, x, mid_grad, fs, gain, mid, returned, place, gates, pieces
):
    rows, cols = stack.shape
    half = rows // 2
    length = x.shape[0]
    deep, wide_half = pieces[0].shape
    span = wide_half // 2
    shapes = [(deep, span), (deep, span), (span, deep)]
    whole = pl.BlockSpec(memory_space=pltpu.VMEM)
    free = pl.BlockSpec(memory_space=pl.ANY)
    f = jax.ShapeDtypeStruct
    vm = pltpu.VMEM
    return pl.pallas_call(
        tail_body,
        in_specs=[free] + [whole] * 8 + [free, whole, whole] + [free] * 6,
        out_specs=[free] + [whole] * 3 + [free] * 3,
        out_shape=[
            f(stack.shape, BF16),
            f((4,) + small.shape, BF16),
            f(x.shape, F32),
            f(x.shape, F32),
        ]
        + [f((2,) + shape, F32) for shape in shapes],
        scratch_shapes=[
            vm((4, half // 64, cols), BF16),
            vm((4, half // 8, cols), BF16),
            vm(returned.shape, BF16),
            vm((4, 3, half // 8, cols), BF16),
            vm((4, half // 8, cols), BF16),
            vm((4, 3, half // 32, cols), BF16),
            vm((4, half // 32, cols), BF16),
            vm((4, half // 64, cols), BF16),
            vm((10,) + small.shape, BF16),
            vm((length, 2 * cols), BF16),
            vm((length, 2 * cols), BF16),
            vm((length, 2 * cols), BF16),
            vm((length, cols), BF16),
            vm((length, cols), BF16),
            vm((length, cols), BF16),
            vm((length, cols), BF16),
            vm((4, length, LANES), F32),
            vm((2, 512, wide_half), F32),
            vm((2, 512, wide_half), BF16),
            vm((2, 512, span), F32),
            vm((2, span, deep), F32),
            vm((2, span, deep), BF16),
            vm((deep, span), BF16),
            vm((deep, span), BF16),
            vm((span, deep), BF16),
        ]
        + [vm(shape, BF16) for shape in shapes]
        + [
            pltpu.SemaphoreType.DMA((6, 4, 3)),
            pltpu.SemaphoreType.DMA((6, 4, 3)),
            pltpu.SemaphoreType.DMA((7,)),
            pltpu.SemaphoreType.DMA((7,)),
            pltpu.SemaphoreType.DMA((12,)),
            pltpu.SemaphoreType.DMA((12,)),
            pltpu.SemaphoreType.DMA((4, 3)),
            pltpu.SemaphoreType.DMA((5,)),
        ],
        compiler_params=pltpu.CompilerParams(
            collective_id=0, has_side_effects=True, vmem_limit_bytes=62 << 20
        ),
        cost_estimate=pl.CostEstimate(flops=0, bytes_accessed=500_000_000, transcendentals=0),
        name="sum_over_dp",
    )(stack, small, keep, sent, x, mid_grad, fs, gain, mid, returned, place, gates, *pieces)


def per_device(
    layer_input,
    attn_norm,
    w_query,
    w_key,
    w_value,
    query_norm,
    key_norm,
    w_output,
    moe_norm,
    w_router,
    w_gate,
    w_up,
    w_down,
    segments,
    positions,
    routes,
    out_grad,
):
    length, quarter = layer_input.shape
    width = 4 * quarter
    rank_t = lax.axis_index("tensor")
    groups = lax.axis_size("dp")
    experts = 2 * groups

    labels = segments
    gain_q = query_norm[None, :]
    gain_k = key_norm[None, :]
    gain_1 = attn_norm[None, :]
    gain_2 = moe_norm[None, :]
    (
        cosine, sine, first_scale, gates, place, normed_in, qpre, kpre, query, key, values, mixed, mid,
        mids, grads_full, normed_mid, rows, late_rows, grad_rows, *expert_weights,
    ) = run_front(
        layer_input, out_grad, gain_1, gain_2, w_query, w_key, w_value, w_output, gain_q, gain_k,
        positions, labels, routes.T, w_router, w_gate, w_up, w_down, groups,
    )

    expert_out, back_rows, *pieces = run_experts(rows, late_rows, grad_rows, expert_weights)

    stack, small, mid_grad, keep, sent, returned = run_middle(
        back_rows, expert_out, place, gates, normed_mid, w_router, mid, out_grad, mids,
        grads_full, gain_2, normed_in, w_query, w_key, w_value, w_output, gain_q, gain_k, cosine,
        sine, labels, qpre, kpre, query, key, values, mixed,
    )

    big, everywhere, input_grad, layer_output, *expert_grads = run_tail(
        stack, small, keep, sent, layer_input, mid_grad, first_scale, gain_1, mid,
        returned, place, gates, pieces,
    )
    small = lax.dynamic_index_in_dim(everywhere, rank_t, 0, keepdims=False)
    everywhere = everywhere.astype(F32)
    rows_w = w_query.shape[0]
    rows_o = w_output.shape[0]
    summed = [big[width + i * rows_w : width + (i + 1) * rows_w].astype(F32) for i in range(3)]
    output_grad = jnp.concatenate(
        [big[i * rows_o : (i + 1) * rows_o] for i in range(4)], axis=1
    ).astype(F32)
    return (
        layer_output,
        input_grad,
        everywhere[:, experts].reshape(width),
        summed[0],
        summed[1],
        summed[2],
        small[experts + 2].astype(F32),
        small[experts + 3].astype(F32),
        output_grad,
        everywhere[:, experts + 1].reshape(width),
        everywhere[:, :experts]
        .reshape(4, 2, groups, quarter)
        .transpose(0, 3, 2, 1)
        .reshape(width, experts),
        expert_grads[0],
        expert_grads[1],
        expert_grads[2],
    )


def solution(mesh):
    placed = (
        P("dp", "tensor"),
        P(),
        P(None, "tensor"),
        P(None, "tensor"),
        P(None, "tensor"),
        P("tensor"),
        P("tensor"),
        P("tensor", None),
        P(),
        P(),
        P("dp", None, "tensor"),
        P("dp", None, "tensor"),
        P("dp", "tensor", None),
        P("dp", None),
        P("dp", None),
        P("dp", None),
        P("dp", "tensor"),
    )
    return jax.shard_map(
        per_device,
        mesh=mesh,
        in_specs=placed,
        out_specs=(
            P("dp", "tensor"),
            P("dp", "tensor"),
            P(),
            P(None, "tensor"),
            P(None, "tensor"),
            P(None, "tensor"),
            P("tensor"),
            P("tensor"),
            P("tensor", None),
            P(),
            P(),
            P("dp", None, "tensor"),
            P("dp", None, "tensor"),
            P("dp", "tensor", None),
        ),
        check_vma=False,
    )
```
